256 devices in a mesh: gx: 4 (over x), gy: 8 (over z), gz: 8 (over y, core).
Axes of the slice: x: 4, y: 4, z: 8, core: 2. Of those that a mesh axis runs over, the one named last changes fastest.
Arguments:
- rhs: float32 [64, 128, 1024], P('gx', 'gy', 'gz'), may hold values from -6 to 6
- face_x: float32 [64, 128, 1024], P('gx', 'gy', 'gz'), may hold values from 0.25 to 4
- face_y: float32 [64, 128, 1024], P('gx', 'gy', 'gz'), may hold values from 0.25 to 4
- face_z: float32 [64, 128, 1024], P('gx', 'gy', 'gz'), may hold values from 0.25 to 4
Outputs:
- solution: float32 [64, 128, 1024], P('gx', 'gy', 'gz')
The draws below stay inside these ranges and needn't reach their ends.
All inputs are finite; a program needn't handle non-finite values.
Results may differ from the reference program's by a relative error of at most 0.00002.
Values sent between devices are 32-bit elements; how exact they have to be, the bound alone decides.
A program may use at most 64 MiB of HBM per device.

```python
import math
import jax
import jax.numpy as jnp
from jax import lax

LEVELS = 6
PRE = 2
POST = 2
COARSE_SWEEPS = 24
NX = 64
NY = 128
NZ = 1024


def levels(key, shape, cuts, low, top_value):
    def one(position, parts):
        heights = jax.random.uniform(jax.random.fold_in(jax.random.fold_in(key, 6), position), (parts,), jnp.float32, low / len(cuts), top_value / len(cuts))
        return jnp.repeat(jnp.exp(heights), shape[position] // parts).reshape((-1,) + (1,) * (len(shape) - position - 1))

    loudness = one(*cuts[0])
    for cut in cuts[1:]:
        loudness = loudness * one(*cut)
    return loudness


def noise(key, extent, width, most, split=(), kind=jnp.bfloat16):
    drawn = width * jax.random.normal(key, extent, jnp.float32)
    if split:
        drawn = drawn * levels(key, extent, split, -0.22, 0.18)
    return jnp.clip(drawn, -most, most).astype(kind)


def setup_inputs(seed: int = 0) -> dict:
    streams_of = jax.random.split(jax.random.key(seed), 5)
    rhs = noise(streams_of[0], (NX, NY, NZ), 1.0, 6.0, ((0, 4), (1, 8), (2, 8)), jnp.float32)
    face_x = jnp.clip(jnp.exp(math.log(4.0) - 2.7725887 * jax.random.uniform(streams_of[1], (NX, NY, NZ), jnp.float32) ** levels(streams_of[1], (NX, NY, NZ), ((0, 4), (1, 8), (2, 8)), -0.2, 0.2)), 0.25, 4.0)
    face_y = jnp.clip(jnp.exp(math.log(4.0) - 2.7725887 * jax.random.uniform(streams_of[2], (NX, NY, NZ), jnp.float32) ** levels(streams_of[2], (NX, NY, NZ), ((0, 4), (1, 8), (2, 8)), -0.2, 0.2)), 0.25, 4.0)
    face_z = jnp.clip(jnp.exp(math.log(4.0) - 2.7725887 * jax.random.uniform(streams_of[3], (NX, NY, NZ), jnp.float32) ** levels(streams_of[3], (NX, NY, NZ), ((0, 4), (1, 8), (2, 8)), -0.2, 0.2)), 0.25, 4.0)
    return {"rhs": rhs, "face_x": face_x, "face_y": face_y, "face_z": face_z}


RELAX = 2.0 / 3.0


def face_flux(center, padded, lower, upper, weight):
    total = lower[0] * (center - padded[:-2, 1:-1, 1:-1]) + upper[0] * (center - padded[2:, 1:-1, 1:-1])
    total = total + lower[1] * (center - padded[1:-1, :-2, 1:-1]) + upper[1] * (center - padded[1:-1, 2:, 1:-1])
    total = total + lower[2] * (center - padded[1:-1, 1:-1, :-2]) + upper[2] * (center - padded[1:-1, 1:-1, 2:])
    return weight * total


def diagonal_of(lower, upper, weight):
    return weight * (lower[0] + lower[1] + lower[2] + upper[0] + upper[1] + upper[2])


def coarsen_face(field, axis, offset):
    dims = field.shape
    blocks = field.reshape(dims[0] // 2, 2, dims[1] // 2, 2, dims[2] // 2, 2)
    picked = lax.slice_in_dim(blocks, offset, offset + 1, axis=2 * axis + 1)
    return jnp.mean(picked, axis=(1, 3, 5))


def coarsen_cells(field):
    dims = field.shape
    return jnp.mean(field.reshape(dims[0] // 2, 2, dims[1] // 2, 2, dims[2] // 2, 2), axis=(1, 3, 5))


def refine_cells(field):
    dims = field.shape
    wide = jnp.broadcast_to(field[:, None, :, None, :, None], (dims[0], 2, dims[1], 2, dims[2], 2))
    return wide.reshape(dims[0] * 2, dims[1] * 2, dims[2] * 2)


def coarsen_level(lower, upper):
    new_lower = (coarsen_face(lower[0], 0, 0), coarsen_face(lower[1], 1, 0), coarsen_face(lower[2], 2, 0))
    new_upper = (coarsen_face(upper[0], 0, 1), coarsen_face(upper[1], 1, 1), coarsen_face(upper[2], 2, 1))
    return new_lower, new_upper


def local_apply(value, lower, upper, weight):
    return face_flux(value, jnp.pad(value, 1), lower, upper, weight)


def local_cycle(level, forcing, lower, upper):
    weight = 0.25 ** level
    diagonal = diagonal_of(lower, upper, weight)
    value = RELAX * forcing / diagonal

    def smooth(value_now):
        return value_now + RELAX * (forcing - local_apply(value_now, lower, upper, weight)) / diagonal

    if level == LEVELS - 1:
        return lax.fori_loop(0, COARSE_SWEEPS - 1, lambda index, carry: smooth(carry), value)
    for sweep_index in range(PRE - 1):
        value = smooth(value)
    residual = forcing - local_apply(value, lower, upper, weight)
    coarse_lower, coarse_upper = coarsen_level(lower, upper)
    correction = local_cycle(level + 1, coarsen_cells(residual), coarse_lower, coarse_upper)
    value = value + refine_cells(correction)
    for sweep_index in range(POST):
        value = smooth(value)
    return value


def reference(rhs, face_x, face_y, face_z):
    upper_x = jnp.concatenate([face_x[1:], jnp.zeros_like(face_x[:1])], axis=0)
    upper_y = jnp.concatenate([face_y[:, 1:], jnp.zeros_like(face_y[:, :1])], axis=1)
    upper_z = jnp.concatenate([face_z[:, :, 1:], jnp.zeros_like(face_z[:, :, :1])], axis=2)
    return local_cycle(0, rhs, (face_x, face_y, face_z), (upper_x, upper_y, upper_z))
```

```python
import jax
import jax.numpy as jnp
from jax import lax
from jax.experimental import pallas as pl
from jax.experimental.pallas import tpu as pltpu
from jax.sharding import PartitionSpec as P

RELAX = 2.0 / 3.0
THIRD = 1.0 / 3.0
COARSE_SWEEPS = 24
GX, GY, GZ = 4, 8, 8
F32 = jnp.float32
MESH = pl.DeviceIdType.MESH

FACES = [(1, 0, 0), (-1, 0, 0), (0, 1, 0), (0, -1, 0), (0, 0, 1), (0, 0, -1)]
DOWN = [(-1, 0, 0), (0, -1, 0), (0, 0, -1)]
RING_Z = [(0, 0, k) for k in (4, 3, 5, 2, 6, 1, 7)]
RING_Y = [(0, k, 0) for k in (4, 3, 5, 2, 6, 1, 7)]
PLANE = [(2, 1, 0), (2, -1, 0), (1, 1, 0), (1, -1, 0), (3, 1, 0), (3, -1, 0)]
PLANE += [(2, 0, 0), (0, 1, 0), (0, -1, 0), (1, 0, 0), (3, 0, 0)]


def lanes(rows):
    return lax.broadcasted_iota(jnp.int32, (rows, 128), 1)


def sublanes(rows):
    return lax.broadcasted_iota(jnp.int32, (rows, 128), 0)


def turn(value, steps, axis=1):
    steps %= value.shape[axis]
    return value if steps == 0 else pltpu.roll(value, steps, axis)


def take(value, index):
    return jnp.take_along_axis(value, index, axis=1, mode="promise_in_bounds")


class Block:
    def __init__(self, size_x, size_y, size_z, weight):
        self.X, self.Y, self.Z, self.weight = size_x, size_y, size_z, weight
        self.pitch = size_y + 8
        self.rows = size_x * size_y
        self.padded = 8 + (size_x + 2) * self.pitch

    def base(self, i):
        return 8 + (i + 1) * self.pitch

    def own(self, i):
        return pl.ds(i * self.Y, self.Y)

    def at(self, i, shift=0):
        return pl.ds(self.base(i) + shift, self.Y)

    def row_of_each(self, y):
        return pl.ds(self.base(0) + y, self.X, stride=self.pitch)


B0 = Block(16, 16, 128, 1.0)
B1 = Block(8, 8, 64, 0.25)
BLOCKS = (B0, B1)

SCRATCH = {}


def vmem(name, *shape):
    SCRATCH[name] = pltpu.VMEM(shape, F32)


def dma(name, *shape):
    SCRATCH[name] = pltpu.SemaphoreType.DMA(shape)


for key in ("rhs", "fx", "fy", "fz"):
    vmem(key, 256, 128)
dma("in_sem", 5)
for level, block in enumerate(BLOCKS):
    for key in ("cxl", "cxu", "cyl", "cyu", "czl", "czu", "g", "d15", "kw", "r", "w"):
        vmem(f"{key}{level}", block.rows, 128)
    vmem(f"va{level}", block.padded, 128)
    vmem(f"vb{level}", block.padded, 128)
    vmem(f"lyp{level}", block.X * block.pitch, 128)
for key in ("fx1", "fy1", "fz1"):
    vmem(key, 64, 128)
for key, rows, count in (
    ("a0", 16, 3), ("a1", 8, 3), ("b", 16, 6), ("c", 16, 6), ("d", 8, 6),
    ("e", 8, 6), ("f", 8, 6), ("q", 8, 6), ("h", 16, 6),
):
    vmem(f"{key}_snd", count, rows, 128)
    vmem(f"{key}_rcv", count, rows, 128)
    dma(f"{key}_ss", count)
    dma(f"{key}_rs", count)
vmem("t16", 3, 16, 128)
for key, arrays in (("zf", 3), ("zr", 1)):
    vmem(f"{key}_snd", 16, 128)
    vmem(f"{key}_rcv", 7, 16, 128)
    dma(f"{key}_ss", 7)
    dma(f"{key}_rs", 7)
for key, arrays in (("xf", 3), ("xr", 1)):
    vmem(f"{key}_snd", arrays * 2, 16, 128)
    vmem(f"{key}_rcv", 11, arrays * 2, 16, 128)
    dma(f"{key}_ss", 11)
    dma(f"{key}_rs", 11)
for key in ("f2", "lx2", "ly2", "lz2", "va2", "vb2"):
    vmem(key, 36, 16, 128)
for key in ("cxl2", "cxu2", "cyl2", "cyu2", "czl2", "czu2", "g2", "d152", "kw2"):
    vmem(key, 36, 16, 128)
vmem("s2", 128, 128)
vmem("p2", 256, 128)
vmem("face3", 3, 128, 128)
vmem("f3", 128, 128)
for key in ("yf", "yr"):
    dma(f"{key}_ss", 7)
    dma(f"{key}_rs", 7)
for key in ("cxl3", "cxu3", "cyl3", "cyu3", "czl3", "czu3", "g3", "d153", "kw3", "r3", "p3"):
    vmem(key, 128, 128)
vmem("va3", 160, 128)
vmem("vb3", 160, 128)
for key in ("t4", "cxl4", "cxu4", "cyl4", "cyu4", "czl4", "czu4", "d154", "kw4", "r4", "p4"):
    vmem(key, 32, 128)
vmem("fc4", 3, 32, 128)
for key in ("t5", "cx5", "cyl5", "cyu5", "czl5", "czu5", "kw5", "e5"):
    vmem(key, 8, 128)
vmem("q1", 96, 128)
vmem("h1", 6, 8, 128)


class Space:
    pass


def cycle(rhs_in, fx_in, fy_in, fz_in, out, *scratch):
    s = Space()
    for name, ref in zip(SCRATCH, scratch):
        setattr(s, name, ref)
    gx, gy, gz = lax.axis_index("gx"), lax.axis_index("gy"), lax.axis_index("gz")

    def peer(offset):
        return (
            (gx + offset[0]) & (GX - 1),
            (gy + offset[1]) & (GY - 1),
            (gz + offset[2]) & (GZ - 1),
        )

    loads = [
        pltpu.make_async_copy(source, target, s.in_sem.at[k])
        for k, (source, target) in enumerate(
            ((fx_in, s.fx), (fy_in, s.fy), (fz_in, s.fz), (rhs_in, s.rhs))
        )
    ]
    for load in loads:
        load.start()

    barrier = pltpu.get_barrier_semaphore()
    friends = list(dict.fromkeys(RING_Y + RING_Z + PLANE))
    friends = list(dict.fromkeys((x & 3, y & 7, z & 7) for x, y, z in friends))
    for offset in friends:
        pl.semaphore_signal(barrier, inc=1, device_id=peer(offset), device_id_type=MESH)

    def copies(offsets, sources, targets, ss, rs):
        made = [
            pltpu.make_async_remote_copy(
                src_ref=sources(k),
                dst_ref=targets(k),
                send_sem=ss.at[k],
                recv_sem=rs.at[k],
                device_id=peer(offset),
                device_id_type=MESH,
            )
            for k, offset in enumerate(offsets)
        ]
        for one in made:
            one.start()
        return made

    def finish(made):
        for one in made:
            one.wait_recv()
        for one in made:
            one.wait_send()

    def flag(condition):
        return jnp.where(condition, 1.0, 0.0).astype(F32)

    low_x, low_y, low_z = flag(gx > 0), flag(gy > 0), flag(gz > 0)
    top_x, top_y, top_z = flag(gx < GX - 1), flag(gy < GY - 1), flag(gz < GZ - 1)


    def pack(read, block, column):
        packed = jnp.zeros((block.Y, 128), F32)
        lane = lanes(block.Y)
        for i in range(block.X):
            packed = jnp.where(lane == i, turn(read(i), i - column), packed)
        return packed

    def send_faces(block, ref, key):
        snd = getattr(s, key + "_snd")
        snd[0] = ref[block.at(block.X - 1)]
        snd[1] = ref[block.at(0)]
        snd[2] = ref[block.row_of_each(block.Y - 1)]
        snd[3] = ref[block.row_of_each(0)]
        snd[4] = pack(lambda i: ref[block.at(i)], block, block.Z - 1)
        snd[5] = pack(lambda i: ref[block.at(i)], block, 0)
        rcv = getattr(s, key + "_rcv")
        return copies(
            FACES,
            lambda k: snd.at[k],
            lambda k: rcv.at[k],
            getattr(s, key + "_ss"),
            getattr(s, key + "_rs"),
        )

    def fill(block, ref, halo):
        ref[block.at(-1)] = halo[0]
        ref[block.at(block.X)] = halo[1]
        ref[block.row_of_each(-1)] = halo[2]
        ref[block.row_of_each(block.Y)] = halo[3]

    def send_upper(level, lx, ly, lz, key):
        block = BLOCKS[level]
        snd = getattr(s, key + "_snd")
        snd[0] = lx[block.own(0)]
        snd[1] = ly[pl.ds(0, block.X, stride=block.Y)]
        snd[2] = pack(lambda i: lz[block.own(i)], block, 0)
        rcv = getattr(s, key + "_rcv")
        return copies(
            DOWN,
            lambda k: snd.at[k],
            lambda k: rcv.at[k],
            getattr(s, key + "_ss"),
            getattr(s, key + "_rs"),
        )

    def coefficients(level, lx, ly, lz, key):
        block = BLOCKS[level]
        rcv = getattr(s, key + "_rcv")
        lyp = getattr(s, f"lyp{level}")
        c = {k: getattr(s, f"{k}{level}") for k in ("cxl", "cxu", "cyl", "cyu", "czl", "czu")}
        d15, kw = getattr(s, f"d15{level}"), getattr(s, f"kw{level}")
        for i in range(block.X):
            lyp[pl.ds(i * block.pitch, block.Y)] = ly[block.own(i)]
        lyp[pl.ds(block.Y, block.X, stride=block.pitch)] = rcv[1] * top_y
        next_x = rcv[0] * top_x
        next_z = rcv[2] * top_z
        lane, row = lanes(block.Y), sublanes(block.Y)
        keep_y = jnp.where(row == 0, low_y, 1.0)
        keep_z = jnp.where(lane == 0, low_z, 1.0)
        for i in range(block.X):
            own = block.own(i)
            a_xl = lx[own]
            a_xu = lx[block.own(i + 1)] if i + 1 < block.X else next_x
            a_yl = ly[own]
            a_yu = lyp[pl.ds(i * block.pitch + 1, block.Y)]
            a_zl = lz[own]
            a_zu = jnp.where(
                lane == block.Z - 1, turn(next_z, block.Z - 1 - i), turn(a_zl, -1)
            )
            total = (a_xl + a_yl + a_zl) + (a_xu + a_yu + a_zu)
            scale = RELAX / total
            d15[own] = (1.5 * block.weight) * total
            kw[own] = scale * (1.0 / block.weight)
            c["cxl"][own] = scale * a_xl * (low_x if i == 0 else 1.0)
            c["cxu"][own] = scale * a_xu
            c["cyl"][own] = scale * a_yl * keep_y
            c["cyu"][own] = scale * a_yu
            c["czl"][own] = scale * a_zl * keep_z
            c["czu"][own] = scale * a_zu

    def stencil(level, ref, low, high, emit):
        block = BLOCKS[level]
        lane = lanes(block.Y)
        get = lambda k: getattr(s, f"{k}{level}")
        for i in range(block.X):
            own = block.own(i)
            v = ref[block.at(i)]
            down = jnp.where(lane == 0, turn(low, -i), turn(v, 1))
            up = jnp.where(lane == block.Z - 1, turn(high, block.Z - 1 - i), turn(v, -1))
            t_x = get("cxl")[own] * ref[block.at(i - 1)] + get("cxu")[own] * ref[block.at(i + 1)]
            t_y = get("cyl")[own] * ref[block.at(i, -1)] + get("cyu")[own] * ref[block.at(i, 1)]
            t_z = get("czl")[own] * down + get("czu")[own] * up
            emit(i, v, get("g")[own] + (t_x + t_y + t_z))

    def smooth(level, source, target, low, high):
        block = BLOCKS[level]

        def emit(i, v, total):
            target[block.at(i)] = v * THIRD + total

        stencil(level, source, low, high, emit)

    def residual(level, source, low, high):
        block = BLOCKS[level]
        d15, r = getattr(s, f"d15{level}"), getattr(s, f"r{level}")

        def emit(i, v, total):
            r[block.own(i)] = d15[block.own(i)] * (total - RELAX * v)

        stencil(level, source, low, high, emit)

    lane8, lane16 = lanes(8), lanes(16)
    even8 = (2 * lane8) & 127
    half16 = lane16 >> 1

    def pair_z(value):
        return value + turn(value, -1)

    def stage_z(arrays, snd):
        group = lane16 >> 4
        packed = jnp.zeros((16, 128), F32)
        for a in range(arrays):
            whole = s.t16[a]
            for p in range(2):
                moved = take(whole, 4 * (lane16 & 15) + 2 * p)
                packed = jnp.where(group == ((gz + 2 * a + p) & 7), moved, packed)
        snd[...] = packed

    def merge_z(arrays, snd, rcv, target):
        group = lane16 >> 4
        parts = [(0, snd[...])] + [(RING_Z[k][2], rcv[k]) for k in range(7)]
        for q in range(2 * arrays):
            merged = jnp.zeros((16, 128), F32)
            for distance, part in parts:
                merged = jnp.where(group == ((gz - distance + q) & 7), part, merged)
            target[q] = turn(merged, -16 * q)

    for load in loads[:3]:
        load.wait()
    for i in range(8):
        own = pl.ds(8 * i, 8)
        here = lambda ref, shift: ref[pl.ds(32 * i + shift, 8, stride=2)]
        s.fx1[own] = take(pair_z(here(s.fx, 0) + here(s.fx, 1)), even8) * 0.25
        s.fy1[own] = take(pair_z(here(s.fy, 0) + here(s.fy, 16)), even8) * 0.25
        total = (here(s.fz, 0) + here(s.fz, 1)) + (here(s.fz, 16) + here(s.fz, 17))
        s.fz1[own] = take(total, even8) * 0.25
    for i in range(4):
        own = pl.ds(4 * i, 4)
        here = lambda ref, shift: ref[pl.ds(16 * i + shift, 4, stride=2)]
        s.t16[0, own] = here(s.fx1, 0) + here(s.fx1, 1)
        s.t16[1, own] = here(s.fy1, 0) + here(s.fy1, 8)
        total = (here(s.fz1, 0) + here(s.fz1, 1)) + (here(s.fz1, 8) + here(s.fz1, 9))
        s.t16[2, own] = total * 0.25
    s.t16[0] = pair_z(s.t16[0]) * 0.25
    s.t16[1] = pair_z(s.t16[1]) * 0.25
    stage_z(3, s.zf_snd)
    for ref in (s.va0, s.vb0, s.va1, s.vb1):
        ref[...] = jnp.zeros_like(ref)
    for ref in (s.lx2, s.ly2, s.lz2):
        ref[...] = jnp.ones_like(ref)
    for ref in (s.f2, s.va2, s.vb2):
        ref[...] = jnp.zeros_like(ref)
    for ref in (s.va3, s.vb3, s.p2):
        ref[...] = jnp.zeros_like(ref)

    pl.semaphore_wait(barrier, len(friends))
    round_a0 = send_upper(0, s.fx, s.fy, s.fz, "a0")
    round_a1 = send_upper(1, s.fx1, s.fy1, s.fz1, "a1")
    round_zf = copies(
        RING_Z, lambda k: s.zf_snd, lambda k: s.zf_rcv.at[k], s.zf_ss, s.zf_rs
    )
    loads[3].wait()
    finish(round_a0)
    coefficients(0, s.fx, s.fy, s.fz, "a0")
    for i in range(16):
        own = B0.own(i)
        start = s.kw0[own] * s.rhs[own]
        s.g0[own] = start
        s.va0[B0.at(i)] = start
    round_b = send_faces(B0, s.va0, "b")
    finish(round_a1)
    coefficients(1, s.fx1, s.fy1, s.fz1, "a1")
    finish(round_b)
    fill(B0, s.va0, s.b_rcv)
    smooth(0, s.va0, s.vb0, s.b_rcv[4], s.b_rcv[5])
    round_c = send_faces(B0, s.vb0, "c")
    finish(round_zf)
    merge_z(3, s.zf_snd, s.zf_rcv, s.xf_snd)
    finish(round_c)
    round_xf = copies(
        PLANE, lambda k: s.xf_snd, lambda k: s.xf_rcv.at[k], s.xf_ss, s.xf_rs
    )
    fill(B0, s.vb0, s.c_rcv)
    residual(0, s.vb0, s.c_rcv[4], s.c_rcv[5])

    for i in range(8):
        own = pl.ds(8 * i, 8)
        here = lambda shift: s.r0[pl.ds(32 * i + shift, 8, stride=2)]
        total = (here(0) + here(1)) + (here(16) + here(17))
        start = s.kw1[own] * (take(pair_z(total), even8) * 0.125)
        s.g1[own] = start
        s.va1[B1.at(i)] = start
    round_d = send_faces(B1, s.va1, "d")
    finish(round_d)
    fill(B1, s.va1, s.d_rcv)
    smooth(1, s.va1, s.vb1, s.d_rcv[4], s.d_rcv[5])
    round_e = send_faces(B1, s.vb1, "e")


    def block2(p, x):
        return 18 * p + 1 + x

    def spread(arrays, snd, rcv, targets):
        parts = [((0, 0, 0), lambda q: snd.at[q])]
        for k in range(11):
            parts.append((PLANE[k], lambda q, k=k: rcv.at[k, q]))
        for offset, part in parts:
            first = 4 * ((gx - offset[0]) & 3)
            place = pl.ds(4 * (1 - offset[1]), 4)
            for a in range(arrays):
                for p in range(2):
                    for x in range(4):
                        piece = part(2 * a + p)[pl.ds(4 * x, 4)]
                        targets[a][block2(p, x) + first, place] = piece

    finish(round_xf)
    spread(3, s.xf_snd, s.xf_rcv, (s.lx2, s.ly2, s.lz2))
    row16 = sublanes(16)
    global_y = row16 + 4 * gy - 4
    not_low, not_top = global_y != 0, global_y != 4 * GY - 1

    for a, ref in enumerate((s.lx2, s.ly2, s.lz2)):
        for i in range(8):
            total = ref[block2(0, 2 * i)]
            if a != 2:
                total = total + ref[block2(1, 2 * i)]
            if a != 0:
                total = total + ref[block2(0, 2 * i + 1)]
            if a == 1:
                total = total + ref[block2(1, 2 * i + 1)]
            s.s2[pl.ds(16 * i, 16)] = total
        for j in range(2):
            total = s.s2[pl.ds(4 + 2 * j, 8, stride=16)]
            if a != 1:
                total = total + s.s2[pl.ds(5 + 2 * j, 8, stride=16)]
            s.face3[a, pl.ds(pl.multiple_of(16 * gy + 8 * j, 8), 8)] = total * 0.25
    mine = pl.ds(pl.multiple_of(16 * gy, 16), 16)
    round_yf = copies(
        RING_Y,
        lambda k: s.face3.at[:, mine],
        lambda k: s.face3.at[:, mine],
        s.yf_ss,
        s.yf_rs,
    )

    for p in range(2):
        for x in range(16):
            j = block2(p, x)
            a_xl, a_yl, a_zl = s.lx2[j], s.ly2[j], s.lz2[j]
            a_xu = s.lx2[j + 1] if x < 15 else jnp.zeros((16, 128), F32)
            a_yu = jnp.where(not_top, turn(a_yl, -1, 0), 0.0)
            if p == 0:
                a_zu = s.lz2[block2(1, x)]
            else:
                a_zu = jnp.where(lane16 == 127, 0.0, turn(s.lz2[block2(0, x)], -1))
            total = (a_xl + a_yl + a_zl) + (a_xu + a_yu + a_zu)
            scale = RELAX / total
            s.d152[j] = (1.5 * 0.0625) * total
            s.kw2[j] = scale * 16.0
            s.cxl2[j] = scale * a_xl if x > 0 else jnp.zeros((16, 128), F32)
            s.cxu2[j] = scale * a_xu
            s.cyl2[j] = jnp.where(not_low, scale * a_yl, 0.0)
            s.cyu2[j] = scale * a_yu
            s.czl2[j] = scale * a_zl if p == 1 else jnp.where(lane16 == 0, 0.0, scale * a_zl)
            s.czu2[j] = scale * a_zu

    def stencil2(ref, emit):
        for p in range(2):
            for x in range(16):
                j, other = block2(p, x), block2(1 - p, x)
                v, w = ref[j], ref[other]
                t_x = s.cxl2[j] * ref[j - 1] + s.cxu2[j] * ref[j + 1]
                t_y = s.cyl2[j] * turn(v, 1, 0) + s.cyu2[j] * turn(v, -1, 0)
                down, up = (turn(w, 1), w) if p == 0 else (w, turn(w, -1))
                t_z = s.czl2[j] * down + s.czu2[j] * up
                emit(j, v, s.g2[j] + (t_x + t_y + t_z))

    def smooth2(source, target):
        def emit(j, v, total):
            target[j] = v * THIRD + total

        stencil2(source, emit)

    finish(round_e)
    fill(B1, s.vb1, s.e_rcv)
    residual(1, s.vb1, s.e_rcv[4], s.e_rcv[5])
    for i in range(4):
        here = lambda shift: s.r1[pl.ds(16 * i + shift, 4, stride=2)]
        s.t16[0, pl.ds(4 * i, 4)] = (here(0) + here(1)) + (here(8) + here(9))
    s.t16[0] = pair_z(s.t16[0]) * 0.125
    stage_z(1, s.zr_snd)
    round_zr = copies(
        RING_Z, lambda k: s.zr_snd, lambda k: s.zr_rcv.at[k], s.zr_ss, s.zr_rs
    )

    finish(round_yf)
    row8 = sublanes(8)
    zero8 = jnp.zeros((8, 128), F32)
    for y in range(16):
        own = pl.ds(8 * y, 8)
        a_xl, a_yl, a_zl = s.face3[0, own], s.face3[1, own], s.face3[2, own]
        a_xu = jnp.where(row8 == 7, 0.0, turn(a_xl, -1, 0))
        a_yu = s.face3[1, pl.ds(8 * y + 8, 8)] if y < 15 else zero8
        a_zu = jnp.where(lane8 == 127, 0.0, turn(a_zl, -1))
        total = (a_xl + a_yl + a_zl) + (a_xu + a_yu + a_zu)
        scale = RELAX / total
        s.d153[own] = (1.5 * 0.25**3) * total
        s.kw3[own] = scale * 64.0
        s.cxl3[own] = jnp.where(row8 == 0, 0.0, scale * a_xl)
        s.cxu3[own] = scale * a_xu
        s.cyl3[own] = scale * a_yl if y > 0 else zero8
        s.cyu3[own] = scale * a_yu
        s.czl3[own] = jnp.where(lane8 == 0, 0.0, scale * a_zl)
        s.czu3[own] = scale * a_zu

    lane32, row32 = lanes(32), sublanes(32)

    def both(value, lane, step):
        return value + jnp.where(
            (lane & step) == 0, turn(value, -step), turn(value, step)
        )

    def lower_of(value, lane, step):
        return jnp.where((lane & step) == 0, value, turn(value, step))

    for a in range(3):
        for y in range(8):
            here = lambda shift: s.face3[a, pl.ds(16 * y + shift, 4, stride=2)]
            if a == 0:
                total = here(0) + here(8)
            elif a == 1:
                total = here(0) + here(1)
            else:
                total = (here(0) + here(1)) + (here(8) + here(9))
            s.t4[pl.ds(4 * y, 4)] = total
        total = s.t4[...]
        total = both(total, lane32, 1) if a < 2 else lower_of(total, lane32, 1)
        s.fc4[a] = total * 0.25
    a_xl, a_yl, a_zl = s.fc4[0], s.fc4[1], s.fc4[2]
    a_xu = jnp.where((row32 & 3) == 3, 0.0, turn(a_xl, -1, 0))
    a_yu = jnp.where(row32 >= 28, 0.0, turn(a_yl, -4, 0))
    a_zu = jnp.where(lane32 >= 126, 0.0, turn(a_zl, -2))
    total = (a_xl + a_yl + a_zl) + (a_xu + a_yu + a_zu)
    scale = RELAX / total
    s.d154[...] = (1.5 * 0.25**4) * total
    s.kw4[...] = scale * 256.0
    s.cxl4[...] = jnp.where((row32 & 3) == 0, 0.0, scale * a_xl)
    s.cxu4[...] = scale * a_xu
    s.cyl4[...] = jnp.where(row32 < 4, 0.0, scale * a_yl)
    s.cyu4[...] = scale * a_yu
    s.czl4[...] = jnp.where(lane32 < 2, 0.0, scale * a_zl)
    s.czu4[...] = scale * a_zu

    faces5 = []
    for a in range(3):
        for x in range(2):
            here = lambda shift: s.fc4[a, pl.ds(2 * x + shift, 4, stride=8)]
            if a == 0:
                total = here(0) + here(4)
            elif a == 1:
                total = here(0) + here(1)
            else:
                total = (here(0) + here(1)) + (here(4) + here(5))
            s.t5[pl.ds(4 * x, 4)] = total
        total = s.t5[...]
        total = both(total, lane8, 2) if a < 2 else lower_of(total, lane8, 2)
        faces5.append(total * 0.25)
    a_xl, a_yl, a_zl = faces5
    a_xu = jnp.where(row8 >= 4, 0.0, turn(a_xl, 4, 0))
    a_yu = jnp.where((row8 & 3) == 3, 0.0, turn(a_yl, -1, 0))
    a_zu = jnp.where(lane8 >= 124, 0.0, turn(a_zl, -4))
    total = (a_xl + a_yl + a_zl) + (a_xu + a_yu + a_zu)
    scale = RELAX / total
    s.kw5[...] = scale * 1024.0
    s.cx5[...] = jnp.where(row8 >= 4, scale * a_xl, scale * a_xu)
    s.cyl5[...] = jnp.where((row8 & 3) == 0, 0.0, scale * a_yl)
    s.cyu5[...] = scale * a_yu
    s.czl5[...] = jnp.where(lane8 < 4, 0.0, scale * a_zl)
    s.czu5[...] = scale * a_zu

    finish(round_zr)
    merge_z(1, s.zr_snd, s.zr_rcv, s.xr_snd)
    round_xr = copies(
        PLANE, lambda k: s.xr_snd, lambda k: s.xr_rcv.at[k], s.xr_ss, s.xr_rs
    )
    finish(round_xr)
    spread(1, s.xr_snd, s.xr_rcv, (s.f2,))
    for p in range(2):
        for x in range(16):
            j = block2(p, x)
            start = s.kw2[j] * s.f2[j]
            s.g2[j] = start
            s.va2[j] = start
    smooth2(s.va2, s.vb2)

    def emit_r2(j, v, total):
        s.f2[j] = s.d152[j] * (total - RELAX * v)

    stencil2(s.vb2, emit_r2)
    for i in range(8):
        total = (s.f2[block2(0, 2 * i)] + s.f2[block2(1, 2 * i)]) + (
            s.f2[block2(0, 2 * i + 1)] + s.f2[block2(1, 2 * i + 1)]
        )
        s.s2[pl.ds(16 * i, 16)] = total
    for j in range(2):
        total = s.s2[pl.ds(4 + 2 * j, 8, stride=16)] + s.s2[pl.ds(5 + 2 * j, 8, stride=16)]
        s.f3[pl.ds(pl.multiple_of(16 * gy + 8 * j, 8), 8)] = total * 0.125
    round_yr = copies(
        RING_Y, lambda k: s.f3.at[mine], lambda k: s.f3.at[mine], s.yr_ss, s.yr_rs
    )
    finish(round_yr)

    def at3(y):
        return pl.ds(16 + 8 * y, 8)

    def stencil3(ref, emit):
        for y in range(16):
            own = pl.ds(8 * y, 8)
            v = ref[at3(y)]
            t_x = s.cxl3[own] * turn(v, 1, 0) + s.cxu3[own] * turn(v, -1, 0)
            t_y = s.cyl3[own] * ref[at3(y - 1)] + s.cyu3[own] * ref[at3(y + 1)]
            t_z = s.czl3[own] * turn(v, 1) + s.czu3[own] * turn(v, -1)
            emit(y, v, s.g3[own] + (t_x + t_y + t_z))

    def smooth3(source, target):
        def emit(y, v, total):
            target[at3(y)] = v * THIRD + total

        stencil3(source, emit)

    for y in range(16):
        own = pl.ds(8 * y, 8)
        start = s.kw3[own] * s.f3[own]
        s.g3[own] = start
        s.va3[at3(y)] = start
    smooth3(s.va3, s.vb3)

    def emit_r3(y, v, total):
        own = pl.ds(8 * y, 8)
        s.r3[own] = s.d153[own] * (total - RELAX * v)

    stencil3(s.vb3, emit_r3)
    for y in range(8):
        here = lambda shift: s.r3[pl.ds(16 * y + shift, 4, stride=2)]
        s.t4[pl.ds(4 * y, 4)] = (here(0) + here(1)) + (here(8) + here(9))
    f4 = both(s.t4[...], lane32, 1) * 0.125

    def total4(v):
        t_x = s.cxl4[...] * turn(v, 1, 0) + s.cxu4[...] * turn(v, -1, 0)
        t_y = s.cyl4[...] * turn(v, 4, 0) + s.cyu4[...] * turn(v, -4, 0)
        t_z = s.czl4[...] * turn(v, 2) + s.czu4[...] * turn(v, -2)
        return g4 + (t_x + t_y + t_z)

    g4 = s.kw4[...] * f4
    v4 = g4
    v4 = v4 * THIRD + total4(v4)
    s.r4[...] = s.d154[...] * (total4(v4) - RELAX * v4)
    for x in range(2):
        here = lambda shift: s.r4[pl.ds(2 * x + shift, 4, stride=8)]
        s.t5[pl.ds(4 * x, 4)] = (here(0) + here(1)) + (here(4) + here(5))
    g5 = s.kw5[...] * (both(s.t5[...], lane8, 2) * 0.125)
    cx5, cyl5, cyu5, czl5, czu5 = s.cx5[...], s.cyl5[...], s.cyu5[...], s.czl5[...], s.czu5[...]

    def sweep5(index, v):
        t_y = cyl5 * turn(v, 1, 0) + cyu5 * turn(v, -1, 0)
        t_z = czl5 * turn(v, 4) + czu5 * turn(v, -4)
        return (v * THIRD + g5) + (cx5 * turn(v, 4, 0) + (t_y + t_z))

    s.e5[...] = lax.fori_loop(0, COARSE_SWEEPS - 1, sweep5, g5)
    for x in range(2):
        piece = s.e5[pl.ds(4 * x, 4)]
        for shift in (0, 1, 4, 5):
            s.p4[pl.ds(2 * x + shift, 4, stride=8)] = piece
    v4 = v4 + s.p4[...]
    v4 = v4 * THIRD + total4(v4)
    v4 = v4 * THIRD + total4(v4)
    s.r4[...] = v4
    for x in range(4):
        piece = s.r4[pl.ds(x, 8, stride=4)]
        for shift in (0, 1, 8, 9):
            s.p3[pl.ds(2 * x + shift, 8, stride=16)] = piece
    for y in range(16):
        s.vb3[at3(y)] = s.vb3[at3(y)] + s.p3[pl.ds(8 * y, 8)]
    smooth3(s.vb3, s.va3)
    smooth3(s.va3, s.vb3)

    for k in range(6):
        piece = s.vb3[pl.ds(pl.multiple_of(16 * gy + 8 * k, 8), 8)]
        for x in range(2):
            for y in range(2):
                s.p2[pl.ds(16 * x + 2 * k + y, 8, stride=32)] = piece
    for x in range(16):
        more = s.p2[pl.ds(16 * x, 16)]
        for p in range(2):
            s.vb2[block2(p, x)] = s.vb2[block2(p, x)] + more
    smooth2(s.vb2, s.va2)
    smooth2(s.va2, s.vb2)

    signed = jnp.where(lane16 < 96, lane16, lane16 - 128)
    index = (16 * gz + (signed >> 2)) & 127
    odd = ((signed >> 1) & 1) == 1
    for k in range(6):
        x = 4 * gx + k - 1
        s.q1[pl.ds(16 * k, 16)] = jnp.where(
            odd, take(s.vb2[block2(1, x)], index), take(s.vb2[block2(0, x)], index)
        )
    for k, source in ((0, 0), (1, 5)):
        for y in range(2):
            s.h1[k, pl.ds(y, 4, stride=2)] = s.q1[pl.ds(16 * source + 4, 4)]
    for k, source in ((2, 3), (3, 8)):
        for x in range(2):
            s.h1[k, pl.ds(x, 4, stride=2)] = s.q1[pl.ds(16 + source, 4, stride=16)]
    for i in range(8):
        for y in range(2):
            s.w1[pl.ds(8 * i + y, 4, stride=2)] = s.q1[pl.ds(16 * (i // 2 + 1) + 4, 4)]
    s.h1[4] = pack(lambda i: s.w1[B1.own(i)], B1, 127)
    s.h1[5] = pack(lambda i: s.w1[B1.own(i)], B1, 64)
    for k in range(6):
        s.h1[k] = s.h1[k] + s.e_rcv[k]
    for i in range(8):
        s.vb1[B1.at(i)] = s.vb1[B1.at(i)] + s.w1[B1.own(i)]
    fill(B1, s.vb1, s.h1)
    smooth(1, s.vb1, s.va1, s.h1[4], s.h1[5])
    round_f = send_faces(B1, s.va1, "f")
    finish(round_f)
    fill(B1, s.va1, s.f_rcv)
    smooth(1, s.va1, s.vb1, s.f_rcv[4], s.f_rcv[5])
    round_q = send_faces(B1, s.vb1, "q")

    def widen(value, ref, start):
        ref[pl.ds(start, 8, stride=2)] = value
        ref[pl.ds(start + 1, 8, stride=2)] = value
        return take(ref[pl.ds(start, 16)], half16)

    for i in range(8):
        more = widen(s.vb1[B1.at(i)], s.w0, 16 * i)
        for x in (2 * i, 2 * i + 1):
            s.vb0[B0.at(x)] = s.vb0[B0.at(x)] + more
    finish(round_q)
    for k in range(6):
        s.c_rcv[k] = s.c_rcv[k] + widen(s.q_rcv[k], s.w0, 128 + 16 * k)
    fill(B0, s.vb0, s.c_rcv)
    smooth(0, s.vb0, s.va0, s.c_rcv[4], s.c_rcv[5])
    round_h = send_faces(B0, s.va0, "h")
    finish(round_h)
    fill(B0, s.va0, s.h_rcv)

    def emit_out(i, v, total):
        out[B0.own(i)] = v * THIRD + total

    stencil(0, s.va0, s.h_rcv[4], s.h_rcv[5], emit_out)


def shards(rhs, face_x, face_y, face_z):
    flat = [a.reshape(256, 128) for a in (rhs, face_x, face_y, face_z)]
    whole = pl.pallas_call(
        cycle,
        out_shape=jax.ShapeDtypeStruct((256, 128), F32),
        in_specs=[pl.BlockSpec(memory_space=pl.ANY)] * 4,
        out_specs=pl.BlockSpec(memory_space=pltpu.VMEM),
        scratch_shapes=list(SCRATCH.values()),
        compiler_params=pltpu.CompilerParams(
            collective_id=0, has_side_effects=True, vmem_limit_bytes=48 * 1024 * 1024
        ),
        name="vcycle",
    )(*flat)
    return whole.reshape(16, 16, 128)


def solution(mesh):
    placed = P("gx", "gy", "gz")
    return jax.shard_map(
        shards, mesh=mesh, in_specs=(placed,) * 4, out_specs=placed, check_vma=False
    )
```

```python
import jax
import jax.numpy as jnp
from jax import lax
from jax.experimental import pallas as pl
from jax.experimental.pallas import tpu as pltpu
from jax.sharding import PartitionSpec as P

RELAX = 2.0 / 3.0
THIRD = 1.0 / 3.0
COARSE_SWEEPS = 24
GX, GY, GZ = 4, 8, 8
F32 = jnp.float32
MESH = pl.DeviceIdType.MESH

FACES = [(1, 0, 0), (-1, 0, 0), (0, 1, 0), (0, -1, 0), (0, 0, 1), (0, 0, -1)]
DOWN = [(-1, 0, 0), (0, -1, 0), (0, 0, -1)]
RING_Z = [(0, 0, k) for k in (4, 3, 5, 2, 6, 1, 7)]
RING_Y = [(0, k, 0) for k in (4, 3, 5, 2, 6, 1, 7)]
AROUND = [
    (x, y, z) for x in (1, -1, 0) for y in (1, -1, 0) for z in (1, -1, 0) if (x, y, z) != (0, 0, 0)
]
AROUND.sort(key=lambda d: -(abs(d[0]) + abs(d[1]) + abs(d[2])))
LINE = [(2, 0, 0), (1, 0, 0), (3, 0, 0)]
SIDES = [(0, 1, 0), (0, -1, 0)]
PLANE = [(2, 1, 0), (2, -1, 0), (1, 1, 0), (1, -1, 0), (3, 1, 0), (3, -1, 0)]
PLANE += [(2, 0, 0), (0, 1, 0), (0, -1, 0), (1, 0, 0), (3, 0, 0)]


def lanes(rows):
    return lax.broadcasted_iota(jnp.int32, (rows, 128), 1)


def sublanes(rows):
    return lax.broadcasted_iota(jnp.int32, (rows, 128), 0)


def turn(value, steps, axis=1):
    steps %= value.shape[axis]
    return value if steps == 0 else pltpu.roll(value, steps, axis)


def take(value, index):
    return jnp.take_along_axis(value, index, axis=1, mode="promise_in_bounds")


class Block:
    def __init__(self, size_x, size_y, size_z, weight):
        self.X, self.Y, self.Z, self.weight = size_x, size_y, size_z, weight
        self.pitch = size_y + 8
        self.rows = size_x * size_y
        self.padded = 8 + (size_x + 2) * self.pitch

    def base(self, i):
        return 8 + (i + 1) * self.pitch

    def own(self, i):
        return pl.ds(i * self.Y, self.Y)

    def at(self, i, shift=0):
        return pl.ds(self.base(i) + shift, self.Y)

    def row_of_each(self, y):
        return pl.ds(self.base(0) + y, self.X, stride=self.pitch)


B0 = Block(16, 16, 128, 1.0)

SCRATCH = {}


def vmem(name, *shape):
    SCRATCH[name] = pltpu.VMEM(shape, F32)


def dma(name, *shape):
    SCRATCH[name] = pltpu.SemaphoreType.DMA(shape)


for key in ("rhs", "fx", "fy", "fz"):
    vmem(key, 256, 128)
dma("in_sem", 5)
for key in ("cxl0", "cxu0", "cyl0", "cyu0", "czl0", "czu0", "g0", "d150", "kw0", "r0", "w0"):
    vmem(key, 256, 128)
vmem("va0", B0.padded, 128)
vmem("vb0", B0.padded, 128)
vmem("lyp0", B0.X * B0.pitch, 128)
for key in ("fx1", "fy1", "fz1", "r1"):
    vmem(key, 64, 128)
for key in ("cxl1", "cxu1", "cyl1", "cyu1", "czl1", "czu1", "g1", "d151", "kw1"):
    vmem(key, 17 * 16, 128)
for key in ("va1", "vb1"):
    vmem(key, 19 * 16, 128)
for key, arrays in (("hf", 4), ("hr", 1)):
    vmem(f"{key}_own", arrays, 8, 8, 128)
    vmem(f"{key}_low", arrays, 4, 8, 128)
    vmem(f"{key}_high", arrays, 4, 8, 128)
    vmem(f"{key}_zed", arrays, 8, 128)
    vmem(f"{key}_xr", 2, arrays, 5, 8, 128)
    vmem(f"{key}_yr", 6, arrays, 4, 8, 128)
    vmem(f"{key}_zr", 18, arrays, 8, 128)
    vmem(f"{key}_ext", arrays, 17 * 16, 128)
    dma(f"{key}_ss", 26)
    dma(f"{key}_rs", 26)
vmem("a1_snd", 8, 128)
vmem("a1_rcv", 8, 128)
dma("a1_ss", 1)
dma("a1_rs", 1)
vmem("lyp1", 8 * 16, 128)
vmem("q1", 8 * 16, 128)
vmem("h1", 6, 8, 128)
for key, rows, count in (("a0", 16, 3), ("b", 16, 6), ("c", 16, 6), ("h", 16, 6)):
    vmem(f"{key}_snd", count, rows, 128)
    vmem(f"{key}_rcv", count, rows, 128)
    dma(f"{key}_ss", count)
    dma(f"{key}_rs", count)
vmem("t16", 3, 16, 128)
for key, arrays in (("zf", 3), ("zr", 1)):
    vmem(f"{key}_snd", 16, 128)
    vmem(f"{key}_rcv", 7, 16, 128)
    dma(f"{key}_ss", 7)
    dma(f"{key}_rs", 7)
for key, arrays in (("xf", 3), ("xr", 1)):
    vmem(f"{key}_snd", arrays * 2, 16, 128)
    vmem(f"{key}_rcv", 11, arrays * 2, 16, 128)
    dma(f"{key}_ss", 11)
    dma(f"{key}_rs", 11)
for key in ("f2", "lx2", "ly2", "lz2", "va2", "vb2"):
    vmem(key, 2, 20, 16, 128)
for key in ("cxl2", "cxu2", "cyl2", "cyu2", "czl2", "czu2", "g2", "d152", "kw2"):
    vmem(key, 2, 20, 16, 128)
for key, arrays in (("nf", 3), ("nv", 1)):
    vmem(f"{key}_snd", arrays, 2, 8, 8, 128)
    vmem(f"{key}_rcv", 2, arrays, 2, 8, 8, 128)
    dma(f"{key}_ss", 2)
    dma(f"{key}_rs", 2)
vmem("s2", 128, 128)
vmem("p2", 256, 128)
vmem("face3", 3, 128, 128)
vmem("f3", 128, 128)
for key in ("yf", "yr"):
    dma(f"{key}_ss", 7)
    dma(f"{key}_rs", 7)
for key in ("cxl3", "cxu3", "cyl3", "cyu3", "czl3", "czu3", "g3", "d153", "kw3", "r3", "p3"):
    vmem(key, 128, 128)
vmem("va3", 160, 128)
vmem("vb3", 160, 128)
for key in ("t4", "cxl4", "cxu4", "cyl4", "cyu4", "czl4", "czu4", "d154", "kw4", "r4", "p4"):
    vmem(key, 32, 128)
vmem("fc4", 3, 32, 128)
for key in ("t5", "cx5", "cyl5", "cyu5", "czl5", "czu5", "kw5", "e5"):
    vmem(key, 8, 128)


class Space:
    pass


def cycle(rhs_in, fx_in, fy_in, fz_in, out, *scratch):
    s = Space()
    for name, ref in zip(SCRATCH, scratch):
        setattr(s, name, ref)
    gx, gy, gz = lax.axis_index("gx"), lax.axis_index("gy"), lax.axis_index("gz")

    def peer(offset):
        return (
            (gx + offset[0]) & (GX - 1),
            (gy + offset[1]) & (GY - 1),
            (gz + offset[2]) & (GZ - 1),
        )

    loads = [
        pltpu.make_async_copy(source, target, s.in_sem.at[k])
        for k, (source, target) in enumerate(
            ((fx_in, s.fx), (fy_in, s.fy), (fz_in, s.fz), (rhs_in, s.rhs))
        )
    ]
    for load in loads:
        load.start()

    barrier = pltpu.get_barrier_semaphore()
    friends = [(x & 3, y & 7, z & 7) for x, y, z in RING_Z + AROUND]
    friends = list(dict.fromkeys(friends))
    for offset in friends:
        pl.semaphore_signal(barrier, inc=1, device_id=peer(offset), device_id_type=MESH)

    def copies(offsets, sources, targets, ss, rs):
        made = [
            pltpu.make_async_remote_copy(
                src_ref=sources(k),
                dst_ref=targets(k),
                send_sem=ss.at[k],
                recv_sem=rs.at[k],
                device_id=peer(offset),
                device_id_type=MESH,
            )
            for k, offset in enumerate(offsets)
        ]
        for one in made:
            one.start()
        return made

    def finish(made):
        for one in made:
            one.wait_recv()
        for one in made:
            one.wait_send()

    def flag(condition):
        return jnp.where(condition, 1.0, 0.0).astype(F32)

    low_x, low_y, low_z = flag(gx > 0), flag(gy > 0), flag(gz > 0)
    top_x, top_y, top_z = flag(gx < GX - 1), flag(gy < GY - 1), flag(gz < GZ - 1)


    def pack(read, rows, count, column):
        packed = jnp.zeros((rows, 128), F32)
        lane = lanes(rows)
        for i in range(count):
            packed = jnp.where(lane == i, turn(read(i), i - column), packed)
        return packed

    def send_faces(block, ref, key):
        snd = getattr(s, key + "_snd")
        snd[0] = ref[block.at(block.X - 1)]
        snd[1] = ref[block.at(0)]
        snd[2] = ref[block.row_of_each(block.Y - 1)]
        snd[3] = ref[block.row_of_each(0)]
        snd[4] = pack(lambda i: ref[block.at(i)], 16, 16, 127)
        snd[5] = pack(lambda i: ref[block.at(i)], 16, 16, 0)
        rcv = getattr(s, key + "_rcv")
        return copies(
            FACES,
            lambda k: snd.at[k],
            lambda k: rcv.at[k],
            getattr(s, key + "_ss"),
            getattr(s, key + "_rs"),
        )

    def fill(block, ref, halo):
        ref[block.at(-1)] = halo[0]
        ref[block.at(block.X)] = halo[1]
        ref[block.row_of_each(-1)] = halo[2]
        ref[block.row_of_each(block.Y)] = halo[3]

    def send_upper(lx, ly, lz, key):
        block = B0
        snd = getattr(s, key + "_snd")
        snd[0] = lx[block.own(0)]
        snd[1] = ly[pl.ds(0, block.X, stride=block.Y)]
        snd[2] = pack(lambda i: lz[block.own(i)], 16, 16, 0)
        rcv = getattr(s, key + "_rcv")
        return copies(
            DOWN,
            lambda k: snd.at[k],
            lambda k: rcv.at[k],
            getattr(s, key + "_ss"),
            getattr(s, key + "_rs"),
        )

    def coefficients(level, lx, ly, lz, key):
        block = B0
        rcv = getattr(s, key + "_rcv")
        lyp = getattr(s, f"lyp{level}")
        c = {k: getattr(s, f"{k}{level}") for k in ("cxl", "cxu", "cyl", "cyu", "czl", "czu")}
        d15, kw = getattr(s, f"d15{level}"), getattr(s, f"kw{level}")
        for i in range(block.X):
            lyp[pl.ds(i * block.pitch, block.Y)] = ly[block.own(i)]
        lyp[pl.ds(block.Y, block.X, stride=block.pitch)] = rcv[1] * top_y
        next_x = rcv[0] * top_x
        next_z = rcv[2] * top_z
        lane, row = lanes(block.Y), sublanes(block.Y)
        keep_y = jnp.where(row == 0, low_y, 1.0)
        keep_z = jnp.where(lane == 0, low_z, 1.0)
        for i in range(block.X):
            own = block.own(i)
            a_xl = lx[own]
            a_xu = lx[block.own(i + 1)] if i + 1 < block.X else next_x
            a_yl = ly[own]
            a_yu = lyp[pl.ds(i * block.pitch + 1, block.Y)]
            a_zl = lz[own]
            a_zu = jnp.where(
                lane == block.Z - 1, turn(next_z, block.Z - 1 - i), turn(a_zl, -1)
            )
            total = (a_xl + a_yl + a_zl) + (a_xu + a_yu + a_zu)
            scale = RELAX / total
            d15[own] = (1.5 * block.weight) * total
            kw[own] = scale * (1.0 / block.weight)
            c["cxl"][own] = scale * a_xl * (low_x if i == 0 else 1.0)
            c["cxu"][own] = scale * a_xu
            c["cyl"][own] = scale * a_yl * keep_y
            c["cyu"][own] = scale * a_yu
            c["czl"][own] = scale * a_zl * keep_z
            c["czu"][own] = scale * a_zu

    def stencil(level, ref, low, high, emit):
        block = B0
        lane = lanes(block.Y)
        get = lambda k: getattr(s, f"{k}{level}")
        for i in range(block.X):
            own = block.own(i)
            v = ref[block.at(i)]
            down = jnp.where(lane == 0, turn(low, -i), turn(v, 1))
            up = jnp.where(lane == block.Z - 1, turn(high, block.Z - 1 - i), turn(v, -1))
            t_x = get("cxl")[own] * ref[block.at(i - 1)] + get("cxu")[own] * ref[block.at(i + 1)]
            t_y = get("cyl")[own] * ref[block.at(i, -1)] + get("cyu")[own] * ref[block.at(i, 1)]
            t_z = get("czl")[own] * down + get("czu")[own] * up
            emit(i, v, get("g")[own] + (t_x + t_y + t_z))

    def smooth(level, source, target, low, high):
        block = B0

        def emit(i, v, total):
            target[block.at(i)] = v * THIRD + total

        stencil(level, source, low, high, emit)

    def residual(level, source, low, high):
        block = B0
        d15, r = getattr(s, f"d15{level}"), getattr(s, f"r{level}")

        def emit(i, v, total):
            r[block.own(i)] = d15[block.own(i)] * (total - RELAX * v)

        stencil(level, source, low, high, emit)


    lane8, lane16 = lanes(8), lanes(16)
    row8, row16 = sublanes(8), sublanes(16)
    upper_half = row8 < 4
    slices_x = {1: (4, 4), -1: (0, 5), 0: (0, 8)}
    pairs_x = {1: (2, 2), -1: (0, 3), 0: (0, 4)}
    flat_yr = [(x, y) for x in (1, -1, 0) for y in (1, -1)]
    flat_zr = [(x, y, z) for x in (1, -1, 0) for y in (1, -1, 0) for z in (1, -1)]

    def send_around(arrays, key):
        get = lambda name: getattr(s, f"{key}_{name}")
        own, low, high, zed = get("own"), get("low"), get("high"), get("zed")
        for a in range(arrays):
            for i in range(4):
                even, odd = own[a, 2 * i], own[a, 2 * i + 1]
                low[a, i] = jnp.where(upper_half, even, turn(odd, 4, 0))
                high[a, i] = jnp.where(upper_half, turn(even, 4, 0), odd)
            packed = jnp.zeros((8, 128), F32)
            for x in range(8):
                v = own[a, x]
                packed = jnp.where((lane8 >> 3) == 2 * x, turn(v, 16 * x), packed)
                packed = jnp.where((lane8 >> 3) == 2 * x + 1, turn(v, 16 * x - 48), packed)
            zed[a] = packed

        def source(k):
            x, y, z = AROUND[k]
            if z != 0:
                return zed
            if y != 0:
                first, count = pairs_x[x]
                return (low if y < 0 else high).at[:, pl.ds(first, count)]
            first, count = slices_x[x]
            return own.at[:, pl.ds(first, count)]

        def target(k):
            x, y, z = AROUND[k]
            if z != 0:
                return get("zr").at[flat_zr.index((x, y, z))]
            if y != 0:
                return get("yr").at[flat_yr.index((x, y)), :, pl.ds(0, pairs_x[x][1])]
            return get("xr").at[0 if x > 0 else 1, :, pl.ds(0, slices_x[x][1])]

        return copies(AROUND, source, target, get("ss"), get("rs"))

    def assemble(arrays, key):
        get = lambda name: getattr(s, f"{key}_{name}")
        own, xr, yr, zr, ext = get("own"), get("xr"), get("yr"), get("zr"), get("ext")
        first8 = (lane8 & 15) < 8
        side_high, side_low = (lane16 >= 64) & (lane16 < 72), lane16 >= 120

        def zed(a, x, y):
            above = zr[flat_zr.index((x, y, -1)), a]
            below = zr[flat_zr.index((x, y, 1)), a]
            return jnp.where(first8, above, below)

        for a in range(arrays):
            combs = {}
            for x in (1, -1, 0):
                outer = jnp.where(upper_half, zed(a, x, -1), zed(a, x, 1))
                combs[x] = jnp.concatenate([zed(a, x, 0), outer], axis=0)
            for k in range(17):
                x = k - 4
                if x < 0:
                    d, layer, place = 1, x + 4, x + 8
                elif x < 8:
                    d, layer, place = 0, x, x
                else:
                    d, layer, place = -1, x - 8, x - 8
                inner = own[a, layer] if d == 0 else xr[0 if d > 0 else 1, a, layer]
                above = yr[flat_yr.index((d, -1)), a, layer // 2]
                below = yr[flat_yr.index((d, 1)), a, layer // 2]
                if layer % 2 == 0:
                    below = turn(below, 4, 0)
                else:
                    above = turn(above, 4, 0)
                outer = jnp.where(upper_half, above, below)
                whole = jnp.concatenate([inner, outer], axis=0)
                comb = combs[d]
                whole = jnp.where(side_high, turn(comb, 64 - 16 * place), whole)
                whole = jnp.where(side_low, turn(comb, 112 - 16 * place), whole)
                ext[a, pl.ds(16 * k, 16)] = whole

    def ext1(k):
        return pl.ds(16 * k, 16)

    def pad1(k):
        return pl.ds(16 * k + 16, 16)

    def coefficients1():
        keep_y = jnp.where(row16 == 0, low_y, 1.0)
        keep_z = jnp.where(lane16 == 0, low_z, 1.0)
        last_z = jnp.where(lane16 == 63, top_z, 1.0)
        for k in range(16):
            own = ext1(k)
            a_xl, a_yl, a_zl = s.hf_ext[0, own], s.hf_ext[1, own], s.hf_ext[2, own]
            a_xu = s.hf_ext[0, ext1(k + 1)]
            if k == 11:
                a_xu = a_xu * top_x
            a_yu = s.hf_ext[3, own]
            a_zu = turn(a_zl, -1) * last_z
            total = (a_xl + a_yl + a_zl) + (a_xu + a_yu + a_zu)
            scale = RELAX / total
            s.kw1[own] = scale * 4.0
            if 1 <= k <= 14:
                s.d151[own] = (1.5 * 0.25) * total
                s.cxl1[own] = scale * a_xl * (low_x if k == 4 else 1.0)
                s.cxu1[own] = scale * a_xu
                s.cyl1[own] = scale * a_yl * keep_y
                s.cyu1[own] = scale * a_yu
                s.czl1[own] = scale * a_zl * keep_z
                s.czu1[own] = scale * a_zu

    def stencil1(first, last, ref, emit):
        for k in range(first, last + 1):
            own = ext1(k)
            v = ref[pad1(k)]
            t_x = s.cxl1[own] * ref[pad1(k - 1)] + s.cxu1[own] * ref[pad1(k + 1)]
            t_y = s.cyl1[own] * turn(v, 1, 0) + s.cyu1[own] * turn(v, -1, 0)
            t_z = s.czl1[own] * turn(v, 1) + s.czu1[own] * turn(v, -1)
            emit(k, v, s.g1[own] + (t_x + t_y + t_z))

    def smooth1(first, last, source, target):
        def emit(k, v, total):
            target[pad1(k)] = v * THIRD + total

        stencil1(first, last, source, emit)

    even8 = (2 * lane8) & 127
    half16 = lane16 >> 1

    def pair_z(value):
        return value + turn(value, -1)

    def stage_z(arrays, snd):
        group = lane16 >> 4
        packed = jnp.zeros((16, 128), F32)
        for a in range(arrays):
            whole = s.t16[a]
            for p in range(2):
                moved = take(whole, 4 * (lane16 & 15) + 2 * p)
                packed = jnp.where(group == ((gz + 2 * a + p) & 7), moved, packed)
        snd[...] = packed

    def merge_z(arrays, snd, rcv, target):
        group = lane16 >> 4
        parts = [(0, snd[...])] + [(RING_Z[k][2], rcv[k]) for k in range(7)]
        for q in range(2 * arrays):
            merged = jnp.zeros((16, 128), F32)
            for distance, part in parts:
                merged = jnp.where(group == ((gz - distance + q) & 7), part, merged)
            target[q] = turn(merged, -16 * q)

    for load in loads[:3]:
        load.wait()
    for i in range(8):
        own = pl.ds(8 * i, 8)
        here = lambda ref, shift: ref[pl.ds(32 * i + shift, 8, stride=2)]
        s.fx1[own] = take(pair_z(here(s.fx, 0) + here(s.fx, 1)), even8) * 0.25
        s.fy1[own] = take(pair_z(here(s.fy, 0) + here(s.fy, 16)), even8) * 0.25
        total = (here(s.fz, 0) + here(s.fz, 1)) + (here(s.fz, 16) + here(s.fz, 17))
        s.fz1[own] = take(total, even8) * 0.25
    for i in range(4):
        own = pl.ds(4 * i, 4)
        here = lambda ref, shift: ref[pl.ds(16 * i + shift, 4, stride=2)]
        s.t16[0, own] = here(s.fx1, 0) + here(s.fx1, 1)
        s.t16[1, own] = here(s.fy1, 0) + here(s.fy1, 8)
        total = (here(s.fz1, 0) + here(s.fz1, 1)) + (here(s.fz1, 8) + here(s.fz1, 9))
        s.t16[2, own] = total * 0.25
    s.t16[0] = pair_z(s.t16[0]) * 0.25
    s.t16[1] = pair_z(s.t16[1]) * 0.25
    stage_z(3, s.zf_snd)
    for ref in (s.va1, s.vb1):
        for k in (-1, 17):
            ref[pad1(k)] = jnp.zeros((16, 128), F32)
    for p in range(2):
        for x in (0, 1, 18, 19):
            for ref in (s.va2, s.vb2):
                ref[p, x] = jnp.zeros((16, 128), F32)
        for x in range(16):
            s.f2[p, x + 2] = jnp.zeros((16, 128), F32)
    for ref in (s.va3, s.vb3):
        for k in range(2):
            ref[pl.ds(8 * k, 8)] = jnp.zeros((8, 128), F32)
            ref[pl.ds(144 + 8 * k, 8)] = jnp.zeros((8, 128), F32)
    s.p2[...] = jnp.zeros_like(s.p2)
    s.a1_snd[...] = s.fy1[pl.ds(0, 8, stride=8)]

    pl.semaphore_wait(barrier, len(friends))
    round_a0 = send_upper(s.fx, s.fy, s.fz, "a0")
    round_a1 = copies([DOWN[1]], lambda k: s.a1_snd, lambda k: s.a1_rcv, s.a1_ss, s.a1_rs)
    round_zf = copies(
        RING_Z, lambda k: s.zf_snd, lambda k: s.zf_rcv.at[k], s.zf_ss, s.zf_rs
    )
    loads[3].wait()
    finish(round_a0)
    coefficients(0, s.fx, s.fy, s.fz, "a0")
    for i in range(16):
        own = B0.own(i)
        start = s.kw0[own] * s.rhs[own]
        s.g0[own] = start
        s.va0[B0.at(i)] = start
    round_b = send_faces(B0, s.va0, "b")
    finish(round_a1)
    for i in range(8):
        s.lyp1[pl.ds(16 * i, 8)] = s.fy1[pl.ds(8 * i, 8)]
    s.lyp1[pl.ds(8, 8, stride=16)] = s.a1_rcv[...] * top_y
    for i in range(8):
        own = pl.ds(8 * i, 8)
        s.hf_own[0, i] = s.fx1[own]
        s.hf_own[1, i] = s.fy1[own]
        s.hf_own[2, i] = s.fz1[own]
        s.hf_own[3, i] = s.lyp1[pl.ds(16 * i + 1, 8)]
    finish(round_b)
    fill(B0, s.va0, s.b_rcv)
    smooth(0, s.va0, s.vb0, s.b_rcv[4], s.b_rcv[5])
    round_c = send_faces(B0, s.vb0, "c")
    round_hf = send_around(4, "hf")
    finish(round_zf)
    merge_z(3, s.zf_snd, s.zf_rcv, s.xf_snd)
    round_xf = copies(
        LINE, lambda k: s.xf_snd, lambda k: s.xf_rcv.at[k], s.xf_ss, s.xf_rs
    )
    finish(round_c)
    fill(B0, s.vb0, s.c_rcv)
    residual(0, s.vb0, s.c_rcv[4], s.c_rcv[5])

    for i in range(8):
        here = lambda shift: s.r0[pl.ds(32 * i + shift, 8, stride=2)]
        total = (here(0) + here(1)) + (here(16) + here(17))
        s.hr_own[0, i] = take(pair_z(total), even8) * 0.125
    round_hr = send_around(1, "hr")
    finish(round_hf)
    assemble(4, "hf")
    coefficients1()


    def block2(p, x):
        return (p, x + 2)

    def spread(arrays, offsets, snd, rcv, targets):
        parts = [((0, 0, 0), lambda q: snd.at[q])]
        for k, offset in enumerate(offsets):
            parts.append((offset, lambda q, k=k: rcv.at[k, q]))
        for offset, part in parts:
            first = 4 * ((gx - offset[0]) & 3)
            place = pl.ds(4 * (1 - offset[1]), 4)
            for a in range(arrays):
                for p in range(2):
                    for x in range(4):
                        piece = part(2 * a + p)[pl.ds(4 * x, 4)]
                        targets[a][p, x + 2 + first, place] = piece

    def send_sides(refs, key):
        snd, rcv = getattr(s, key + "_snd"), getattr(s, key + "_rcv")
        for a, ref in enumerate(refs):
            for p in range(2):
                for i in range(8):
                    even = ref[p, 2 * i + 2, pl.ds(0, 8)]
                    odd = ref[p, 2 * i + 3, pl.ds(0, 8)]
                    snd[a, p, i] = jnp.where(upper_half, turn(even, 4, 0), odd)
        return copies(
            SIDES,
            lambda k: snd,
            lambda k: rcv.at[k],
            getattr(s, key + "_ss"),
            getattr(s, key + "_rs"),
        )

    def take_sides(refs, key, rest):
        rcv = getattr(s, key + "_rcv")
        for a, ref in enumerate(refs):
            for p in range(2):
                for x in range(16):
                    below, above = rcv[0, a, p, x // 2], rcv[1, a, p, x // 2]
                    if x % 2 == 1:
                        below, above = turn(below, 4, 0), turn(above, 4, 0)
                    own = ref[p, x + 2, pl.ds(0, 8)]
                    ref[p, x + 2, pl.ds(0, 8)] = jnp.where(upper_half, below, own)
                    ref[p, x + 2, pl.ds(8, 8)] = jnp.where(upper_half, above, rest)

    faces2 = (s.lx2, s.ly2, s.lz2)
    finish(round_xf)
    spread(3, LINE, s.xf_snd, s.xf_rcv, faces2)
    round_nf = send_sides(faces2, "nf")
    global_y = row16 + 4 * gy - 4
    not_low, not_top = global_y != 0, global_y != 4 * GY - 1

    finish(round_hr)
    assemble(1, "hr")
    for k in range(16):
        start = s.kw1[ext1(k)] * s.hr_ext[0, ext1(k)]
        s.g1[ext1(k)] = start
        s.va1[pad1(k)] = start
    smooth1(1, 14, s.va1, s.vb1)

    def emit_r1(k, v, total):
        r = s.d151[ext1(k)] * (total - RELAX * v)
        s.r1[pl.ds(8 * (k - 4), 8)] = r[0:8]

    stencil1(4, 11, s.vb1, emit_r1)
    for i in range(4):
        here = lambda shift: s.r1[pl.ds(16 * i + shift, 4, stride=2)]
        s.t16[0, pl.ds(4 * i, 4)] = (here(0) + here(1)) + (here(8) + here(9))
    s.t16[0] = pair_z(s.t16[0]) * 0.125
    stage_z(1, s.zr_snd)
    round_zr = copies(
        RING_Z, lambda k: s.zr_snd, lambda k: s.zr_rcv.at[k], s.zr_ss, s.zr_rs
    )

    finish(round_nf)
    take_sides(faces2, "nf", 1.0)

    for a, ref in enumerate((s.lx2, s.ly2, s.lz2)):
        for i in range(8):
            total = ref[block2(0, 2 * i)]
            if a != 2:
                total = total + ref[block2(1, 2 * i)]
            if a != 0:
                total = total + ref[block2(0, 2 * i + 1)]
            if a == 1:
                total = total + ref[block2(1, 2 * i + 1)]
            s.s2[pl.ds(16 * i, 16)] = total
        for j in range(2):
            total = s.s2[pl.ds(4 + 2 * j, 8, stride=16)]
            if a != 1:
                total = total + s.s2[pl.ds(5 + 2 * j, 8, stride=16)]
            s.face3[a, pl.ds(pl.multiple_of(16 * gy + 8 * j, 8), 8)] = total * 0.25
    mine = pl.ds(pl.multiple_of(16 * gy, 16), 16)
    round_yf = copies(
        RING_Y,
        lambda k: s.face3.at[:, mine],
        lambda k: s.face3.at[:, mine],
        s.yf_ss,
        s.yf_rs,
    )

    for p in range(2):
        for x in range(16):
            j = block2(p, x)
            a_xl, a_yl, a_zl = s.lx2[j], s.ly2[j], s.lz2[j]
            a_xu = s.lx2[block2(p, x + 1)] if x < 15 else jnp.zeros((16, 128), F32)
            a_yu = jnp.where(not_top, turn(a_yl, -1, 0), 0.0)
            if p == 0:
                a_zu = s.lz2[block2(1, x)]
            else:
                a_zu = jnp.where(lane16 == 127, 0.0, turn(s.lz2[block2(0, x)], -1))
            total = (a_xl + a_yl + a_zl) + (a_xu + a_yu + a_zu)
            scale = RELAX / total
            s.d152[j] = (1.5 * 0.0625) * total
            s.kw2[j] = scale * 16.0
            s.cxl2[j] = scale * a_xl if x > 0 else jnp.zeros((16, 128), F32)
            s.cxu2[j] = scale * a_xu
            s.cyl2[j] = jnp.where(not_low, scale * a_yl, 0.0)
            s.cyu2[j] = scale * a_yu
            s.czl2[j] = scale * a_zl if p == 1 else jnp.where(lane16 == 0, 0.0, scale * a_zl)
            s.czu2[j] = scale * a_zu

    def stencil2(ref, emit):
        for p in range(2):
            for x in range(16):
                j, other = block2(p, x), block2(1 - p, x)
                v, w = ref[j], ref[other]
                t_x = s.cxl2[j] * ref[block2(p, x - 1)] + s.cxu2[j] * ref[block2(p, x + 1)]
                t_y = s.cyl2[j] * turn(v, 1, 0) + s.cyu2[j] * turn(v, -1, 0)
                down, up = (turn(w, 1), w) if p == 0 else (w, turn(w, -1))
                t_z = s.czl2[j] * down + s.czu2[j] * up
                emit(j, v, s.g2[j] + (t_x + t_y + t_z))

    def smooth2(source, target):
        def emit(j, v, total):
            target[j] = v * THIRD + total

        stencil2(source, emit)

    finish(round_zr)
    merge_z(1, s.zr_snd, s.zr_rcv, s.xr_snd)
    round_xr = copies(
        PLANE, lambda k: s.xr_snd, lambda k: s.xr_rcv.at[k], s.xr_ss, s.xr_rs
    )

    finish(round_yf)
    zero8 = jnp.zeros((8, 128), F32)
    for y in range(16):
        own = pl.ds(8 * y, 8)
        a_xl, a_yl, a_zl = s.face3[0, own], s.face3[1, own], s.face3[2, own]
        a_xu = jnp.where(row8 == 7, 0.0, turn(a_xl, -1, 0))
        a_yu = s.face3[1, pl.ds(8 * y + 8, 8)] if y < 15 else zero8
        a_zu = jnp.where(lane8 == 127, 0.0, turn(a_zl, -1))
        total = (a_xl + a_yl + a_zl) + (a_xu + a_yu + a_zu)
        scale = RELAX / total
        s.d153[own] = (1.5 * 0.25**3) * total
        s.kw3[own] = scale * 64.0
        s.cxl3[own] = jnp.where(row8 == 0, 0.0, scale * a_xl)
        s.cxu3[own] = scale * a_xu
        s.cyl3[own] = scale * a_yl if y > 0 else zero8
        s.cyu3[own] = scale * a_yu
        s.czl3[own] = jnp.where(lane8 == 0, 0.0, scale * a_zl)
        s.czu3[own] = scale * a_zu

    lane32, row32 = lanes(32), sublanes(32)

    def both(value, lane, step):
        return value + jnp.where(
            (lane & step) == 0, turn(value, -step), turn(value, step)
        )

    def lower_of(value, lane, step):
        return jnp.where((lane & step) == 0, value, turn(value, step))

    for a in range(3):
        for y in range(8):
            here = lambda shift: s.face3[a, pl.ds(16 * y + shift, 4, stride=2)]
            if a == 0:
                total = here(0) + here(8)
            elif a == 1:
                total = here(0) + here(1)
            else:
                total = (here(0) + here(1)) + (here(8) + here(9))
            s.t4[pl.ds(4 * y, 4)] = total
        total = s.t4[...]
        total = both(total, lane32, 1) if a < 2 else lower_of(total, lane32, 1)
        s.fc4[a] = total * 0.25
    a_xl, a_yl, a_zl = s.fc4[0], s.fc4[1], s.fc4[2]
    a_xu = jnp.where((row32 & 3) == 3, 0.0, turn(a_xl, -1, 0))
    a_yu = jnp.where(row32 >= 28, 0.0, turn(a_yl, -4, 0))
    a_zu = jnp.where(lane32 >= 126, 0.0, turn(a_zl, -2))
    total = (a_xl + a_yl + a_zl) + (a_xu + a_yu + a_zu)
    scale = RELAX / total
    s.d154[...] = (1.5 * 0.25**4) * total
    s.kw4[...] = scale * 256.0
    s.cxl4[...] = jnp.where((row32 & 3) == 0, 0.0, scale * a_xl)
    s.cxu4[...] = scale * a_xu
    s.cyl4[...] = jnp.where(row32 < 4, 0.0, scale * a_yl)
    s.cyu4[...] = scale * a_yu
    s.czl4[...] = jnp.where(lane32 < 2, 0.0, scale * a_zl)
    s.czu4[...] = scale * a_zu

    faces5 = []
    for a in range(3):
        for x in range(2):
            here = lambda shift: s.fc4[a, pl.ds(2 * x + shift, 4, stride=8)]
            if a == 0:
                total = here(0) + here(4)
            elif a == 1:
                total = here(0) + here(1)
            else:
                total = (here(0) + here(1)) + (here(4) + here(5))
            s.t5[pl.ds(4 * x, 4)] = total
        total = s.t5[...]
        total = both(total, lane8, 2) if a < 2 else lower_of(total, lane8, 2)
        faces5.append(total * 0.25)
    a_xl, a_yl, a_zl = faces5
    a_xu = jnp.where(row8 >= 4, 0.0, turn(a_xl, 4, 0))
    a_yu = jnp.where((row8 & 3) == 3, 0.0, turn(a_yl, -1, 0))
    a_zu = jnp.where(lane8 >= 124, 0.0, turn(a_zl, -4))
    total = (a_xl + a_yl + a_zl) + (a_xu + a_yu + a_zu)
    scale = RELAX / total
    s.kw5[...] = scale * 1024.0
    s.cx5[...] = jnp.where(row8 >= 4, scale * a_xl, scale * a_xu)
    s.cyl5[...] = jnp.where((row8 & 3) == 0, 0.0, scale * a_yl)
    s.cyu5[...] = scale * a_yu
    s.czl5[...] = jnp.where(lane8 < 4, 0.0, scale * a_zl)
    s.czu5[...] = scale * a_zu

    finish(round_xr)
    spread(1, PLANE, s.xr_snd, s.xr_rcv, (s.f2,))
    for p in range(2):
        for x in range(16):
            j = block2(p, x)
            start = s.kw2[j] * s.f2[j]
            s.g2[j] = start
            s.va2[j] = start
    smooth2(s.va2, s.vb2)

    def emit_r2(j, v, total):
        s.f2[j] = s.d152[j] * (total - RELAX * v)

    stencil2(s.vb2, emit_r2)
    for i in range(8):
        total = (s.f2[block2(0, 2 * i)] + s.f2[block2(1, 2 * i)]) + (
            s.f2[block2(0, 2 * i + 1)] + s.f2[block2(1, 2 * i + 1)]
        )
        s.s2[pl.ds(16 * i, 16)] = total
    for j in range(2):
        total = s.s2[pl.ds(4 + 2 * j, 8, stride=16)] + s.s2[pl.ds(5 + 2 * j, 8, stride=16)]
        s.f3[pl.ds(pl.multiple_of(16 * gy + 8 * j, 8), 8)] = total * 0.125
    round_yr = copies(
        RING_Y, lambda k: s.f3.at[mine], lambda k: s.f3.at[mine], s.yr_ss, s.yr_rs
    )
    round_nv = send_sides((s.vb2,), "nv")
    finish(round_yr)

    def at3(y):
        return pl.ds(16 + 8 * y, 8)

    def stencil3(ref, emit):
        for y in range(16):
            own = pl.ds(8 * y, 8)
            v = ref[at3(y)]
            t_x = s.cxl3[own] * turn(v, 1, 0) + s.cxu3[own] * turn(v, -1, 0)
            t_y = s.cyl3[own] * ref[at3(y - 1)] + s.cyu3[own] * ref[at3(y + 1)]
            t_z = s.czl3[own] * turn(v, 1) + s.czu3[own] * turn(v, -1)
            emit(y, v, s.g3[own] + (t_x + t_y + t_z))

    def smooth3(source, target):
        def emit(y, v, total):
            target[at3(y)] = v * THIRD + total

        stencil3(source, emit)

    for y in range(16):
        own = pl.ds(8 * y, 8)
        start = s.kw3[own] * s.f3[own]
        s.g3[own] = start
        s.va3[at3(y)] = start
    smooth3(s.va3, s.vb3)

    def emit_r3(y, v, total):
        own = pl.ds(8 * y, 8)
        s.r3[own] = s.d153[own] * (total - RELAX * v)

    stencil3(s.vb3, emit_r3)
    for y in range(8):
        here = lambda shift: s.r3[pl.ds(16 * y + shift, 4, stride=2)]
        s.t4[pl.ds(4 * y, 4)] = (here(0) + here(1)) + (here(8) + here(9))
    f4 = both(s.t4[...], lane32, 1) * 0.125

    def total4(v):
        t_x = s.cxl4[...] * turn(v, 1, 0) + s.cxu4[...] * turn(v, -1, 0)
        t_y = s.cyl4[...] * turn(v, 4, 0) + s.cyu4[...] * turn(v, -4, 0)
        t_z = s.czl4[...] * turn(v, 2) + s.czu4[...] * turn(v, -2)
        return g4 + (t_x + t_y + t_z)

    g4 = s.kw4[...] * f4
    v4 = g4
    v4 = v4 * THIRD + total4(v4)
    s.r4[...] = s.d154[...] * (total4(v4) - RELAX * v4)
    for x in range(2):
        here = lambda shift: s.r4[pl.ds(2 * x + shift, 4, stride=8)]
        s.t5[pl.ds(4 * x, 4)] = (here(0) + here(1)) + (here(4) + here(5))
    g5 = s.kw5[...] * (both(s.t5[...], lane8, 2) * 0.125)
    cx5, cyl5, cyu5, czl5, czu5 = s.cx5[...], s.cyl5[...], s.cyu5[...], s.czl5[...], s.czu5[...]

    def sweep5(index, v):
        t_y = cyl5 * turn(v, 1, 0) + cyu5 * turn(v, -1, 0)
        t_z = czl5 * turn(v, 4) + czu5 * turn(v, -4)
        return (v * THIRD + g5) + (cx5 * turn(v, 4, 0) + (t_y + t_z))

    s.e5[...] = lax.fori_loop(0, COARSE_SWEEPS - 1, sweep5, g5)
    for x in range(2):
        piece = s.e5[pl.ds(4 * x, 4)]
        for shift in (0, 1, 4, 5):
            s.p4[pl.ds(2 * x + shift, 4, stride=8)] = piece
    v4 = v4 + s.p4[...]
    v4 = v4 * THIRD + total4(v4)
    v4 = v4 * THIRD + total4(v4)
    s.r4[...] = v4
    for x in range(4):
        piece = s.r4[pl.ds(x, 8, stride=4)]
        for shift in (0, 1, 8, 9):
            s.p3[pl.ds(2 * x + shift, 8, stride=16)] = piece
    for y in range(16):
        s.vb3[at3(y)] = s.vb3[at3(y)] + s.p3[pl.ds(8 * y, 8)]
    smooth3(s.vb3, s.va3)
    smooth3(s.va3, s.vb3)

    finish(round_nv)
    take_sides((s.vb2,), "nv", 0.0)
    for k in range(6):
        piece = s.vb3[pl.ds(pl.multiple_of(16 * gy + 8 * k, 8), 8)]
        for x in range(2):
            for y in range(2):
                s.p2[pl.ds(16 * x + 2 * k + y, 8, stride=32)] = piece
    for x in range(16):
        more = s.p2[pl.ds(16 * x, 16)]
        for p in range(2):
            s.vb2[block2(p, x)] = s.vb2[block2(p, x)] + more
    smooth2(s.vb2, s.va2)
    smooth2(s.va2, s.vb2)

    signed = jnp.where(lane16 < 96, lane16, lane16 - 128)
    index = (16 * gz + (signed >> 2)) & 127
    odd = ((signed >> 1) & 1) == 1
    for k in range(8):
        x = 4 * gx + k
        piece = jnp.where(odd, take(s.vb2[1, x], index), take(s.vb2[0, x], index))
        rows = jnp.where(row16 < 6, turn(piece, -4, 0), turn(piece, 4, 0))[0:8]
        for y in range(2):
            s.q1[pl.ds(16 * k + y, 8, stride=2)] = rows
        more = s.q1[pl.ds(16 * k, 16)]
        for i in (2 * k, 2 * k + 1):
            if 1 <= i <= 14:
                s.vb1[pad1(i)] = s.vb1[pad1(i)] + more
    smooth1(2, 13, s.vb1, s.va1)
    smooth1(3, 12, s.va1, s.vb1)
    s.h1[0] = s.vb1[pl.ds(16 * 4, 8)]
    s.h1[1] = s.vb1[pl.ds(16 * 13, 8)]
    s.h1[2] = s.vb1[pl.ds(16 * 5 + 15, 8, stride=16)]
    s.h1[3] = s.vb1[pl.ds(16 * 5 + 8, 8, stride=16)]
    inner = lambda i: s.vb1[pl.ds(16 * (i + 5), 8)]
    s.h1[4] = pack(inner, 8, 8, 127)
    s.h1[5] = pack(inner, 8, 8, 64)

    def widen(value, ref, start):
        ref[pl.ds(start, 8, stride=2)] = value
        ref[pl.ds(start + 1, 8, stride=2)] = value
        return take(ref[pl.ds(start, 16)], half16)

    for i in range(8):
        more = widen(inner(i), s.w0, 16 * i)
        for x in (2 * i, 2 * i + 1):
            s.vb0[B0.at(x)] = s.vb0[B0.at(x)] + more
    for k in range(6):
        s.c_rcv[k] = s.c_rcv[k] + widen(s.h1[k], s.w0, 128 + 16 * k)
    fill(B0, s.vb0, s.c_rcv)
    smooth(0, s.vb0, s.va0, s.c_rcv[4], s.c_rcv[5])
    round_h = send_faces(B0, s.va0, "h")
    finish(round_h)
    fill(B0, s.va0, s.h_rcv)

    def emit_out(i, v, total):
        out[B0.own(i)] = v * THIRD + total

    stencil(0, s.va0, s.h_rcv[4], s.h_rcv[5], emit_out)


def shards(rhs, face_x, face_y, face_z):
    flat = [a.reshape(256, 128) for a in (rhs, face_x, face_y, face_z)]
    whole = pl.pallas_call(
        cycle,
        out_shape=jax.ShapeDtypeStruct((256, 128), F32),
        in_specs=[pl.BlockSpec(memory_space=pltpu.HBM)] * 4,
        out_specs=pl.BlockSpec(memory_space=pltpu.VMEM),
        scratch_shapes=list(SCRATCH.values()),
        compiler_params=pltpu.CompilerParams(
            collective_id=0, has_side_effects=True, vmem_limit_bytes=48 * 1024 * 1024
        ),
        name="vcycle",
    )(*flat)
    return whole.reshape(16, 16, 128)


def solution(mesh):
    placed = P("gx", "gy", "gz")
    return jax.shard_map(
        shards, mesh=mesh, in_specs=(placed,) * 4, out_specs=placed, check_vma=False
    )
```

```python
import jax
import jax.numpy as jnp
from jax import lax
from jax.experimental import pallas as pl
from jax.experimental.pallas import tpu as pltpu
from jax.sharding import PartitionSpec as P

RELAX = 2.0 / 3.0
THIRD = 1.0 / 3.0
COARSE_SWEEPS = 24
GX, GY, GZ = 4, 8, 8
F32 = jnp.float32
MESH = pl.DeviceIdType.MESH

FACES = [(1, 0, 0), (-1, 0, 0), (0, 1, 0), (0, -1, 0), (0, 0, 1), (0, 0, -1)]
DOWN = [(-1, 0, 0), (0, -1, 0), (0, 0, -1)]
RING_Z = [(0, 0, k) for k in (4, 3, 5, 2, 6, 1, 7)]
RING_Y = [(0, k, 0) for k in (4, 3, 5, 2, 6, 1, 7)]
AROUND = [
    (x, y, z) for x in (1, -1, 0) for y in (1, -1, 0) for z in (1, -1, 0) if (x, y, z) != (0, 0, 0)
]
AROUND.sort(key=lambda d: -(abs(d[0]) + abs(d[1]) + abs(d[2])))
LINE = [(2, 0, 0), (1, 0, 0), (3, 0, 0)]
SIDES = [(0, 1, 0), (0, -1, 0)]
PLANE = [(2, 1, 0), (2, -1, 0), (1, 1, 0), (1, -1, 0), (3, 1, 0), (3, -1, 0)]
PLANE += [(2, 0, 0), (0, 1, 0), (0, -1, 0), (1, 0, 0), (3, 0, 0)]


def lanes(rows):
    return lax.broadcasted_iota(jnp.int32, (rows, 128), 1)


def sublanes(rows):
    return lax.broadcasted_iota(jnp.int32, (rows, 128), 0)


def turn(value, steps, axis=1):
    steps %= value.shape[axis]
    return value if steps == 0 else pltpu.roll(value, steps, axis)


def take(value, index):
    return jnp.take_along_axis(value, index, axis=1, mode="promise_in_bounds")


class Block:
    def __init__(self, size_x, size_y, size_z, weight):
        self.X, self.Y, self.Z, self.weight = size_x, size_y, size_z, weight
        self.pitch = size_y + 8
        self.rows = size_x * size_y
        self.padded = 8 + (size_x + 2) * self.pitch

    def base(self, i):
        return 8 + (i + 1) * self.pitch

    def own(self, i):
        return pl.ds(i * self.Y, self.Y)

    def at(self, i, shift=0):
        return pl.ds(self.base(i) + shift, self.Y)

    def row_of_each(self, y):
        return pl.ds(self.base(0) + y, self.X, stride=self.pitch)


B0 = Block(16, 16, 128, 1.0)

SCRATCH = {}


def vmem(name, *shape):
    SCRATCH[name] = pltpu.VMEM(shape, F32)


def dma(name, *shape):
    SCRATCH[name] = pltpu.SemaphoreType.DMA(shape)


for key in ("rhs", "fx", "fy", "fz"):
    vmem(key, 256, 128)
dma("in_sem", 5)
for key in ("cxl0", "cxu0", "cyl0", "cyu0", "czl0", "czu0", "g0", "d150", "kw0", "r0", "w0"):
    vmem(key, 256, 128)
vmem("va0", B0.padded, 128)
vmem("vb0", B0.padded, 128)
vmem("lyp0", B0.X * B0.pitch, 128)
for key in ("fx1", "fy1", "fz1", "r1"):
    vmem(key, 64, 128)
for key in ("cxl1", "cxu1", "cyl1", "cyu1", "czl1", "czu1", "g1", "d151", "kw1"):
    vmem(key, 17 * 16, 128)
for key in ("va1", "vb1"):
    vmem(key, 19 * 16, 128)
vmem("ext1", 4, 17 * 16, 128)
vmem("hw_own", 5, 8, 8, 128)
vmem("hw_low", 5, 4, 8, 128)
vmem("hw_high", 5, 4, 8, 128)
vmem("hw_zed", 2, 8, 128)
vmem("hw_xr", 2, 5, 3, 8, 128)
vmem("hw_yr", 6, 5, 4, 8, 128)
vmem("hw_zr", 18, 8, 128)
dma("hw_ss", 26)
dma("hw_rs", 26)
vmem("q1", 8 * 16, 128)
vmem("h1", 6, 8, 128)
for key, rows, count in (("a0", 16, 3), ("b", 16, 6), ("c", 16, 6), ("h", 16, 6), ("a1", 8, 3), ("d", 8, 6), ("e", 8, 6)):
    vmem(f"{key}_snd", count, rows, 128)
    vmem(f"{key}_rcv", count, rows, 128)
    dma(f"{key}_ss", count)
    dma(f"{key}_rs", count)
vmem("t16", 3, 16, 128)
for key, arrays in (("zf", 3), ("zr", 1)):
    vmem(f"{key}_snd", 16, 128)
    vmem(f"{key}_rcv", 7, 16, 128)
    dma(f"{key}_ss", 7)
    dma(f"{key}_rs", 7)
for key, arrays in (("xf", 3), ("xr", 1)):
    vmem(f"{key}_snd", arrays * 2, 16, 128)
    vmem(f"{key}_rcv", 11, arrays * 2, 16, 128)
    dma(f"{key}_ss", 11)
    dma(f"{key}_rs", 11)
for key in ("f2", "lx2", "ly2", "lz2", "va2", "vb2"):
    vmem(key, 2, 20, 16, 128)
for key in ("cxl2", "cxu2", "cyl2", "cyu2", "czl2", "czu2", "g2", "d152", "kw2"):
    vmem(key, 2, 20, 16, 128)
for key, arrays in (("nf", 3), ("nv", 1)):
    vmem(f"{key}_snd", arrays, 2, 8, 8, 128)
    vmem(f"{key}_rcv", 2, arrays, 2, 8, 8, 128)
    dma(f"{key}_ss", 2)
    dma(f"{key}_rs", 2)
vmem("s2", 128, 128)
vmem("p2", 256, 128)
vmem("face3", 3, 128, 128)
vmem("f3", 128, 128)
for key in ("yf", "yr"):
    dma(f"{key}_ss", 7)
    dma(f"{key}_rs", 7)
for key in ("cxl3", "cxu3", "cyl3", "cyu3", "czl3", "czu3", "g3", "d153", "kw3", "r3", "p3"):
    vmem(key, 128, 128)
vmem("va3", 160, 128)
vmem("vb3", 160, 128)
for key in ("t4", "cxl4", "cxu4", "cyl4", "cyu4", "czl4", "czu4", "d154", "kw4", "r4", "p4"):
    vmem(key, 32, 128)
vmem("fc4", 3, 32, 128)
for key in ("t5", "cx5", "cyl5", "cyu5", "czl5", "czu5", "kw5", "e5"):
    vmem(key, 8, 128)


class Space:
    pass


def cycle(rhs_in, fx_in, fy_in, fz_in, out, *scratch):
    s = Space()
    for name, ref in zip(SCRATCH, scratch):
        setattr(s, name, ref)
    gx, gy, gz = lax.axis_index("gx"), lax.axis_index("gy"), lax.axis_index("gz")

    def peer(offset):
        return (
            (gx + offset[0]) & (GX - 1),
            (gy + offset[1]) & (GY - 1),
            (gz + offset[2]) & (GZ - 1),
        )

    loads = [
        pltpu.make_async_copy(source, target, s.in_sem.at[k])
        for k, (source, target) in enumerate(
            ((fx_in, s.fx), (fy_in, s.fy), (fz_in, s.fz), (rhs_in, s.rhs))
        )
    ]
    for load in loads:
        load.start()

    barrier = pltpu.get_barrier_semaphore()
    for offset in FACES:
        pl.semaphore_signal(barrier, inc=1, device_id=peer(offset), device_id_type=MESH)

    def copies(offsets, sources, targets, ss, rs):
        made = [
            pltpu.make_async_remote_copy(
                src_ref=sources(k),
                dst_ref=targets(k),
                send_sem=ss.at[k],
                recv_sem=rs.at[k],
                device_id=peer(offset),
                device_id_type=MESH,
            )
            for k, offset in enumerate(offsets)
        ]
        for one in made:
            one.start()
        return made

    def finish(made):
        for one in made:
            one.wait_recv()
        for one in made:
            one.wait_send()

    def flag(condition):
        return jnp.where(condition, 1.0, 0.0).astype(F32)

    low_x, low_y, low_z = flag(gx > 0), flag(gy > 0), flag(gz > 0)
    top_x, top_y, top_z = flag(gx < GX - 1), flag(gy < GY - 1), flag(gz < GZ - 1)


    def pack(read, rows, count, column):
        packed = jnp.zeros((rows, 128), F32)
        lane = lanes(rows)
        for i in range(count):
            packed = jnp.where(lane == i, turn(read(i), i - column), packed)
        return packed

    def send_faces(block, ref, key):
        snd = getattr(s, key + "_snd")
        snd[0] = ref[block.at(block.X - 1)]
        snd[1] = ref[block.at(0)]
        snd[2] = ref[block.row_of_each(block.Y - 1)]
        snd[3] = ref[block.row_of_each(0)]
        snd[4] = pack(lambda i: ref[block.at(i)], 16, 16, 127)
        snd[5] = pack(lambda i: ref[block.at(i)], 16, 16, 0)
        rcv = getattr(s, key + "_rcv")
        return copies(
            FACES,
            lambda k: snd.at[k],
            lambda k: rcv.at[k],
            getattr(s, key + "_ss"),
            getattr(s, key + "_rs"),
        )

    def fill(block, ref, halo):
        ref[block.at(-1)] = halo[0]
        ref[block.at(block.X)] = halo[1]
        ref[block.row_of_each(-1)] = halo[2]
        ref[block.row_of_each(block.Y)] = halo[3]

    def send_upper(lx, ly, lz, key):
        block = B0
        snd = getattr(s, key + "_snd")
        snd[0] = lx[block.own(0)]
        snd[1] = ly[pl.ds(0, block.X, stride=block.Y)]
        snd[2] = pack(lambda i: lz[block.own(i)], 16, 16, 0)
        rcv = getattr(s, key + "_rcv")
        pl.semaphore_wait(barrier, len(FACES))
        return copies(
            DOWN,
            lambda k: snd.at[k],
            lambda k: rcv.at[k],
            getattr(s, key + "_ss"),
            getattr(s, key + "_rs"),
        )

    def coefficients(level, lx, ly, lz, key):
        block = B0
        rcv = getattr(s, key + "_rcv")
        lyp = getattr(s, f"lyp{level}")
        c = {k: getattr(s, f"{k}{level}") for k in ("cxl", "cxu", "cyl", "cyu", "czl", "czu")}
        d15, kw = getattr(s, f"d15{level}"), getattr(s, f"kw{level}")
        for i in range(block.X):
            lyp[pl.ds(i * block.pitch, block.Y)] = ly[block.own(i)]
        lyp[pl.ds(block.Y, block.X, stride=block.pitch)] = rcv[1] * top_y
        next_x = rcv[0] * top_x
        next_z = rcv[2] * top_z
        lane, row = lanes(block.Y), sublanes(block.Y)
        keep_y = jnp.where(row == 0, low_y, 1.0)
        keep_z = jnp.where(lane == 0, low_z, 1.0)
        for i in range(block.X):
            own = block.own(i)
            a_xl = lx[own]
            a_xu = lx[block.own(i + 1)] if i + 1 < block.X else next_x
            a_yl = ly[own]
            a_yu = lyp[pl.ds(i * block.pitch + 1, block.Y)]
            a_zl = lz[own]
            a_zu = jnp.where(
                lane == block.Z - 1, turn(next_z, block.Z - 1 - i), turn(a_zl, -1)
            )
            total = (a_xl + a_yl + a_zl) + (a_xu + a_yu + a_zu)
            scale = RELAX / total
            d15[own] = (1.5 * block.weight) * total
            kw[own] = scale * (1.0 / block.weight)
            c["cxl"][own] = scale * a_xl * (low_x if i == 0 else 1.0)
            c["cxu"][own] = scale * a_xu
            c["cyl"][own] = scale * a_yl * keep_y
            c["cyu"][own] = scale * a_yu
            c["czl"][own] = scale * a_zl * keep_z
            c["czu"][own] = scale * a_zu

    def stencil(level, ref, low, high, emit):
        block = B0
        lane = lanes(block.Y)
        get = lambda k: getattr(s, f"{k}{level}")
        for i in range(block.X):
            own = block.own(i)
            v = ref[block.at(i)]
            down = jnp.where(lane == 0, turn(low, -i), turn(v, 1))
            up = jnp.where(lane == block.Z - 1, turn(high, block.Z - 1 - i), turn(v, -1))
            t_x = get("cxl")[own] * ref[block.at(i - 1)] + get("cxu")[own] * ref[block.at(i + 1)]
            t_y = get("cyl")[own] * ref[block.at(i, -1)] + get("cyu")[own] * ref[block.at(i, 1)]
            t_z = get("czl")[own] * down + get("czu")[own] * up
            emit(i, v, get("g")[own] + (t_x + t_y + t_z))

    def smooth(level, source, target, low, high):
        block = B0

        def emit(i, v, total):
            target[block.at(i)] = v * THIRD + total

        stencil(level, source, low, high, emit)

    def residual(level, source, low, high):
        block = B0
        d15, r = getattr(s, f"d15{level}"), getattr(s, f"r{level}")

        def emit(i, v, total):
            r[block.own(i)] = d15[block.own(i)] * (total - RELAX * v)

        stencil(level, source, low, high, emit)


    lane8, lane16 = lanes(8), lanes(16)
    row8, row16 = sublanes(8), sublanes(16)
    upper_half = row8 < 4
    slices_x = {1: (5, 3), -1: (0, 3), 0: (0, 8)}
    pairs_x = {1: (2, 2), -1: (0, 2), 0: (0, 4)}
    flat_yr = [(x, y) for x in (1, -1, 0) for y in (1, -1)]
    flat_zr = [(x, y, z) for x in (1, -1, 0) for y in (1, -1, 0) for z in (1, -1)]

    def send_around():
        zeds = [jnp.zeros((8, 128), F32)] * 2
        group = lane8 // 3
        for a in range(5):
            for i in range(4):
                even, odd = s.hw_own[a, 2 * i], s.hw_own[a, 2 * i + 1]
                s.hw_low[a, i] = jnp.where(upper_half, even, turn(odd, 4, 0))
                s.hw_high[a, i] = jnp.where(upper_half, turn(even, 4, 0), odd)
            for x in range(8):
                v, place = s.hw_own[a, x], 8 * a + x
                zeds = [
                    jnp.where(group == place, turn(v, 3 * place - first), zed)
                    for zed, first in zip(zeds, (61, 0))
                ]
        s.hw_zed[0], s.hw_zed[1] = zeds

        def source(k):
            x, y, z = AROUND[k]
            if z != 0:
                return s.hw_zed.at[0 if z > 0 else 1]
            if y != 0:
                return (s.hw_low if y < 0 else s.hw_high).at[:, pl.ds(*pairs_x[x])]
            return s.hw_own.at[:, pl.ds(*slices_x[x])]

        def target(k):
            x, y, z = AROUND[k]
            if z != 0:
                return s.hw_zr.at[flat_zr.index((x, y, z))]
            if y != 0:
                return s.hw_yr.at[flat_yr.index((x, y)), :, pl.ds(0, pairs_x[x][1])]
            return s.hw_xr.at[0 if x > 0 else 1]

        return copies(AROUND, source, target, s.hw_ss, s.hw_rs)

    def assemble(a, k):
        x = k - 4
        if x < 0:
            d, layer, first = 1, x + 8, 5
        elif x < 8:
            d, layer, first = 0, x, 0
        else:
            d, layer, first = -1, x - 8, 0
        place = 3 * (8 * a + layer)
        inner = s.hw_own[a, layer] if d == 0 else s.hw_xr[0 if d > 0 else 1, a, layer - first]
        pair = layer // 2 - pairs_x[d][0]
        above = s.hw_yr[flat_yr.index((d, -1)), a, pair]
        below = s.hw_yr[flat_yr.index((d, 1)), a, pair]
        if layer % 2 == 0:
            below = turn(below, 4, 0)
        else:
            above = turn(above, 4, 0)
        outer = jnp.where(upper_half, above, below)
        whole = jnp.concatenate([inner, outer], axis=0)

        def side(z):
            zed = lambda y: s.hw_zr[flat_zr.index((d, y, z))]
            outer = jnp.where(upper_half, zed(-1), zed(1))
            return jnp.concatenate([zed(0), outer], axis=0)

        whole = jnp.where((lane16 >= 64) & (lane16 < 72), turn(side(-1), 64 - place), whole)
        return jnp.where(lane16 >= 120, turn(side(1), 125 - place), whole)

    def ext1(k):
        return pl.ds(16 * k, 16)

    def pad1(k):
        return pl.ds(16 * k + 16, 16)

    def coefficients1(first, last):
        keep_y = jnp.where(row16 == 0, low_y, 1.0)
        keep_z = jnp.where(lane16 == 0, low_z, 1.0)
        last_y = jnp.where(row16 == 7, top_y, 1.0)
        last_z = jnp.where(lane16 == 63, top_z, 1.0)
        for k in range(first, last + 1):
            own = ext1(k)
            a_xl, a_yl, a_zl = s.ext1[0, own], s.ext1[1, own], s.ext1[2, own]
            a_xu = s.ext1[0, ext1(k + 1)]
            if k == 11:
                a_xu = a_xu * top_x
            a_yu = turn(a_yl, -1, 0) * last_y
            a_zu = turn(a_zl, -1) * last_z
            total = (a_xl + a_yl + a_zl) + (a_xu + a_yu + a_zu)
            scale = RELAX / total
            s.kw1[own] = scale * 4.0
            s.d151[own] = (1.5 * 0.25) * total
            s.cxl1[own] = scale * a_xl * (low_x if k == 4 else 1.0)
            s.cxu1[own] = scale * a_xu
            s.cyl1[own] = scale * a_yl * keep_y
            s.cyu1[own] = scale * a_yu
            s.czl1[own] = scale * a_zl * keep_z
            s.czu1[own] = scale * a_zu

    def send_faces1(ref, key):
        snd, rcv = getattr(s, key + "_snd"), getattr(s, key + "_rcv")
        inner = lambda i: ref[pl.ds(16 * (i + 5), 8)]
        snd[0] = inner(7)
        snd[1] = inner(0)
        snd[2] = ref[pl.ds(16 * 5 + 7, 8, stride=16)]
        snd[3] = ref[pl.ds(16 * 5, 8, stride=16)]
        snd[4] = pack(inner, 8, 8, 63)
        snd[5] = pack(inner, 8, 8, 0)
        return copies(
            FACES,
            lambda k: snd.at[k],
            lambda k: rcv.at[k],
            getattr(s, key + "_ss"),
            getattr(s, key + "_rs"),
        )

    def fill1(ref, halo):
        low, high = halo[4], halo[5]
        for i in range(8):
            own = pl.ds(16 * (i + 5), 8)
            v = jnp.where(lane8 == 64, turn(high, 64 - i), ref[own])
            ref[own] = jnp.where(lane8 == 127, turn(low, 127 - i), v)
        ref[pl.ds(16 * 4, 8)] = halo[0]
        ref[pl.ds(16 * 13, 8)] = halo[1]
        ref[pl.ds(16 * 5 + 15, 8, stride=16)] = halo[2]
        ref[pl.ds(16 * 5 + 8, 8, stride=16)] = halo[3]

    def stencil1(first, last, ref, emit):
        for k in range(first, last + 1):
            own = ext1(k)
            v = ref[pad1(k)]
            t_x = s.cxl1[own] * ref[pad1(k - 1)] + s.cxu1[own] * ref[pad1(k + 1)]
            t_y = s.cyl1[own] * turn(v, 1, 0) + s.cyu1[own] * turn(v, -1, 0)
            t_z = s.czl1[own] * turn(v, 1) + s.czu1[own] * turn(v, -1)
            emit(k, v, s.g1[own] + (t_x + t_y + t_z))

    def smooth1(first, last, source, target):
        def emit(k, v, total):
            target[pad1(k)] = v * THIRD + total

        stencil1(first, last, source, emit)

    even8 = (2 * lane8) & 127
    half16 = lane16 >> 1

    def pair_z(value):
        return value + turn(value, -1)

    def stage_z(arrays, snd):
        group = lane16 >> 4
        packed = jnp.zeros((16, 128), F32)
        for a in range(arrays):
            whole = s.t16[a]
            for p in range(2):
                moved = take(whole, 4 * (lane16 & 15) + 2 * p)
                packed = jnp.where(group == ((gz + 2 * a + p) & 7), moved, packed)
        snd[...] = packed

    def merge_z(arrays, snd, rcv, target):
        group = lane16 >> 4
        parts = [(0, snd[...])] + [(RING_Z[k][2], rcv[k]) for k in range(7)]
        for q in range(2 * arrays):
            merged = jnp.zeros((16, 128), F32)
            for distance, part in parts:
                merged = jnp.where(group == ((gz - distance + q) & 7), part, merged)
            target[q] = turn(merged, -16 * q)

    for load in loads[:3]:
        load.wait()
    round_a0 = send_upper(s.fx, s.fy, s.fz, "a0")

    for i in range(8):
        own = pl.ds(8 * i, 8)
        here = lambda ref, shift: ref[pl.ds(32 * i + shift, 8, stride=2)]
        s.fx1[own] = take(pair_z(here(s.fx, 0) + here(s.fx, 1)), even8) * 0.25
        s.fy1[own] = take(pair_z(here(s.fy, 0) + here(s.fy, 16)), even8) * 0.25
        total = (here(s.fz, 0) + here(s.fz, 1)) + (here(s.fz, 16) + here(s.fz, 17))
        s.fz1[own] = take(total, even8) * 0.25
    s.a1_snd[0] = s.fx1[pl.ds(0, 8)]
    s.a1_snd[1] = s.fy1[pl.ds(0, 8, stride=8)]
    s.a1_snd[2] = pack(lambda i: s.fz1[pl.ds(8 * i, 8)], 8, 8, 0)
    round_a1 = copies(
        DOWN, lambda k: s.a1_snd.at[k], lambda k: s.a1_rcv.at[k], s.a1_ss, s.a1_rs
    )
    for i in range(4):
        own = pl.ds(4 * i, 4)
        here = lambda ref, shift: ref[pl.ds(16 * i + shift, 4, stride=2)]
        s.t16[0, own] = here(s.fx1, 0) + here(s.fx1, 1)
        s.t16[1, own] = here(s.fy1, 0) + here(s.fy1, 8)
        total = (here(s.fz1, 0) + here(s.fz1, 1)) + (here(s.fz1, 8) + here(s.fz1, 9))
        s.t16[2, own] = total * 0.25
    s.t16[0] = pair_z(s.t16[0]) * 0.25
    s.t16[1] = pair_z(s.t16[1]) * 0.25
    stage_z(3, s.zf_snd)
    for ref in (s.va1, s.vb1):
        for k in (-1, 17):
            ref[pad1(k)] = jnp.zeros((16, 128), F32)
    for p in range(2):
        for x in (0, 1, 18, 19):
            for ref in (s.va2, s.vb2):
                ref[p, x] = jnp.zeros((16, 128), F32)
        for x in range(16):
            s.f2[p, x + 2] = jnp.zeros((16, 128), F32)
    for ref in (s.va3, s.vb3):
        for k in range(2):
            ref[pl.ds(8 * k, 8)] = jnp.zeros((8, 128), F32)
            ref[pl.ds(144 + 8 * k, 8)] = jnp.zeros((8, 128), F32)
    s.p2[...] = jnp.zeros_like(s.p2)
    s.ext1[...] = jnp.ones_like(s.ext1)
    for k in (0, 1, 2, 3, 12, 13, 14, 15):
        s.va1[pad1(k)] = jnp.zeros((16, 128), F32)
        s.vb1[pad1(k)] = jnp.zeros((16, 128), F32)

    loads[3].wait()
    finish(round_a0)
    coefficients(0, s.fx, s.fy, s.fz, "a0")
    for i in range(16):
        own = B0.own(i)
        start = s.kw0[own] * s.rhs[own]
        s.g0[own] = start
        s.va0[B0.at(i)] = start
    round_b = send_faces(B0, s.va0, "b")
    finish(round_a1)
    for i in range(8):
        own, here = pl.ds(8 * i, 8), pl.ds(16 * (i + 4), 8)
        s.ext1[0, here] = s.fx1[own]
        s.ext1[1, here] = s.fy1[own]
        upper = turn(s.a1_rcv[2], 64 - i)
        s.ext1[2, here] = jnp.where(lane8 == 64, upper, s.fz1[own])
        s.hw_own[0, i] = s.fx1[own]
        s.hw_own[1, i] = s.fy1[own]
        s.hw_own[2, i] = s.fz1[own]
    s.ext1[0, pl.ds(16 * 12, 8)] = s.a1_rcv[0]
    s.ext1[1, pl.ds(16 * 4 + 8, 8, stride=16)] = s.a1_rcv[1]
    coefficients1(4, 11)
    finish(round_b)
    fill(B0, s.va0, s.b_rcv)
    smooth(0, s.va0, s.vb0, s.b_rcv[4], s.b_rcv[5])
    round_c = send_faces(B0, s.vb0, "c")
    finish(round_c)
    fill(B0, s.vb0, s.c_rcv)
    residual(0, s.vb0, s.c_rcv[4], s.c_rcv[5])

    for i in range(8):
        here = lambda shift: s.r0[pl.ds(32 * i + shift, 8, stride=2)]
        total = (here(0) + here(1)) + (here(16) + here(17))
        forcing = take(pair_z(total), even8) * 0.125
        s.hw_own[3, i] = forcing
        start = s.kw1[pl.ds(16 * (i + 4), 8)] * forcing
        s.g1[pl.ds(16 * (i + 4), 8)] = start
        s.g1[pl.ds(16 * (i + 4) + 8, 8)] = jnp.zeros((8, 128), F32)
        s.va1[pl.ds(16 * (i + 5), 8)] = start
        s.va1[pl.ds(16 * (i + 5) + 8, 8)] = jnp.zeros((8, 128), F32)
    round_d = send_faces1(s.va1, "d")
    round_zf = copies(
        RING_Z, lambda k: s.zf_snd, lambda k: s.zf_rcv.at[k], s.zf_ss, s.zf_rs
    )
    finish(round_d)
    fill1(s.va1, s.d_rcv)
    smooth1(4, 11, s.va1, s.vb1)
    for i in range(8):
        s.hw_own[4, i] = s.vb1[pl.ds(16 * (i + 5), 8)]
    round_e = send_faces1(s.vb1, "e")
    finish(round_zf)
    merge_z(3, s.zf_snd, s.zf_rcv, s.xf_snd)
    round_xf = copies(
        LINE, lambda k: s.xf_snd, lambda k: s.xf_rcv.at[k], s.xf_ss, s.xf_rs
    )


    def block2(p, x):
        return (p, x + 2)

    def spread(arrays, offsets, snd, rcv, targets):
        parts = [((0, 0, 0), lambda q: snd.at[q])]
        for k, offset in enumerate(offsets):
            parts.append((offset, lambda q, k=k: rcv.at[k, q]))
        for offset, part in parts:
            first = 4 * ((gx - offset[0]) & 3)
            place = pl.ds(4 * (1 - offset[1]), 4)
            for a in range(arrays):
                for p in range(2):
                    for x in range(4):
                        piece = part(2 * a + p)[pl.ds(4 * x, 4)]
                        targets[a][p, x + 2 + first, place] = piece

    def send_sides(refs, key):
        snd, rcv = getattr(s, key + "_snd"), getattr(s, key + "_rcv")
        for a, ref in enumerate(refs):
            for p in range(2):
                for i in range(8):
                    even = ref[p, 2 * i + 2, pl.ds(0, 8)]
                    odd = ref[p, 2 * i + 3, pl.ds(0, 8)]
                    snd[a, p, i] = jnp.where(upper_half, turn(even, 4, 0), odd)
        return copies(
            SIDES,
            lambda k: snd,
            lambda k: rcv.at[k],
            getattr(s, key + "_ss"),
            getattr(s, key + "_rs"),
        )

    def take_sides(refs, key, rest):
        rcv = getattr(s, key + "_rcv")
        for a, ref in enumerate(refs):
            for p in range(2):
                for x in range(16):
                    below, above = rcv[0, a, p, x // 2], rcv[1, a, p, x // 2]
                    if x % 2 == 1:
                        below, above = turn(below, 4, 0), turn(above, 4, 0)
                    own = ref[p, x + 2, pl.ds(0, 8)]
                    ref[p, x + 2, pl.ds(0, 8)] = jnp.where(upper_half, below, own)
                    ref[p, x + 2, pl.ds(8, 8)] = jnp.where(upper_half, above, rest)

    faces2 = (s.lx2, s.ly2, s.lz2)
    global_y = row16 + 4 * gy - 4
    not_low, not_top = global_y != 0, global_y != 4 * GY - 1

    finish(round_e)
    fill1(s.vb1, s.e_rcv)

    def emit_r1(k, v, total):
        r = s.d151[ext1(k)] * (total - RELAX * v)
        s.r1[pl.ds(8 * (k - 4), 8)] = r[0:8]

    stencil1(4, 11, s.vb1, emit_r1)
    for i in range(4):
        here = lambda shift: s.r1[pl.ds(16 * i + shift, 4, stride=2)]
        s.t16[0, pl.ds(4 * i, 4)] = (here(0) + here(1)) + (here(8) + here(9))
    s.t16[0] = pair_z(s.t16[0]) * 0.125
    stage_z(1, s.zr_snd)
    round_zr = copies(
        RING_Z, lambda k: s.zr_snd, lambda k: s.zr_rcv.at[k], s.zr_ss, s.zr_rs
    )

    finish(round_xf)
    spread(3, LINE, s.xf_snd, s.xf_rcv, faces2)
    round_nf = send_sides(faces2, "nf")

    for a, ref in enumerate((s.lx2, s.ly2, s.lz2)):
        for i in range(8):
            total = ref[block2(0, 2 * i)]
            if a != 2:
                total = total + ref[block2(1, 2 * i)]
            if a != 0:
                total = total + ref[block2(0, 2 * i + 1)]
            if a == 1:
                total = total + ref[block2(1, 2 * i + 1)]
            s.s2[pl.ds(16 * i, 16)] = total
        for j in range(2):
            total = s.s2[pl.ds(4 + 2 * j, 8, stride=16)]
            if a != 1:
                total = total + s.s2[pl.ds(5 + 2 * j, 8, stride=16)]
            s.face3[a, pl.ds(pl.multiple_of(16 * gy + 8 * j, 8), 8)] = total * 0.25
    mine = pl.ds(pl.multiple_of(16 * gy, 16), 16)
    round_yf = copies(
        RING_Y,
        lambda k: s.face3.at[:, mine],
        lambda k: s.face3.at[:, mine],
        s.yf_ss,
        s.yf_rs,
    )
    round_hw = send_around()

    def stencil2(ref, emit):
        for p in range(2):
            for x in range(16):
                j, other = block2(p, x), block2(1 - p, x)
                v, w = ref[j], ref[other]
                t_x = s.cxl2[j] * ref[block2(p, x - 1)] + s.cxu2[j] * ref[block2(p, x + 1)]
                t_y = s.cyl2[j] * turn(v, 1, 0) + s.cyu2[j] * turn(v, -1, 0)
                down, up = (turn(w, 1), w) if p == 0 else (w, turn(w, -1))
                t_z = s.czl2[j] * down + s.czu2[j] * up
                emit(j, v, s.g2[j] + (t_x + t_y + t_z))

    def smooth2(source, target):
        def emit(j, v, total):
            target[j] = v * THIRD + total

        stencil2(source, emit)

    finish(round_zr)
    merge_z(1, s.zr_snd, s.zr_rcv, s.xr_snd)
    round_xr = copies(
        PLANE, lambda k: s.xr_snd, lambda k: s.xr_rcv.at[k], s.xr_ss, s.xr_rs
    )

    finish(round_nf)
    take_sides(faces2, "nf", 1.0)
    for p in range(2):
        for x in range(16):
            j = block2(p, x)
            a_xl, a_yl, a_zl = s.lx2[j], s.ly2[j], s.lz2[j]
            a_xu = s.lx2[block2(p, x + 1)] if x < 15 else jnp.zeros((16, 128), F32)
            a_yu = jnp.where(not_top, turn(a_yl, -1, 0), 0.0)
            if p == 0:
                a_zu = s.lz2[block2(1, x)]
            else:
                a_zu = jnp.where(lane16 == 127, 0.0, turn(s.lz2[block2(0, x)], -1))
            total = (a_xl + a_yl + a_zl) + (a_xu + a_yu + a_zu)
            scale = RELAX / total
            s.d152[j] = (1.5 * 0.0625) * total
            s.kw2[j] = scale * 16.0
            s.cxl2[j] = scale * a_xl if x > 0 else jnp.zeros((16, 128), F32)
            s.cxu2[j] = scale * a_xu
            s.cyl2[j] = jnp.where(not_low, scale * a_yl, 0.0)
            s.cyu2[j] = scale * a_yu
            s.czl2[j] = scale * a_zl if p == 1 else jnp.where(lane16 == 0, 0.0, scale * a_zl)
            s.czu2[j] = scale * a_zu

    finish(round_yf)
    zero8 = jnp.zeros((8, 128), F32)
    for y in range(16):
        own = pl.ds(8 * y, 8)
        a_xl, a_yl, a_zl = s.face3[0, own], s.face3[1, own], s.face3[2, own]
        a_xu = jnp.where(row8 == 7, 0.0, turn(a_xl, -1, 0))
        a_yu = s.face3[1, pl.ds(8 * y + 8, 8)] if y < 15 else zero8
        a_zu = jnp.where(lane8 == 127, 0.0, turn(a_zl, -1))
        total = (a_xl + a_yl + a_zl) + (a_xu + a_yu + a_zu)
        scale = RELAX / total
        s.d153[own] = (1.5 * 0.25**3) * total
        s.kw3[own] = scale * 64.0
        s.cxl3[own] = jnp.where(row8 == 0, 0.0, scale * a_xl)
        s.cxu3[own] = scale * a_xu
        s.cyl3[own] = scale * a_yl if y > 0 else zero8
        s.cyu3[own] = scale * a_yu
        s.czl3[own] = jnp.where(lane8 == 0, 0.0, scale * a_zl)
        s.czu3[own] = scale * a_zu

    lane32, row32 = lanes(32), sublanes(32)

    def both(value, lane, step):
        return value + jnp.where(
            (lane & step) == 0, turn(value, -step), turn(value, step)
        )

    def lower_of(value, lane, step):
        return jnp.where((lane & step) == 0, value, turn(value, step))

    for a in range(3):
        for y in range(8):
            here = lambda shift: s.face3[a, pl.ds(16 * y + shift, 4, stride=2)]
            if a == 0:
                total = here(0) + here(8)
            elif a == 1:
                total = here(0) + here(1)
            else:
                total = (here(0) + here(1)) + (here(8) + here(9))
            s.t4[pl.ds(4 * y, 4)] = total
        total = s.t4[...]
        total = both(total, lane32, 1) if a < 2 else lower_of(total, lane32, 1)
        s.fc4[a] = total * 0.25
    a_xl, a_yl, a_zl = s.fc4[0], s.fc4[1], s.fc4[2]
    a_xu = jnp.where((row32 & 3) == 3, 0.0, turn(a_xl, -1, 0))
    a_yu = jnp.where(row32 >= 28, 0.0, turn(a_yl, -4, 0))
    a_zu = jnp.where(lane32 >= 126, 0.0, turn(a_zl, -2))
    total = (a_xl + a_yl + a_zl) + (a_xu + a_yu + a_zu)
    scale = RELAX / total
    s.d154[...] = (1.5 * 0.25**4) * total
    s.kw4[...] = scale * 256.0
    s.cxl4[...] = jnp.where((row32 & 3) == 0, 0.0, scale * a_xl)
    s.cxu4[...] = scale * a_xu
    s.cyl4[...] = jnp.where(row32 < 4, 0.0, scale * a_yl)
    s.cyu4[...] = scale * a_yu
    s.czl4[...] = jnp.where(lane32 < 2, 0.0, scale * a_zl)
    s.czu4[...] = scale * a_zu

    faces5 = []
    for a in range(3):
        for x in range(2):
            here = lambda shift: s.fc4[a, pl.ds(2 * x + shift, 4, stride=8)]
            if a == 0:
                total = here(0) + here(4)
            elif a == 1:
                total = here(0) + here(1)
            else:
                total = (here(0) + here(1)) + (here(4) + here(5))
            s.t5[pl.ds(4 * x, 4)] = total
        total = s.t5[...]
        total = both(total, lane8, 2) if a < 2 else lower_of(total, lane8, 2)
        faces5.append(total * 0.25)
    a_xl, a_yl, a_zl = faces5
    a_xu = jnp.where(row8 >= 4, 0.0, turn(a_xl, 4, 0))
    a_yu = jnp.where((row8 & 3) == 3, 0.0, turn(a_yl, -1, 0))
    a_zu = jnp.where(lane8 >= 124, 0.0, turn(a_zl, -4))
    total = (a_xl + a_yl + a_zl) + (a_xu + a_yu + a_zu)
    scale = RELAX / total
    s.kw5[...] = scale * 1024.0
    s.cx5[...] = jnp.where(row8 >= 4, scale * a_xl, scale * a_xu)
    s.cyl5[...] = jnp.where((row8 & 3) == 0, 0.0, scale * a_yl)
    s.cyu5[...] = scale * a_yu
    s.czl5[...] = jnp.where(lane8 < 4, 0.0, scale * a_zl)
    s.czu5[...] = scale * a_zu

    finish(round_xr)
    spread(1, PLANE, s.xr_snd, s.xr_rcv, (s.f2,))
    for p in range(2):
        for x in range(16):
            j = block2(p, x)
            start = s.kw2[j] * s.f2[j]
            s.g2[j] = start
            s.va2[j] = start
    smooth2(s.va2, s.vb2)

    def emit_r2(j, v, total):
        s.f2[j] = s.d152[j] * (total - RELAX * v)

    stencil2(s.vb2, emit_r2)
    for i in range(8):
        total = (s.f2[block2(0, 2 * i)] + s.f2[block2(1, 2 * i)]) + (
            s.f2[block2(0, 2 * i + 1)] + s.f2[block2(1, 2 * i + 1)]
        )
        s.s2[pl.ds(16 * i, 16)] = total
    for j in range(2):
        total = s.s2[pl.ds(4 + 2 * j, 8, stride=16)] + s.s2[pl.ds(5 + 2 * j, 8, stride=16)]
        s.f3[pl.ds(pl.multiple_of(16 * gy + 8 * j, 8), 8)] = total * 0.125
    round_yr = copies(
        RING_Y, lambda k: s.f3.at[mine], lambda k: s.f3.at[mine], s.yr_ss, s.yr_rs
    )
    round_nv = send_sides((s.vb2,), "nv")

    finish(round_hw)
    for k in range(1, 15):
        for a in range(4):
            s.ext1[a, ext1(k)] = assemble(a, k)
        s.vb1[pad1(k)] = assemble(4, k)
    coefficients1(2, 13)
    for k in range(2, 14):
        s.g1[ext1(k)] = s.kw1[ext1(k)] * s.ext1[3, ext1(k)]
    finish(round_yr)

    def at3(y):
        return pl.ds(16 + 8 * y, 8)

    def stencil3(ref, emit):
        for y in range(16):
            own = pl.ds(8 * y, 8)
            v = ref[at3(y)]
            t_x = s.cxl3[own] * turn(v, 1, 0) + s.cxu3[own] * turn(v, -1, 0)
            t_y = s.cyl3[own] * ref[at3(y - 1)] + s.cyu3[own] * ref[at3(y + 1)]
            t_z = s.czl3[own] * turn(v, 1) + s.czu3[own] * turn(v, -1)
            emit(y, v, s.g3[own] + (t_x + t_y + t_z))

    def smooth3(source, target):
        def emit(y, v, total):
            target[at3(y)] = v * THIRD + total

        stencil3(source, emit)

    for y in range(16):
        own = pl.ds(8 * y, 8)
        start = s.kw3[own] * s.f3[own]
        s.g3[own] = start
        s.va3[at3(y)] = start
    smooth3(s.va3, s.vb3)

    def emit_r3(y, v, total):
        own = pl.ds(8 * y, 8)
        s.r3[own] = s.d153[own] * (total - RELAX * v)

    stencil3(s.vb3, emit_r3)
    for y in range(8):
        here = lambda shift: s.r3[pl.ds(16 * y + shift, 4, stride=2)]
        s.t4[pl.ds(4 * y, 4)] = (here(0) + here(1)) + (here(8) + here(9))
    f4 = both(s.t4[...], lane32, 1) * 0.125

    def total4(v):
        t_x = s.cxl4[...] * turn(v, 1, 0) + s.cxu4[...] * turn(v, -1, 0)
        t_y = s.cyl4[...] * turn(v, 4, 0) + s.cyu4[...] * turn(v, -4, 0)
        t_z = s.czl4[...] * turn(v, 2) + s.czu4[...] * turn(v, -2)
        return g4 + (t_x + t_y + t_z)

    g4 = s.kw4[...] * f4
    v4 = g4
    v4 = v4 * THIRD + total4(v4)
    s.r4[...] = s.d154[...] * (total4(v4) - RELAX * v4)
    for x in range(2):
        here = lambda shift: s.r4[pl.ds(2 * x + shift, 4, stride=8)]
        s.t5[pl.ds(4 * x, 4)] = (here(0) + here(1)) + (here(4) + here(5))
    g5 = s.kw5[...] * (both(s.t5[...], lane8, 2) * 0.125)
    cx5, cyl5, cyu5, czl5, czu5 = s.cx5[...], s.cyl5[...], s.cyu5[...], s.czl5[...], s.czu5[...]

    def sweep5(index, v):
        t_y = cyl5 * turn(v, 1, 0) + cyu5 * turn(v, -1, 0)
        t_z = czl5 * turn(v, 4) + czu5 * turn(v, -4)
        return (v * THIRD + g5) + (cx5 * turn(v, 4, 0) + (t_y + t_z))

    s.e5[...] = lax.fori_loop(0, COARSE_SWEEPS - 1, sweep5, g5)
    for x in range(2):
        piece = s.e5[pl.ds(4 * x, 4)]
        for shift in (0, 1, 4, 5):
            s.p4[pl.ds(2 * x + shift, 4, stride=8)] = piece
    v4 = v4 + s.p4[...]
    v4 = v4 * THIRD + total4(v4)
    v4 = v4 * THIRD + total4(v4)
    s.r4[...] = v4
    for x in range(4):
        piece = s.r4[pl.ds(x, 8, stride=4)]
        for shift in (0, 1, 8, 9):
            s.p3[pl.ds(2 * x + shift, 8, stride=16)] = piece
    for y in range(16):
        s.vb3[at3(y)] = s.vb3[at3(y)] + s.p3[pl.ds(8 * y, 8)]
    smooth3(s.vb3, s.va3)
    smooth3(s.va3, s.vb3)

    finish(round_nv)
    take_sides((s.vb2,), "nv", 0.0)
    for k in range(6):
        piece = s.vb3[pl.ds(pl.multiple_of(16 * gy + 8 * k, 8), 8)]
        for x in range(2):
            for y in range(2):
                s.p2[pl.ds(16 * x + 2 * k + y, 8, stride=32)] = piece
    for x in range(16):
        more = s.p2[pl.ds(16 * x, 16)]
        for p in range(2):
            s.vb2[block2(p, x)] = s.vb2[block2(p, x)] + more
    smooth2(s.vb2, s.va2)
    smooth2(s.va2, s.vb2)

    signed = jnp.where(lane16 < 96, lane16, lane16 - 128)
    index = (16 * gz + (signed >> 2)) & 127
    odd = ((signed >> 1) & 1) == 1
    for k in range(8):
        x = 4 * gx + k
        piece = jnp.where(odd, take(s.vb2[1, x], index), take(s.vb2[0, x], index))
        rows = jnp.where(row16 < 6, turn(piece, -4, 0), turn(piece, 4, 0))[0:8]
        for y in range(2):
            s.q1[pl.ds(16 * k + y, 8, stride=2)] = rows
        more = s.q1[pl.ds(16 * k, 16)]
        for i in (2 * k, 2 * k + 1):
            if 1 <= i <= 14:
                s.vb1[pad1(i)] = s.vb1[pad1(i)] + more
    smooth1(2, 13, s.vb1, s.va1)
    smooth1(3, 12, s.va1, s.vb1)
    s.h1[0] = s.vb1[pl.ds(16 * 4, 8)]
    s.h1[1] = s.vb1[pl.ds(16 * 13, 8)]
    s.h1[2] = s.vb1[pl.ds(16 * 5 + 15, 8, stride=16)]
    s.h1[3] = s.vb1[pl.ds(16 * 5 + 8, 8, stride=16)]
    inner = lambda i: s.vb1[pl.ds(16 * (i + 5), 8)]
    s.h1[4] = pack(inner, 8, 8, 127)
    s.h1[5] = pack(inner, 8, 8, 64)

    def widen(value, ref, start):
        ref[pl.ds(start, 8, stride=2)] = value
        ref[pl.ds(start + 1, 8, stride=2)] = value
        return take(ref[pl.ds(start, 16)], half16)

    for i in range(8):
        more = widen(inner(i), s.w0, 16 * i)
        for x in (2 * i, 2 * i + 1):
            s.vb0[B0.at(x)] = s.vb0[B0.at(x)] + more
    for k in range(6):
        s.c_rcv[k] = s.c_rcv[k] + widen(s.h1[k], s.w0, 128 + 16 * k)
    fill(B0, s.vb0, s.c_rcv)
    smooth(0, s.vb0, s.va0, s.c_rcv[4], s.c_rcv[5])
    round_h = send_faces(B0, s.va0, "h")
    finish(round_h)
    fill(B0, s.va0, s.h_rcv)

    def emit_out(i, v, total):
        out[B0.own(i)] = v * THIRD + total

    stencil(0, s.va0, s.h_rcv[4], s.h_rcv[5], emit_out)


def shards(rhs, face_x, face_y, face_z):
    flat = [a.reshape(256, 128) for a in (rhs, face_x, face_y, face_z)]
    whole = pl.pallas_call(
        cycle,
        out_shape=jax.ShapeDtypeStruct((256, 128), F32),
        in_specs=[pl.BlockSpec(memory_space=pltpu.HBM)] * 4,
        out_specs=pl.BlockSpec(memory_space=pltpu.VMEM),
        scratch_shapes=list(SCRATCH.values()),
        compiler_params=pltpu.CompilerParams(
            collective_id=0, has_side_effects=True, vmem_limit_bytes=64 * 1024 * 1024
        ),
        name="vcycle",
    )(*flat)
    return whole.reshape(16, 16, 128)


def solution(mesh):
    placed = P("gx", "gy", "gz")
    return jax.shard_map(
        shards, mesh=mesh, in_specs=(placed,) * 4, out_specs=placed, check_vma=False
    )
```

```python
import jax
import jax.numpy as jnp
from jax import lax
from jax.experimental import pallas as pl
from jax.experimental.pallas import tpu as pltpu
from jax.sharding import PartitionSpec as P

RELAX = 2.0 / 3.0
THIRD = 1.0 / 3.0
COARSE_SWEEPS = 24
GX, GY, GZ = 4, 8, 8
F32 = jnp.float32
MESH = pl.DeviceIdType.MESH

FACES = [(1, 0, 0), (-1, 0, 0), (0, 1, 0), (0, -1, 0), (0, 0, 1), (0, 0, -1)]
DOWN = [(-1, 0, 0), (0, -1, 0), (0, 0, -1)]
RING_Z = [(0, 0, k) for k in (4, 3, 5, 2, 6, 1, 7)]
RING_Y = [(0, k, 0) for k in (4, 3, 5, 2, 6, 1, 7)]
AROUND = [
    (x, y, z) for x in (1, -1, 0) for y in (1, -1, 0) for z in (1, -1, 0) if (x, y, z) != (0, 0, 0)
]
AROUND.sort(key=lambda d: -(abs(d[0]) + abs(d[1]) + abs(d[2])))
LINE = [(2, 0, 0), (1, 0, 0), (3, 0, 0)]
SIDES = [(0, 1, 0), (0, -1, 0)]
PLANE = [(2, 1, 0), (2, -1, 0), (1, 1, 0), (1, -1, 0), (3, 1, 0), (3, -1, 0)]
PLANE += [(2, 0, 0), (0, 1, 0), (0, -1, 0), (1, 0, 0), (3, 0, 0)]


def lanes(rows):
    return lax.broadcasted_iota(jnp.int32, (rows, 128), 1)


def sublanes(rows):
    return lax.broadcasted_iota(jnp.int32, (rows, 128), 0)


def turn(value, steps, axis=1):
    steps %= value.shape[axis]
    return value if steps == 0 else pltpu.roll(value, steps, axis)


def take(value, index):
    return jnp.take_along_axis(value, index, axis=1, mode="promise_in_bounds")


class Block:
    def __init__(self, size_x, size_y, size_z, weight):
        self.X, self.Y, self.Z, self.weight = size_x, size_y, size_z, weight
        self.pitch = size_y + 8
        self.rows = size_x * size_y
        self.padded = 8 + (size_x + 2) * self.pitch

    def base(self, i):
        return 8 + (i + 1) * self.pitch

    def own(self, i):
        return pl.ds(i * self.Y, self.Y)

    def at(self, i, shift=0):
        return pl.ds(self.base(i) + shift, self.Y)

    def row_of_each(self, y):
        return pl.ds(self.base(0) + y, self.X, stride=self.pitch)


B0 = Block(16, 16, 128, 1.0)

SCRATCH = {}


def vmem(name, *shape):
    SCRATCH[name] = pltpu.VMEM(shape, F32)


def dma(name, *shape):
    SCRATCH[name] = pltpu.SemaphoreType.DMA(shape)


for key in ("rhs", "fx", "fy", "fz"):
    vmem(key, 256, 128)
dma("in_sem", 5)
for key in ("cxl0", "cxu0", "cyl0", "cyu0", "czl0", "czu0", "g0", "d150", "kw0", "r0", "w0"):
    vmem(key, 256, 128)
vmem("va0", B0.padded, 128)
vmem("vb0", B0.padded, 128)
vmem("lyp0", B0.X * B0.pitch, 128)
for key in ("fx1", "fy1", "fz1", "r1"):
    vmem(key, 64, 128)
for key in ("cxl1", "cxu1", "cyl1", "cyu1", "czl1", "czu1", "g1", "d151", "kw1"):
    vmem(key, 17 * 16, 128)
for key in ("va1", "vb1"):
    vmem(key, 19 * 16, 128)
vmem("ext1", 4, 17 * 16, 128)
vmem("hw_own", 5, 8, 8, 128)
vmem("hw_pack", 3, 8, 8, 128)
vmem("hw_low", 3, 4, 8, 128)
vmem("hw_high", 3, 4, 8, 128)
vmem("hw_zed", 2, 8, 128)
vmem("hw_xr", 2, 3, 3, 8, 128)
vmem("hw_yr", 6, 3, 4, 8, 128)
vmem("hw_zr", 18, 8, 128)
dma("hw_ss", 26)
dma("hw_rs", 26)
vmem("q1", 8 * 16, 128)
vmem("h1", 6, 8, 128)
for key, rows, count in (("a0", 16, 3), ("b", 16, 6), ("c", 16, 6), ("h", 16, 6), ("a1", 8, 3), ("d", 8, 6), ("e", 8, 6)):
    vmem(f"{key}_snd", count, rows, 128)
    vmem(f"{key}_rcv", count, rows, 128)
    dma(f"{key}_ss", count)
    dma(f"{key}_rs", count)
vmem("t16", 3, 16, 128)
vmem("zf_snd", 4, 3, 16, 128)
vmem("zf_rcv", 7, 4, 3, 16, 128)
vmem("zr_snd", 16, 128)
vmem("zr_rcv", 7, 16, 128)
vmem("xr_snd", 2, 16, 128)
vmem("xr_rcv", 11, 2, 16, 128)
vmem("m2", 6, 16, 128)
for key, count in (("zf", 7), ("zr", 7), ("xr", 11), ("xf", 3), ("nf", 2)):
    dma(f"{key}_ss", count)
    dma(f"{key}_rs", count)
for key in ("f2", "lx2", "ly2", "lz2", "va2", "vb2"):
    vmem(key, 2, 20, 16, 128)
for key in ("cxl2", "cxu2", "cyl2", "cyu2", "czl2", "czu2", "g2", "d152", "kw2"):
    vmem(key, 2, 20, 16, 128)
vmem("nv_snd", 1, 2, 8, 8, 128)
vmem("nv_rcv", 2, 1, 2, 8, 8, 128)
dma("nv_ss", 2)
dma("nv_rs", 2)
vmem("s2", 128, 128)
vmem("p2", 256, 128)
vmem("face3", 3, 128, 128)
vmem("f3", 128, 128)
for key in ("yf", "yr"):
    dma(f"{key}_ss", 7)
    dma(f"{key}_rs", 7)
for key in ("cxl3", "cxu3", "cyl3", "cyu3", "czl3", "czu3", "g3", "d153", "kw3", "r3", "p3"):
    vmem(key, 128, 128)
vmem("va3", 160, 128)
vmem("vb3", 160, 128)
for key in ("t4", "cxl4", "cxu4", "cyl4", "cyu4", "czl4", "czu4", "d154", "kw4", "r4", "p4"):
    vmem(key, 32, 128)
vmem("fc4", 3, 32, 128)
for key in ("t5", "cx5", "cyl5", "cyu5", "czl5", "czu5", "kw5", "e5"):
    vmem(key, 8, 128)


class Space:
    pass


def cycle(rhs_in, fx_in, fy_in, fz_in, out, *scratch):
    s = Space()
    for name, ref in zip(SCRATCH, scratch):
        setattr(s, name, ref)
    gx, gy, gz = lax.axis_index("gx"), lax.axis_index("gy"), lax.axis_index("gz")

    def peer(offset):
        return (
            (gx + offset[0]) & (GX - 1),
            (gy + offset[1]) & (GY - 1),
            (gz + offset[2]) & (GZ - 1),
        )

    loads = [
        pltpu.make_async_copy(source, target, s.in_sem.at[k])
        for k, (source, target) in enumerate(
            ((fx_in, s.fx), (fy_in, s.fy), (fz_in, s.fz), (rhs_in, s.rhs))
        )
    ]
    for load in loads:
        load.start()

    barrier = pltpu.get_barrier_semaphore()
    for offset in FACES:
        pl.semaphore_signal(barrier, inc=1, device_id=peer(offset), device_id_type=MESH)

    def copies(offsets, sources, targets, ss, rs):
        made = [
            pltpu.make_async_remote_copy(
                src_ref=sources(k),
                dst_ref=targets(k),
                send_sem=ss.at[k],
                recv_sem=rs.at[k],
                device_id=peer(offset),
                device_id_type=MESH,
            )
            for k, offset in enumerate(offsets)
        ]
        for one in made:
            one.start()
        return made

    def finish(made):
        for one in made:
            one.wait_recv()
        for one in made:
            one.wait_send()

    def flag(condition):
        return jnp.where(condition, 1.0, 0.0).astype(F32)

    low_x, low_y, low_z = flag(gx > 0), flag(gy > 0), flag(gz > 0)
    top_x, top_y, top_z = flag(gx < GX - 1), flag(gy < GY - 1), flag(gz < GZ - 1)


    def pack(read, rows, count, column):
        packed = jnp.zeros((rows, 128), F32)
        lane = lanes(rows)
        for i in range(count):
            packed = jnp.where(lane == i, turn(read(i), i - column), packed)
        return packed

    def send_faces(block, ref, key):
        snd = getattr(s, key + "_snd")
        snd[0] = ref[block.at(block.X - 1)]
        snd[1] = ref[block.at(0)]
        snd[2] = ref[block.row_of_each(block.Y - 1)]
        snd[3] = ref[block.row_of_each(0)]
        snd[4] = pack(lambda i: ref[block.at(i)], 16, 16, 127)
        snd[5] = pack(lambda i: ref[block.at(i)], 16, 16, 0)
        rcv = getattr(s, key + "_rcv")
        return copies(
            FACES,
            lambda k: snd.at[k],
            lambda k: rcv.at[k],
            getattr(s, key + "_ss"),
            getattr(s, key + "_rs"),
        )

    def fill(block, ref, halo):
        ref[block.at(-1)] = halo[0]
        ref[block.at(block.X)] = halo[1]
        ref[block.row_of_each(-1)] = halo[2]
        ref[block.row_of_each(block.Y)] = halo[3]

    def send_upper(lx, ly, lz, key):
        block = B0
        snd = getattr(s, key + "_snd")
        snd[0] = lx[block.own(0)]
        snd[1] = ly[pl.ds(0, block.X, stride=block.Y)]
        snd[2] = pack(lambda i: lz[block.own(i)], 16, 16, 0)
        rcv = getattr(s, key + "_rcv")
        pl.semaphore_wait(barrier, len(FACES))
        return copies(
            DOWN,
            lambda k: snd.at[k],
            lambda k: rcv.at[k],
            getattr(s, key + "_ss"),
            getattr(s, key + "_rs"),
        )

    def coefficients(level, lx, ly, lz, key):
        block = B0
        rcv = getattr(s, key + "_rcv")
        lyp = getattr(s, f"lyp{level}")
        c = {k: getattr(s, f"{k}{level}") for k in ("cxl", "cxu", "cyl", "cyu", "czl", "czu")}
        d15, kw = getattr(s, f"d15{level}"), getattr(s, f"kw{level}")
        for i in range(block.X):
            lyp[pl.ds(i * block.pitch, block.Y)] = ly[block.own(i)]
        lyp[pl.ds(block.Y, block.X, stride=block.pitch)] = rcv[1] * top_y
        next_x = rcv[0] * top_x
        next_z = rcv[2] * top_z
        lane, row = lanes(block.Y), sublanes(block.Y)
        keep_y = jnp.where(row == 0, low_y, 1.0)
        keep_z = jnp.where(lane == 0, low_z, 1.0)
        for i in range(block.X):
            own = block.own(i)
            a_xl = lx[own]
            a_xu = lx[block.own(i + 1)] if i + 1 < block.X else next_x
            a_yl = ly[own]
            a_yu = lyp[pl.ds(i * block.pitch + 1, block.Y)]
            a_zl = lz[own]
            a_zu = jnp.where(
                lane == block.Z - 1, turn(next_z, block.Z - 1 - i), turn(a_zl, -1)
            )
            total = (a_xl + a_yl + a_zl) + (a_xu + a_yu + a_zu)
            scale = RELAX / total
            d15[own] = (1.5 * block.weight) * total
            kw[own] = scale * (1.0 / block.weight)
            c["cxl"][own] = scale * a_xl * (low_x if i == 0 else 1.0)
            c["cxu"][own] = scale * a_xu
            c["cyl"][own] = scale * a_yl * keep_y
            c["cyu"][own] = scale * a_yu
            c["czl"][own] = scale * a_zl * keep_z
            c["czu"][own] = scale * a_zu

    def stencil(level, ref, low, high, emit):
        block = B0
        lane = lanes(block.Y)
        get = lambda k: getattr(s, f"{k}{level}")
        for i in range(block.X):
            own = block.own(i)
            v = ref[block.at(i)]
            down = jnp.where(lane == 0, turn(low, -i), turn(v, 1))
            up = jnp.where(lane == block.Z - 1, turn(high, block.Z - 1 - i), turn(v, -1))
            t_x = get("cxl")[own] * ref[block.at(i - 1)] + get("cxu")[own] * ref[block.at(i + 1)]
            t_y = get("cyl")[own] * ref[block.at(i, -1)] + get("cyu")[own] * ref[block.at(i, 1)]
            t_z = get("czl")[own] * down + get("czu")[own] * up
            emit(i, v, get("g")[own] + (t_x + t_y + t_z))

    def smooth(level, source, target, low, high):
        block = B0

        def emit(i, v, total):
            target[block.at(i)] = v * THIRD + total

        stencil(level, source, low, high, emit)

    def residual(level, source, low, high):
        block = B0
        d15, r = getattr(s, f"d15{level}"), getattr(s, f"r{level}")

        def emit(i, v, total):
            r[block.own(i)] = d15[block.own(i)] * (total - RELAX * v)

        stencil(level, source, low, high, emit)


    lane8, lane16 = lanes(8), lanes(16)
    row8, row16 = sublanes(8), sublanes(16)
    upper_half = row8 < 4
    slices_x = {1: (5, 3), -1: (0, 3), 0: (0, 8)}
    pairs_x = {1: (2, 2), -1: (0, 2), 0: (0, 4)}
    flat_yr = [(x, y) for x in (1, -1, 0) for y in (1, -1)]
    flat_zr = [(x, y, z) for x in (1, -1, 0) for y in (1, -1, 0) for z in (1, -1)]

    def send_around():
        zeds = [jnp.zeros((8, 128), F32)] * 2
        group = lane8 // 3
        for a in range(5):
            for x in range(8):
                v, place = s.hw_own[a, x], 8 * a + x
                zeds = [
                    jnp.where(group == place, turn(v, 3 * place - first), zed)
                    for zed, first in zip(zeds, (61, 0))
                ]
        s.hw_zed[0], s.hw_zed[1] = zeds
        for t in range(3):
            tiles = []
            for x in range(8):
                v = s.hw_own[2 * t, x]
                if t < 2:
                    v = jnp.where(lane8 < 64, v, turn(s.hw_own[2 * t + 1, x], 64))
                s.hw_pack[t, x] = v
                tiles.append(v)
            for i in range(4):
                even, odd = tiles[2 * i], tiles[2 * i + 1]
                s.hw_low[t, i] = jnp.where(upper_half, even, turn(odd, 4, 0))
                s.hw_high[t, i] = jnp.where(upper_half, turn(even, 4, 0), odd)

        def source(k):
            x, y, z = AROUND[k]
            if z != 0:
                return s.hw_zed.at[0 if z > 0 else 1]
            if y != 0:
                return (s.hw_low if y < 0 else s.hw_high).at[:, pl.ds(*pairs_x[x])]
            return s.hw_pack.at[:, pl.ds(*slices_x[x])]

        def target(k):
            x, y, z = AROUND[k]
            if z != 0:
                return s.hw_zr.at[flat_zr.index((x, y, z))]
            if y != 0:
                return s.hw_yr.at[flat_yr.index((x, y)), :, pl.ds(0, pairs_x[x][1])]
            return s.hw_xr.at[0 if x > 0 else 1]

        return copies(AROUND, source, target, s.hw_ss, s.hw_rs)

    def assemble(a, k):
        x = k - 4
        if x < 0:
            d, layer, first = 1, x + 8, 5
        elif x < 8:
            d, layer, first = 0, x, 0
        else:
            d, layer, first = -1, x - 8, 0
        place = 3 * (8 * a + layer)
        t = a // 2
        inner = s.hw_own[a, layer] if d == 0 else s.hw_xr[0 if d > 0 else 1, t, layer - first]
        pair = layer // 2 - pairs_x[d][0]
        above = s.hw_yr[flat_yr.index((d, -1)), t, pair]
        below = s.hw_yr[flat_yr.index((d, 1)), t, pair]
        if layer % 2 == 0:
            below = turn(below, 4, 0)
        else:
            above = turn(above, 4, 0)
        outer = jnp.where(upper_half, above, below)
        if a % 2 == 1:
            outer = turn(outer, 64)
            inner = inner if d == 0 else turn(inner, 64)
        whole = jnp.concatenate([inner, outer], axis=0)

        def side(z):
            zed = lambda y: s.hw_zr[flat_zr.index((d, y, z))]
            outer = jnp.where(upper_half, zed(-1), zed(1))
            return jnp.concatenate([zed(0), outer], axis=0)

        whole = jnp.where((lane16 >= 64) & (lane16 < 72), turn(side(-1), 64 - place), whole)
        return jnp.where(lane16 >= 120, turn(side(1), 125 - place), whole)

    def ext1(k):
        return pl.ds(16 * k, 16)

    def pad1(k):
        return pl.ds(16 * k + 16, 16)

    def coefficients1(first, last):
        keep_y = jnp.where(row16 == 0, low_y, 1.0)
        keep_z = jnp.where(lane16 == 0, low_z, 1.0)
        last_y = jnp.where(row16 == 7, top_y, 1.0)
        last_z = jnp.where(lane16 == 63, top_z, 1.0)
        for k in range(first, last + 1):
            own = ext1(k)
            a_xl, a_yl, a_zl = s.ext1[0, own], s.ext1[1, own], s.ext1[2, own]
            a_xu = s.ext1[0, ext1(k + 1)]
            if k == 11:
                a_xu = a_xu * top_x
            a_yu = turn(a_yl, -1, 0) * last_y
            a_zu = turn(a_zl, -1) * last_z
            total = (a_xl + a_yl + a_zl) + (a_xu + a_yu + a_zu)
            scale = RELAX / total
            s.kw1[own] = scale * 4.0
            s.d151[own] = (1.5 * 0.25) * total
            s.cxl1[own] = scale * a_xl * (low_x if k == 4 else 1.0)
            s.cxu1[own] = scale * a_xu
            s.cyl1[own] = scale * a_yl * keep_y
            s.cyu1[own] = scale * a_yu
            s.czl1[own] = scale * a_zl * keep_z
            s.czu1[own] = scale * a_zu

    def send_faces1(ref, key):
        snd, rcv = getattr(s, key + "_snd"), getattr(s, key + "_rcv")
        inner = lambda i: ref[pl.ds(16 * (i + 5), 8)]
        snd[0] = inner(7)
        snd[1] = inner(0)
        snd[2] = ref[pl.ds(16 * 5 + 7, 8, stride=16)]
        snd[3] = ref[pl.ds(16 * 5, 8, stride=16)]
        snd[4] = pack(inner, 8, 8, 63)
        snd[5] = pack(inner, 8, 8, 0)
        return copies(
            FACES,
            lambda k: snd.at[k],
            lambda k: rcv.at[k],
            getattr(s, key + "_ss"),
            getattr(s, key + "_rs"),
        )

    def fill1(ref, halo):
        low, high = halo[4], halo[5]
        for i in range(8):
            own = pl.ds(16 * (i + 5), 8)
            v = jnp.where(lane8 == 64, turn(high, 64 - i), ref[own])
            ref[own] = jnp.where(lane8 == 127, turn(low, 127 - i), v)
        ref[pl.ds(16 * 4, 8)] = halo[0]
        ref[pl.ds(16 * 13, 8)] = halo[1]
        ref[pl.ds(16 * 5 + 15, 8, stride=16)] = halo[2]
        ref[pl.ds(16 * 5 + 8, 8, stride=16)] = halo[3]

    def stencil1(first, last, ref, emit):
        for k in range(first, last + 1):
            own = ext1(k)
            v = ref[pad1(k)]
            t_x = s.cxl1[own] * ref[pad1(k - 1)] + s.cxu1[own] * ref[pad1(k + 1)]
            t_y = s.cyl1[own] * turn(v, 1, 0) + s.cyu1[own] * turn(v, -1, 0)
            t_z = s.czl1[own] * turn(v, 1) + s.czu1[own] * turn(v, -1)
            emit(k, v, s.g1[own] + (t_x + t_y + t_z))

    def smooth1(first, last, source, target):
        def emit(k, v, total):
            target[pad1(k)] = v * THIRD + total

        stencil1(first, last, source, emit)

    even8 = (2 * lane8) & 127
    half16 = lane16 >> 1

    def pair_z(value):
        return value + turn(value, -1)

    def stage_z(arrays, snd):
        group = lane16 >> 4
        packed = jnp.zeros((16, 128), F32)
        for a in range(arrays):
            whole = s.t16[a]
            for p in range(2):
                moved = take(whole, 4 * (lane16 & 15) + 2 * p)
                packed = jnp.where(group == ((gz + 2 * a + p) & 7), moved, packed)
        snd[...] = packed

    def merge_z(arrays, own, others, target):
        group = lane16 >> 4
        parts = [(0, own)] + [(RING_Z[k][2], others(k)) for k in range(7)]
        for q in range(2 * arrays):
            merged = jnp.zeros((16, 128), F32)
            for distance, part in parts:
                merged = jnp.where(group == ((gz - distance + q) & 7), part, merged)
            target[q] = turn(merged, -16 * q)

    for load in loads[:3]:
        load.wait()
    round_a0 = send_upper(s.fx, s.fy, s.fz, "a0")

    for i in range(8):
        own = pl.ds(8 * i, 8)
        here = lambda ref, shift: ref[pl.ds(32 * i + shift, 8, stride=2)]
        s.fx1[own] = take(pair_z(here(s.fx, 0) + here(s.fx, 1)), even8) * 0.25
        s.fy1[own] = take(pair_z(here(s.fy, 0) + here(s.fy, 16)), even8) * 0.25
        total = (here(s.fz, 0) + here(s.fz, 1)) + (here(s.fz, 16) + here(s.fz, 17))
        s.fz1[own] = take(total, even8) * 0.25
    s.a1_snd[0] = s.fx1[pl.ds(0, 8)]
    s.a1_snd[1] = s.fy1[pl.ds(0, 8, stride=8)]
    s.a1_snd[2] = pack(lambda i: s.fz1[pl.ds(8 * i, 8)], 8, 8, 0)
    round_a1 = copies(
        DOWN, lambda k: s.a1_snd.at[k], lambda k: s.a1_rcv.at[k], s.a1_ss, s.a1_rs
    )
    for i in range(4):
        own = pl.ds(4 * i, 4)
        here = lambda ref, shift: ref[pl.ds(16 * i + shift, 4, stride=2)]
        s.t16[0, own] = here(s.fx1, 0) + here(s.fx1, 1)
        s.t16[1, own] = here(s.fy1, 0) + here(s.fy1, 8)
        total = (here(s.fz1, 0) + here(s.fz1, 1)) + (here(s.fz1, 8) + here(s.fz1, 9))
        s.t16[2, own] = total * 0.25
    s.t16[0] = pair_z(s.t16[0]) * 0.25
    s.t16[1] = pair_z(s.t16[1]) * 0.25
    stage_z(3, s.zf_snd.at[0, 0])
    round_nf = copies(
        SIDES, lambda k: s.zf_snd.at[0, 0], lambda k: s.zf_snd.at[0, k + 1], s.nf_ss, s.nf_rs
    )
    for ref in (s.va1, s.vb1):
        for k in (-1, 17):
            ref[pad1(k)] = jnp.zeros((16, 128), F32)
    for p in range(2):
        for x in range(16):
            for ref in (s.lx2, s.ly2, s.lz2):
                ref[p, x + 2, pl.ds(8, 8)] = jnp.ones((8, 128), F32)
        for x in (0, 1, 18, 19):
            for ref in (s.va2, s.vb2):
                ref[p, x] = jnp.zeros((16, 128), F32)
        for x in range(16):
            s.f2[p, x + 2] = jnp.zeros((16, 128), F32)
    for ref in (s.va3, s.vb3):
        for k in range(2):
            ref[pl.ds(8 * k, 8)] = jnp.zeros((8, 128), F32)
            ref[pl.ds(144 + 8 * k, 8)] = jnp.zeros((8, 128), F32)
    s.p2[...] = jnp.zeros_like(s.p2)
    s.ext1[...] = jnp.ones_like(s.ext1)
    for k in (0, 1, 2, 3, 12, 13, 14, 15):
        s.va1[pad1(k)] = jnp.zeros((16, 128), F32)
        s.vb1[pad1(k)] = jnp.zeros((16, 128), F32)

    loads[3].wait()
    finish(round_a0)
    coefficients(0, s.fx, s.fy, s.fz, "a0")
    for i in range(16):
        own = B0.own(i)
        start = s.kw0[own] * s.rhs[own]
        s.g0[own] = start
        s.va0[B0.at(i)] = start
    round_b = send_faces(B0, s.va0, "b")
    finish(round_a1)
    for i in range(8):
        own, here = pl.ds(8 * i, 8), pl.ds(16 * (i + 4), 8)
        s.ext1[0, here] = s.fx1[own]
        s.ext1[1, here] = s.fy1[own]
        upper = turn(s.a1_rcv[2], 64 - i)
        s.ext1[2, here] = jnp.where(lane8 == 64, upper, s.fz1[own])
        s.hw_own[0, i] = s.fx1[own]
        s.hw_own[1, i] = s.fy1[own]
        s.hw_own[2, i] = s.fz1[own]
    s.ext1[0, pl.ds(16 * 12, 8)] = s.a1_rcv[0]
    s.ext1[1, pl.ds(16 * 4 + 8, 8, stride=16)] = s.a1_rcv[1]
    coefficients1(4, 11)
    finish(round_b)
    finish(round_nf)
    round_xf = copies(
        LINE, lambda k: s.zf_snd.at[0], lambda k: s.zf_snd.at[k + 1], s.xf_ss, s.xf_rs
    )
    fill(B0, s.va0, s.b_rcv)
    smooth(0, s.va0, s.vb0, s.b_rcv[4], s.b_rcv[5])
    round_c = send_faces(B0, s.vb0, "c")
    finish(round_c)
    fill(B0, s.vb0, s.c_rcv)
    residual(0, s.vb0, s.c_rcv[4], s.c_rcv[5])

    for i in range(8):
        here = lambda shift: s.r0[pl.ds(32 * i + shift, 8, stride=2)]
        total = (here(0) + here(1)) + (here(16) + here(17))
        forcing = take(pair_z(total), even8) * 0.125
        s.hw_own[3, i] = forcing
        start = s.kw1[pl.ds(16 * (i + 4), 8)] * forcing
        s.g1[pl.ds(16 * (i + 4), 8)] = start
        s.g1[pl.ds(16 * (i + 4) + 8, 8)] = jnp.zeros((8, 128), F32)
        s.va1[pl.ds(16 * (i + 5), 8)] = start
        s.va1[pl.ds(16 * (i + 5) + 8, 8)] = jnp.zeros((8, 128), F32)
    round_d = send_faces1(s.va1, "d")
    finish(round_xf)
    round_zf = copies(
        RING_Z, lambda k: s.zf_snd, lambda k: s.zf_rcv.at[k], s.zf_ss, s.zf_rs
    )
    finish(round_d)
    fill1(s.va1, s.d_rcv)
    smooth1(4, 11, s.va1, s.vb1)
    for i in range(8):
        s.hw_own[4, i] = s.vb1[pl.ds(16 * (i + 5), 8)]
    round_e = send_faces1(s.vb1, "e")


    def block2(p, x):
        return (p, x + 2)

    def spread(arrays, offsets, snd, rcv, targets):
        parts = [((0, 0, 0), lambda q: snd.at[q])]
        for k, offset in enumerate(offsets):
            parts.append((offset, lambda q, k=k: rcv.at[k, q]))
        for offset, part in parts:
            first = 4 * ((gx - offset[0]) & 3)
            place = pl.ds(4 * (1 - offset[1]), 4)
            for a in range(arrays):
                for p in range(2):
                    for x in range(4):
                        piece = part(2 * a + p)[pl.ds(4 * x, 4)]
                        targets[a][p, x + 2 + first, place] = piece

    def send_sides(refs, key):
        snd, rcv = getattr(s, key + "_snd"), getattr(s, key + "_rcv")
        for a, ref in enumerate(refs):
            for p in range(2):
                for i in range(8):
                    even = ref[p, 2 * i + 2, pl.ds(0, 8)]
                    odd = ref[p, 2 * i + 3, pl.ds(0, 8)]
                    snd[a, p, i] = jnp.where(upper_half, turn(even, 4, 0), odd)
        return copies(
            SIDES,
            lambda k: snd,
            lambda k: rcv.at[k],
            getattr(s, key + "_ss"),
            getattr(s, key + "_rs"),
        )

    def take_sides(refs, key, rest):
        rcv = getattr(s, key + "_rcv")
        for a, ref in enumerate(refs):
            for p in range(2):
                for x in range(16):
                    below, above = rcv[0, a, p, x // 2], rcv[1, a, p, x // 2]
                    if x % 2 == 1:
                        below, above = turn(below, 4, 0), turn(above, 4, 0)
                    own = ref[p, x + 2, pl.ds(0, 8)]
                    ref[p, x + 2, pl.ds(0, 8)] = jnp.where(upper_half, below, own)
                    ref[p, x + 2, pl.ds(8, 8)] = jnp.where(upper_half, above, rest)

    faces2 = (s.lx2, s.ly2, s.lz2)
    global_y = row16 + 4 * gy - 4
    not_low, not_top = global_y != 0, global_y != 4 * GY - 1

    finish(round_e)
    fill1(s.vb1, s.e_rcv)

    def emit_r1(k, v, total):
        r = s.d151[ext1(k)] * (total - RELAX * v)
        s.r1[pl.ds(8 * (k - 4), 8)] = r[0:8]

    stencil1(4, 11, s.vb1, emit_r1)
    for i in range(4):
        here = lambda shift: s.r1[pl.ds(16 * i + shift, 4, stride=2)]
        s.t16[0, pl.ds(4 * i, 4)] = (here(0) + here(1)) + (here(8) + here(9))
    s.t16[0] = pair_z(s.t16[0]) * 0.125
    stage_z(1, s.zr_snd)
    round_zr = copies(
        RING_Z, lambda k: s.zr_snd, lambda k: s.zr_rcv.at[k], s.zr_ss, s.zr_rs
    )


    mine = pl.ds(pl.multiple_of(16 * gy, 16), 16)
    round_hw = send_around()

    def stencil2(ref, emit):
        for p in range(2):
            for x in range(16):
                j, other = block2(p, x), block2(1 - p, x)
                v, w = ref[j], ref[other]
                t_x = s.cxl2[j] * ref[block2(p, x - 1)] + s.cxu2[j] * ref[block2(p, x + 1)]
                t_y = s.cyl2[j] * turn(v, 1, 0) + s.cyu2[j] * turn(v, -1, 0)
                down, up = (turn(w, 1), w) if p == 0 else (w, turn(w, -1))
                t_z = s.czl2[j] * down + s.czu2[j] * up
                emit(j, v, s.g2[j] + (t_x + t_y + t_z))

    def smooth2(source, target):
        def emit(j, v, total):
            target[j] = v * THIRD + total

        stencil2(source, emit)

    finish(round_zr)
    merge_z(1, s.zr_snd[...], lambda k: s.zr_rcv[k], s.xr_snd)
    round_xr = copies(
        PLANE, lambda k: s.xr_snd, lambda k: s.xr_rcv.at[k], s.xr_ss, s.xr_rs
    )

    finish(round_zf)
    for line in range(4):
        first = 4 * ((gx - ((0, 0, 0), *LINE)[line][0]) & 3)
        for side in range(3):
            place = pl.ds((4, 0, 8)[side], 4)
            merge_z(3, s.zf_snd[line, side], lambda k: s.zf_rcv[k, line, side], s.m2)
            for a in range(3):
                for p in range(2):
                    for x in range(4):
                        piece = s.m2[2 * a + p, pl.ds(4 * x, 4)]
                        faces2[a][p, x + 2 + first, place] = piece
    for a, ref in enumerate((s.lx2, s.ly2, s.lz2)):
        for i in range(8):
            total = ref[block2(0, 2 * i)]
            if a != 2:
                total = total + ref[block2(1, 2 * i)]
            if a != 0:
                total = total + ref[block2(0, 2 * i + 1)]
            if a == 1:
                total = total + ref[block2(1, 2 * i + 1)]
            s.s2[pl.ds(16 * i, 16)] = total
        for j in range(2):
            total = s.s2[pl.ds(4 + 2 * j, 8, stride=16)]
            if a != 1:
                total = total + s.s2[pl.ds(5 + 2 * j, 8, stride=16)]
            s.face3[a, pl.ds(pl.multiple_of(16 * gy + 8 * j, 8), 8)] = total * 0.25
    round_yf = copies(
        RING_Y,
        lambda k: s.face3.at[:, mine],
        lambda k: s.face3.at[:, mine],
        s.yf_ss,
        s.yf_rs,
    )
    for p in range(2):
        for x in range(16):
            j = block2(p, x)
            a_xl, a_yl, a_zl = s.lx2[j], s.ly2[j], s.lz2[j]
            a_xu = s.lx2[block2(p, x + 1)] if x < 15 else jnp.zeros((16, 128), F32)
            a_yu = jnp.where(not_top, turn(a_yl, -1, 0), 0.0)
            if p == 0:
                a_zu = s.lz2[block2(1, x)]
            else:
                a_zu = jnp.where(lane16 == 127, 0.0, turn(s.lz2[block2(0, x)], -1))
            total = (a_xl + a_yl + a_zl) + (a_xu + a_yu + a_zu)
            scale = RELAX / total
            s.d152[j] = (1.5 * 0.0625) * total
            s.kw2[j] = scale * 16.0
            s.cxl2[j] = scale * a_xl if x > 0 else jnp.zeros((16, 128), F32)
            s.cxu2[j] = scale * a_xu
            s.cyl2[j] = jnp.where(not_low, scale * a_yl, 0.0)
            s.cyu2[j] = scale * a_yu
            s.czl2[j] = scale * a_zl if p == 1 else jnp.where(lane16 == 0, 0.0, scale * a_zl)
            s.czu2[j] = scale * a_zu

    finish(round_xr)
    spread(1, PLANE, s.xr_snd, s.xr_rcv, (s.f2,))
    for p in range(2):
        for x in range(16):
            j = block2(p, x)
            start = s.kw2[j] * s.f2[j]
            s.g2[j] = start
            s.va2[j] = start
    smooth2(s.va2, s.vb2)

    def emit_r2(j, v, total):
        s.f2[j] = s.d152[j] * (total - RELAX * v)

    stencil2(s.vb2, emit_r2)
    for i in range(8):
        total = (s.f2[block2(0, 2 * i)] + s.f2[block2(1, 2 * i)]) + (
            s.f2[block2(0, 2 * i + 1)] + s.f2[block2(1, 2 * i + 1)]
        )
        s.s2[pl.ds(16 * i, 16)] = total
    for j in range(2):
        total = s.s2[pl.ds(4 + 2 * j, 8, stride=16)] + s.s2[pl.ds(5 + 2 * j, 8, stride=16)]
        s.f3[pl.ds(pl.multiple_of(16 * gy + 8 * j, 8), 8)] = total * 0.125
    round_yr = copies(
        RING_Y, lambda k: s.f3.at[mine], lambda k: s.f3.at[mine], s.yr_ss, s.yr_rs
    )
    round_nv = send_sides((s.vb2,), "nv")

    finish(round_yf)
    zero8 = jnp.zeros((8, 128), F32)
    for y in range(16):
        own = pl.ds(8 * y, 8)
        a_xl, a_yl, a_zl = s.face3[0, own], s.face3[1, own], s.face3[2, own]
        a_xu = jnp.where(row8 == 7, 0.0, turn(a_xl, -1, 0))
        a_yu = s.face3[1, pl.ds(8 * y + 8, 8)] if y < 15 else zero8
        a_zu = jnp.where(lane8 == 127, 0.0, turn(a_zl, -1))
        total = (a_xl + a_yl + a_zl) + (a_xu + a_yu + a_zu)
        scale = RELAX / total
        s.d153[own] = (1.5 * 0.25**3) * total
        s.kw3[own] = scale * 64.0
        s.cxl3[own] = jnp.where(row8 == 0, 0.0, scale * a_xl)
        s.cxu3[own] = scale * a_xu
        s.cyl3[own] = scale * a_yl if y > 0 else zero8
        s.cyu3[own] = scale * a_yu
        s.czl3[own] = jnp.where(lane8 == 0, 0.0, scale * a_zl)
        s.czu3[own] = scale * a_zu

    lane32, row32 = lanes(32), sublanes(32)

    def both(value, lane, step):
        return value + jnp.where(
            (lane & step) == 0, turn(value, -step), turn(value, step)
        )

    def lower_of(value, lane, step):
        return jnp.where((lane & step) == 0, value, turn(value, step))

    for a in range(3):
        for y in range(8):
            here = lambda shift: s.face3[a, pl.ds(16 * y + shift, 4, stride=2)]
            if a == 0:
                total = here(0) + here(8)
            elif a == 1:
                total = here(0) + here(1)
            else:
                total = (here(0) + here(1)) + (here(8) + here(9))
            s.t4[pl.ds(4 * y, 4)] = total
        total = s.t4[...]
        total = both(total, lane32, 1) if a < 2 else lower_of(total, lane32, 1)
        s.fc4[a] = total * 0.25
    a_xl, a_yl, a_zl = s.fc4[0], s.fc4[1], s.fc4[2]
    a_xu = jnp.where((row32 & 3) == 3, 0.0, turn(a_xl, -1, 0))
    a_yu = jnp.where(row32 >= 28, 0.0, turn(a_yl, -4, 0))
    a_zu = jnp.where(lane32 >= 126, 0.0, turn(a_zl, -2))
    total = (a_xl + a_yl + a_zl) + (a_xu + a_yu + a_zu)
    scale = RELAX / total
    s.d154[...] = (1.5 * 0.25**4) * total
    s.kw4[...] = scale * 256.0
    s.cxl4[...] = jnp.where((row32 & 3) == 0, 0.0, scale * a_xl)
    s.cxu4[...] = scale * a_xu
    s.cyl4[...] = jnp.where(row32 < 4, 0.0, scale * a_yl)
    s.cyu4[...] = scale * a_yu
    s.czl4[...] = jnp.where(lane32 < 2, 0.0, scale * a_zl)
    s.czu4[...] = scale * a_zu

    faces5 = []
    for a in range(3):
        for x in range(2):
            here = lambda shift: s.fc4[a, pl.ds(2 * x + shift, 4, stride=8)]
            if a == 0:
                total = here(0) + here(4)
            elif a == 1:
                total = here(0) + here(1)
            else:
                total = (here(0) + here(1)) + (here(4) + here(5))
            s.t5[pl.ds(4 * x, 4)] = total
        total = s.t5[...]
        total = both(total, lane8, 2) if a < 2 else lower_of(total, lane8, 2)
        faces5.append(total * 0.25)
    a_xl, a_yl, a_zl = faces5
    a_xu = jnp.where(row8 >= 4, 0.0, turn(a_xl, 4, 0))
    a_yu = jnp.where((row8 & 3) == 3, 0.0, turn(a_yl, -1, 0))
    a_zu = jnp.where(lane8 >= 124, 0.0, turn(a_zl, -4))
    total = (a_xl + a_yl + a_zl) + (a_xu + a_yu + a_zu)
    scale = RELAX / total
    s.kw5[...] = scale * 1024.0
    s.cx5[...] = jnp.where(row8 >= 4, scale * a_xl, scale * a_xu)
    s.cyl5[...] = jnp.where((row8 & 3) == 0, 0.0, scale * a_yl)
    s.cyu5[...] = scale * a_yu
    s.czl5[...] = jnp.where(lane8 < 4, 0.0, scale * a_zl)
    s.czu5[...] = scale * a_zu

    finish(round_hw)
    for k in range(1, 15):
        for a in range(4):
            s.ext1[a, ext1(k)] = assemble(a, k)
        s.vb1[pad1(k)] = assemble(4, k)
    coefficients1(2, 13)
    for k in range(2, 14):
        s.g1[ext1(k)] = s.kw1[ext1(k)] * s.ext1[3, ext1(k)]
    finish(round_yr)

    def at3(y):
        return pl.ds(16 + 8 * y, 8)

    def stencil3(ref, emit):
        for y in range(16):
            own = pl.ds(8 * y, 8)
            v = ref[at3(y)]
            t_x = s.cxl3[own] * turn(v, 1, 0) + s.cxu3[own] * turn(v, -1, 0)
            t_y = s.cyl3[own] * ref[at3(y - 1)] + s.cyu3[own] * ref[at3(y + 1)]
            t_z = s.czl3[own] * turn(v, 1) + s.czu3[own] * turn(v, -1)
            emit(y, v, s.g3[own] + (t_x + t_y + t_z))

    def smooth3(source, target):
        def emit(y, v, total):
            target[at3(y)] = v * THIRD + total

        stencil3(source, emit)

    for y in range(16):
        own = pl.ds(8 * y, 8)
        start = s.kw3[own] * s.f3[own]
        s.g3[own] = start
        s.va3[at3(y)] = start
    smooth3(s.va3, s.vb3)

    def emit_r3(y, v, total):
        own = pl.ds(8 * y, 8)
        s.r3[own] = s.d153[own] * (total - RELAX * v)

    stencil3(s.vb3, emit_r3)
    for y in range(8):
        here = lambda shift: s.r3[pl.ds(16 * y + shift, 4, stride=2)]
        s.t4[pl.ds(4 * y, 4)] = (here(0) + here(1)) + (here(8) + here(9))
    f4 = both(s.t4[...], lane32, 1) * 0.125

    def total4(v):
        t_x = s.cxl4[...] * turn(v, 1, 0) + s.cxu4[...] * turn(v, -1, 0)
        t_y = s.cyl4[...] * turn(v, 4, 0) + s.cyu4[...] * turn(v, -4, 0)
        t_z = s.czl4[...] * turn(v, 2) + s.czu4[...] * turn(v, -2)
        return g4 + (t_x + t_y + t_z)

    g4 = s.kw4[...] * f4
    v4 = g4
    v4 = v4 * THIRD + total4(v4)
    s.r4[...] = s.d154[...] * (total4(v4) - RELAX * v4)
    for x in range(2):
        here = lambda shift: s.r4[pl.ds(2 * x + shift, 4, stride=8)]
        s.t5[pl.ds(4 * x, 4)] = (here(0) + here(1)) + (here(4) + here(5))
    g5 = s.kw5[...] * (both(s.t5[...], lane8, 2) * 0.125)
    cx5, cyl5, cyu5, czl5, czu5 = s.cx5[...], s.cyl5[...], s.cyu5[...], s.czl5[...], s.czu5[...]

    def sweep5(index, v):
        t_y = cyl5 * turn(v, 1, 0) + cyu5 * turn(v, -1, 0)
        t_z = czl5 * turn(v, 4) + czu5 * turn(v, -4)
        return (v * THIRD + g5) + (cx5 * turn(v, 4, 0) + (t_y + t_z))

    s.e5[...] = lax.fori_loop(0, COARSE_SWEEPS - 1, sweep5, g5)
    for x in range(2):
        piece = s.e5[pl.ds(4 * x, 4)]
        for shift in (0, 1, 4, 5):
            s.p4[pl.ds(2 * x + shift, 4, stride=8)] = piece
    v4 = v4 + s.p4[...]
    v4 = v4 * THIRD + total4(v4)
    v4 = v4 * THIRD + total4(v4)
    s.r4[...] = v4
    for x in range(4):
        piece = s.r4[pl.ds(x, 8, stride=4)]
        for shift in (0, 1, 8, 9):
            s.p3[pl.ds(2 * x + shift, 8, stride=16)] = piece
    for y in range(16):
        s.vb3[at3(y)] = s.vb3[at3(y)] + s.p3[pl.ds(8 * y, 8)]
    smooth3(s.vb3, s.va3)
    smooth3(s.va3, s.vb3)

    finish(round_nv)
    take_sides((s.vb2,), "nv", 0.0)
    for k in range(6):
        piece = s.vb3[pl.ds(pl.multiple_of(16 * gy + 8 * k, 8), 8)]
        for x in range(2):
            for y in range(2):
                s.p2[pl.ds(16 * x + 2 * k + y, 8, stride=32)] = piece
    for x in range(16):
        more = s.p2[pl.ds(16 * x, 16)]
        for p in range(2):
            s.vb2[block2(p, x)] = s.vb2[block2(p, x)] + more
    smooth2(s.vb2, s.va2)
    smooth2(s.va2, s.vb2)

    signed = jnp.where(lane16 < 96, lane16, lane16 - 128)
    index = (16 * gz + (signed >> 2)) & 127
    odd = ((signed >> 1) & 1) == 1
    for k in range(8):
        x = 4 * gx + k
        piece = jnp.where(odd, take(s.vb2[1, x], index), take(s.vb2[0, x], index))
        rows = jnp.where(row16 < 6, turn(piece, -4, 0), turn(piece, 4, 0))[0:8]
        for y in range(2):
            s.q1[pl.ds(16 * k + y, 8, stride=2)] = rows
        more = s.q1[pl.ds(16 * k, 16)]
        for i in (2 * k, 2 * k + 1):
            if 1 <= i <= 14:
                s.vb1[pad1(i)] = s.vb1[pad1(i)] + more
    smooth1(2, 13, s.vb1, s.va1)
    smooth1(3, 12, s.va1, s.vb1)
    s.h1[0] = s.vb1[pl.ds(16 * 4, 8)]
    s.h1[1] = s.vb1[pl.ds(16 * 13, 8)]
    s.h1[2] = s.vb1[pl.ds(16 * 5 + 15, 8, stride=16)]
    s.h1[3] = s.vb1[pl.ds(16 * 5 + 8, 8, stride=16)]
    inner = lambda i: s.vb1[pl.ds(16 * (i + 5), 8)]
    s.h1[4] = pack(inner, 8, 8, 127)
    s.h1[5] = pack(inner, 8, 8, 64)

    def widen(value, ref, start):
        ref[pl.ds(start, 8, stride=2)] = value
        ref[pl.ds(start + 1, 8, stride=2)] = value
        return take(ref[pl.ds(start, 16)], half16)

    for i in range(8):
        more = widen(inner(i), s.w0, 16 * i)
        for x in (2 * i, 2 * i + 1):
            s.vb0[B0.at(x)] = s.vb0[B0.at(x)] + more
    for k in range(6):
        s.c_rcv[k] = s.c_rcv[k] + widen(s.h1[k], s.w0, 128 + 16 * k)
    fill(B0, s.vb0, s.c_rcv)
    smooth(0, s.vb0, s.va0, s.c_rcv[4], s.c_rcv[5])
    round_h = send_faces(B0, s.va0, "h")
    finish(round_h)
    fill(B0, s.va0, s.h_rcv)

    def emit_out(i, v, total):
        out[B0.own(i)] = v * THIRD + total

    stencil(0, s.va0, s.h_rcv[4], s.h_rcv[5], emit_out)


def shards(rhs, face_x, face_y, face_z):
    flat = [a.reshape(256, 128) for a in (rhs, face_x, face_y, face_z)]
    whole = pl.pallas_call(
        cycle,
        out_shape=jax.ShapeDtypeStruct((256, 128), F32),
        in_specs=[pl.BlockSpec(memory_space=pltpu.HBM)] * 4,
        out_specs=pl.BlockSpec(memory_space=pltpu.VMEM),
        scratch_shapes=list(SCRATCH.values()),
        compiler_params=pltpu.CompilerParams(
            collective_id=0, has_side_effects=True, vmem_limit_bytes=64 * 1024 * 1024
        ),
        name="vcycle",
    )(*flat)
    return whole.reshape(16, 16, 128)


def solution(mesh):
    placed = P("gx", "gy", "gz")
    return jax.shard_map(
        shards, mesh=mesh, in_specs=(placed,) * 4, out_specs=placed, check_vma=False
    )
```

```python
import jax
import jax.numpy as jnp
from jax import lax
from jax.experimental import pallas as pl
from jax.experimental.pallas import tpu as pltpu
from jax.sharding import PartitionSpec as P

RELAX = 2.0 / 3.0
THIRD = 1.0 / 3.0
COARSE_SWEEPS = 24
GX, GY, GZ = 4, 8, 8
F32 = jnp.float32
MESH = pl.DeviceIdType.MESH

FACES = [(1, 0, 0), (-1, 0, 0), (0, 1, 0), (0, -1, 0), (0, 0, 1), (0, 0, -1)]
DOWN = [(-1, 0, 0), (0, -1, 0), (0, 0, -1)]
RING_Z = [(0, 0, k) for k in (4, 3, 5, 2, 6, 1, 7)]
RING_Y = [(0, k, 0) for k in (4, 3, 5, 2, 6, 1, 7)]
AROUND = [
    (x, y, z) for x in (1, -1, 0) for y in (1, -1, 0) for z in (1, -1, 0) if (x, y, z) != (0, 0, 0)
]
AROUND.sort(key=lambda d: -(abs(d[0]) + abs(d[1]) + abs(d[2])))
LINE = [(2, 0, 0), (1, 0, 0), (3, 0, 0)]
SIDES = [(0, 1, 0), (0, -1, 0)]
PLANE = [(2, 1, 0), (2, -1, 0), (1, 1, 0), (1, -1, 0), (3, 1, 0), (3, -1, 0)]
PLANE += [(2, 0, 0), (0, 1, 0), (0, -1, 0), (1, 0, 0), (3, 0, 0)]


def lanes(rows):
    return lax.broadcasted_iota(jnp.int32, (rows, 128), 1)


def sublanes(rows):
    return lax.broadcasted_iota(jnp.int32, (rows, 128), 0)


def turn(value, steps, axis=1):
    steps %= value.shape[axis]
    return value if steps == 0 else pltpu.roll(value, steps, axis)


def take(value, index):
    return jnp.take_along_axis(value, index, axis=1, mode="promise_in_bounds")


class Block:
    def __init__(self, size_x, size_y, size_z, weight):
        self.X, self.Y, self.Z, self.weight = size_x, size_y, size_z, weight
        self.pitch = size_y + 8
        self.rows = size_x * size_y
        self.padded = 8 + (size_x + 2) * self.pitch

    def base(self, i):
        return 8 + (i + 1) * self.pitch

    def own(self, i):
        return pl.ds(i * self.Y, self.Y)

    def at(self, i, shift=0):
        return pl.ds(self.base(i) + shift, self.Y)

    def row_of_each(self, y):
        return pl.ds(self.base(0) + y, self.X, stride=self.pitch)


B0 = Block(16, 16, 128, 1.0)

SCRATCH = {}


def vmem(name, *shape):
    SCRATCH[name] = pltpu.VMEM(shape, F32)


def dma(name, *shape):
    SCRATCH[name] = pltpu.SemaphoreType.DMA(shape)


for key in ("rhs", "fx", "fy", "fz"):
    vmem(key, 256, 128)
dma("in_sem", 5)
for key in ("cxl0", "cxu0", "cyl0", "cyu0", "czl0", "czu0", "g0", "d150", "kw0", "r0", "w0"):
    vmem(key, 256, 128)
vmem("va0", B0.padded, 128)
vmem("vb0", B0.padded, 128)
vmem("lyp0", B0.X * B0.pitch, 128)
for key in ("fx1", "fy1", "fz1", "r1"):
    vmem(key, 64, 128)
for key in ("cxl1", "cxu1", "cyl1", "cyu1", "czl1", "czu1", "g1", "d151", "kw1"):
    vmem(key, 17 * 16, 128)
for key in ("va1", "vb1"):
    vmem(key, 19 * 16, 128)
vmem("ext1", 4, 17 * 16, 128)
vmem("hw_own", 5, 8, 8, 128)
vmem("hw_pack", 3, 8, 8, 128)
vmem("hw_low", 3, 4, 8, 128)
vmem("hw_high", 3, 4, 8, 128)
vmem("hw_zed", 2, 8, 128)
vmem("hw_xr", 2, 3, 3, 8, 128)
vmem("hw_yr", 6, 3, 4, 8, 128)
vmem("hw_zr", 18, 8, 128)
dma("hw_ss", 26)
dma("hw_rs", 26)
vmem("q1", 8 * 16, 128)
for key, rows, count in (("a0", 16, 3), ("b", 16, 6), ("c", 16, 6), ("a1", 8, 3), ("d", 8, 6), ("e", 8, 6)):
    vmem(f"{key}_snd", count, rows, 128)
    vmem(f"{key}_rcv", count, rows, 128)
    dma(f"{key}_ss", count)
    dma(f"{key}_rs", count)
vmem("t0", 256, 128)
vmem("hh_snd", 6, 7, 16, 128)
vmem("hh_rcv", 6, 7, 16, 128)
dma("hh_ss", 6)
dma("hh_rs", 6)
vmem("side1", 6, 16, 128)
vmem("wide1", 6, 4, 16, 128)
vmem("t16", 3, 16, 128)
vmem("zf_snd", 3, 16, 128)
vmem("zf_rcv", 7, 3, 16, 128)
vmem("xf_snd", 3, 6, 16, 128)
vmem("xf_rcv", 3, 3, 6, 16, 128)
vmem("zr_snd", 16, 128)
vmem("zr_rcv", 7, 16, 128)
vmem("xr_snd", 2, 16, 128)
vmem("xr_rcv", 11, 2, 16, 128)
for key, count in (("zf", 7), ("zr", 7), ("xr", 11), ("xf", 3), ("nf", 2)):
    dma(f"{key}_ss", count)
    dma(f"{key}_rs", count)
for key in ("f2", "lx2", "ly2", "lz2", "va2", "vb2"):
    vmem(key, 2, 20, 16, 128)
for key in ("cxl2", "cxu2", "cyl2", "cyu2", "czl2", "czu2", "g2", "d152", "kw2"):
    vmem(key, 2, 20, 16, 128)
vmem("nv_snd", 1, 2, 8, 8, 128)
vmem("nv_rcv", 2, 1, 2, 8, 8, 128)
dma("nv_ss", 2)
dma("nv_rs", 2)
vmem("s2", 128, 128)
vmem("p2", 256, 128)
vmem("face3", 3, 128, 128)
vmem("f3", 128, 128)
for key in ("yf", "yr"):
    dma(f"{key}_ss", 7)
    dma(f"{key}_rs", 7)
for key in ("cxl3", "cxu3", "cyl3", "cyu3", "czl3", "czu3", "g3", "d153", "kw3", "r3", "p3"):
    vmem(key, 128, 128)
vmem("va3", 160, 128)
vmem("vb3", 160, 128)
for key in ("t4", "cxl4", "cxu4", "cyl4", "cyu4", "czl4", "czu4", "d154", "kw4", "r4", "p4"):
    vmem(key, 32, 128)
vmem("fc4", 3, 32, 128)
for key in ("t5", "cx5", "cyl5", "cyu5", "czl5", "czu5", "kw5", "e5"):
    vmem(key, 8, 128)


class Space:
    pass


def cycle(rhs_in, fx_in, fy_in, fz_in, out, *scratch):
    s = Space()
    for name, ref in zip(SCRATCH, scratch):
        setattr(s, name, ref)
    gx, gy, gz = lax.axis_index("gx"), lax.axis_index("gy"), lax.axis_index("gz")

    def peer(offset):
        return (
            (gx + offset[0]) & (GX - 1),
            (gy + offset[1]) & (GY - 1),
            (gz + offset[2]) & (GZ - 1),
        )

    loads = [
        pltpu.make_async_copy(source, target, s.in_sem.at[k])
        for k, (source, target) in enumerate(
            ((fx_in, s.fx), (fy_in, s.fy), (fz_in, s.fz), (rhs_in, s.rhs))
        )
    ]
    for load in loads:
        load.start()

    barrier = pltpu.get_barrier_semaphore()
    for offset in FACES:
        pl.semaphore_signal(barrier, inc=1, device_id=peer(offset), device_id_type=MESH)

    def copies(offsets, sources, targets, ss, rs):
        made = [
            pltpu.make_async_remote_copy(
                src_ref=sources(k),
                dst_ref=targets(k),
                send_sem=ss.at[k],
                recv_sem=rs.at[k],
                device_id=peer(offset),
                device_id_type=MESH,
            )
            for k, offset in enumerate(offsets)
        ]
        for one in made:
            one.start()
        return made

    def finish(made):
        for one in made:
            one.wait_recv()
        for one in made:
            one.wait_send()

    def flag(condition):
        return jnp.where(condition, 1.0, 0.0).astype(F32)

    low_x, low_y, low_z = flag(gx > 0), flag(gy > 0), flag(gz > 0)
    top_x, top_y, top_z = flag(gx < GX - 1), flag(gy < GY - 1), flag(gz < GZ - 1)


    def pack(read, rows, count, column):
        packed = jnp.zeros((rows, 128), F32)
        lane = lanes(rows)
        for i in range(count):
            packed = jnp.where(lane == i, turn(read(i), i - column), packed)
        return packed

    def send_faces(block, ref, key):
        snd = getattr(s, key + "_snd")
        snd[0] = ref[block.at(block.X - 1)]
        snd[1] = ref[block.at(0)]
        snd[2] = ref[block.row_of_each(block.Y - 1)]
        snd[3] = ref[block.row_of_each(0)]
        snd[4] = pack(lambda i: ref[block.at(i)], 16, 16, 127)
        snd[5] = pack(lambda i: ref[block.at(i)], 16, 16, 0)
        rcv = getattr(s, key + "_rcv")
        return copies(
            FACES,
            lambda k: snd.at[k],
            lambda k: rcv.at[k],
            getattr(s, key + "_ss"),
            getattr(s, key + "_rs"),
        )

    def fill(block, ref, halo):
        ref[block.at(-1)] = halo[0]
        ref[block.at(block.X)] = halo[1]
        ref[block.row_of_each(-1)] = halo[2]
        ref[block.row_of_each(block.Y)] = halo[3]

    def send_upper(lx, ly, lz, key):
        block = B0
        snd = getattr(s, key + "_snd")
        snd[0] = lx[block.own(0)]
        snd[1] = ly[pl.ds(0, block.X, stride=block.Y)]
        snd[2] = pack(lambda i: lz[block.own(i)], 16, 16, 0)
        rcv = getattr(s, key + "_rcv")
        pl.semaphore_wait(barrier, len(FACES))
        return copies(
            DOWN,
            lambda k: snd.at[k],
            lambda k: rcv.at[k],
            getattr(s, key + "_ss"),
            getattr(s, key + "_rs"),
        )

    def coefficients(level, lx, ly, lz, key):
        block = B0
        rcv = getattr(s, key + "_rcv")
        lyp = getattr(s, f"lyp{level}")
        c = {k: getattr(s, f"{k}{level}") for k in ("cxl", "cxu", "cyl", "cyu", "czl", "czu")}
        d15, kw = getattr(s, f"d15{level}"), getattr(s, f"kw{level}")
        for i in range(block.X):
            lyp[pl.ds(i * block.pitch, block.Y)] = ly[block.own(i)]
        lyp[pl.ds(block.Y, block.X, stride=block.pitch)] = rcv[1] * top_y
        next_x = rcv[0] * top_x
        next_z = rcv[2] * top_z
        lane, row = lanes(block.Y), sublanes(block.Y)
        keep_y = jnp.where(row == 0, low_y, 1.0)
        keep_z = jnp.where(lane == 0, low_z, 1.0)
        for i in range(block.X):
            own = block.own(i)
            a_xl = lx[own]
            a_xu = lx[block.own(i + 1)] if i + 1 < block.X else next_x
            a_yl = ly[own]
            a_yu = lyp[pl.ds(i * block.pitch + 1, block.Y)]
            a_zl = lz[own]
            a_zu = jnp.where(
                lane == block.Z - 1, turn(next_z, block.Z - 1 - i), turn(a_zl, -1)
            )
            total = (a_xl + a_yl + a_zl) + (a_xu + a_yu + a_zu)
            scale = RELAX / total
            d15[own] = (1.5 * block.weight) * total
            kw[own] = scale * (1.0 / block.weight)
            c["cxl"][own] = scale * a_xl * (low_x if i == 0 else 1.0)
            c["cxu"][own] = scale * a_xu
            c["cyl"][own] = scale * a_yl * keep_y
            c["cyu"][own] = scale * a_yu
            c["czl"][own] = scale * a_zl * keep_z
            c["czu"][own] = scale * a_zu

    def stencil(level, ref, low, high, emit):
        block = B0
        lane = lanes(block.Y)
        get = lambda k: getattr(s, f"{k}{level}")
        for i in range(block.X):
            own = block.own(i)
            v = ref[block.at(i)]
            down = jnp.where(lane == 0, turn(low, -i), turn(v, 1))
            up = jnp.where(lane == block.Z - 1, turn(high, block.Z - 1 - i), turn(v, -1))
            t_x = get("cxl")[own] * ref[block.at(i - 1)] + get("cxu")[own] * ref[block.at(i + 1)]
            t_y = get("cyl")[own] * ref[block.at(i, -1)] + get("cyu")[own] * ref[block.at(i, 1)]
            t_z = get("czl")[own] * down + get("czu")[own] * up
            emit(i, v, get("g")[own] + (t_x + t_y + t_z))

    def smooth(level, source, target, low, high):
        block = B0

        def emit(i, v, total):
            target[block.at(i)] = v * THIRD + total

        stencil(level, source, low, high, emit)

    def residual(level, source, low, high):
        block = B0
        d15, r = getattr(s, f"d15{level}"), getattr(s, f"r{level}")

        def emit(i, v, total):
            r[block.own(i)] = d15[block.own(i)] * (total - RELAX * v)
            s.t0[block.own(i)] = v * THIRD + total

        stencil(level, source, low, high, emit)


    lane8, lane16 = lanes(8), lanes(16)
    row8, row16 = sublanes(8), sublanes(16)
    upper_half = row8 < 4
    slices_x = {1: (5, 3), -1: (0, 3), 0: (0, 8)}
    pairs_x = {1: (2, 2), -1: (0, 2), 0: (0, 4)}
    flat_yr = [(x, y) for x in (1, -1, 0) for y in (1, -1)]
    flat_zr = [(x, y, z) for x in (1, -1, 0) for y in (1, -1, 0) for z in (1, -1)]

    def pack_around():
        zeds = [jnp.zeros((8, 128), F32)] * 2
        group = lane8 // 3
        for a in range(5):
            for x in range(8):
                v, place = s.hw_own[a, x], 8 * a + x
                zeds = [
                    jnp.where(group == place, turn(v, 3 * place - first), zed)
                    for zed, first in zip(zeds, (61, 0))
                ]
        s.hw_zed[0], s.hw_zed[1] = zeds
        for t in range(3):
            tiles = []
            for x in range(8):
                v = s.hw_own[2 * t, x]
                if t < 2:
                    v = jnp.where(lane8 < 64, v, turn(s.hw_own[2 * t + 1, x], 64))
                s.hw_pack[t, x] = v
                tiles.append(v)
            for i in range(4):
                even, odd = tiles[2 * i], tiles[2 * i + 1]
                s.hw_low[t, i] = jnp.where(upper_half, even, turn(odd, 4, 0))
                s.hw_high[t, i] = jnp.where(upper_half, turn(even, 4, 0), odd)

    def send_around():
        def source(k):
            x, y, z = AROUND[k]
            if z != 0:
                return s.hw_zed.at[0 if z > 0 else 1]
            if y != 0:
                return (s.hw_low if y < 0 else s.hw_high).at[:, pl.ds(*pairs_x[x])]
            return s.hw_pack.at[:, pl.ds(*slices_x[x])]

        def target(k):
            x, y, z = AROUND[k]
            if z != 0:
                return s.hw_zr.at[flat_zr.index((x, y, z))]
            if y != 0:
                return s.hw_yr.at[flat_yr.index((x, y)), :, pl.ds(0, pairs_x[x][1])]
            return s.hw_xr.at[0 if x > 0 else 1]

        return copies(AROUND, source, target, s.hw_ss, s.hw_rs)

    def assemble(a, k):
        x = k - 4
        if x < 0:
            d, layer, first = 1, x + 8, 5
        elif x < 8:
            d, layer, first = 0, x, 0
        else:
            d, layer, first = -1, x - 8, 0
        place = 3 * (8 * a + layer)
        t = a // 2
        inner = s.hw_own[a, layer] if d == 0 else s.hw_xr[0 if d > 0 else 1, t, layer - first]
        pair = layer // 2 - pairs_x[d][0]
        above = s.hw_yr[flat_yr.index((d, -1)), t, pair]
        below = s.hw_yr[flat_yr.index((d, 1)), t, pair]
        if layer % 2 == 0:
            below = turn(below, 4, 0)
        else:
            above = turn(above, 4, 0)
        outer = jnp.where(upper_half, above, below)
        if a % 2 == 1:
            outer = turn(outer, 64)
            inner = inner if d == 0 else turn(inner, 64)
        whole = jnp.concatenate([inner, outer], axis=0)

        def side(z):
            zed = lambda y: s.hw_zr[flat_zr.index((d, y, z))]
            outer = jnp.where(upper_half, zed(-1), zed(1))
            return jnp.concatenate([zed(0), outer], axis=0)

        whole = jnp.where((lane16 >= 64) & (lane16 < 72), turn(side(-1), 64 - place), whole)
        return jnp.where(lane16 >= 120, turn(side(1), 125 - place), whole)

    def ext1(k):
        return pl.ds(16 * k, 16)

    def pad1(k):
        return pl.ds(16 * k + 16, 16)

    def coefficients1(first, last):
        keep_y = jnp.where(row16 == 0, low_y, 1.0)
        keep_z = jnp.where(lane16 == 0, low_z, 1.0)
        last_y = jnp.where(row16 == 7, top_y, 1.0)
        last_z = jnp.where(lane16 == 63, top_z, 1.0)
        for k in range(first, last + 1):
            own = ext1(k)
            a_xl, a_yl, a_zl = s.ext1[0, own], s.ext1[1, own], s.ext1[2, own]
            a_xu = s.ext1[0, ext1(k + 1)]
            if k == 11:
                a_xu = a_xu * top_x
            a_yu = turn(a_yl, -1, 0) * last_y
            a_zu = turn(a_zl, -1) * last_z
            total = (a_xl + a_yl + a_zl) + (a_xu + a_yu + a_zu)
            scale = RELAX / total
            s.kw1[own] = scale * 4.0
            s.d151[own] = (1.5 * 0.25) * total
            s.cxl1[own] = scale * a_xl * (low_x if k == 4 else 1.0)
            s.cxu1[own] = scale * a_xu
            s.cyl1[own] = scale * a_yl * keep_y
            s.cyu1[own] = scale * a_yu
            s.czl1[own] = scale * a_zl * keep_z
            s.czu1[own] = scale * a_zu

    def send_faces1(ref, key):
        snd, rcv = getattr(s, key + "_snd"), getattr(s, key + "_rcv")
        inner = lambda i: ref[pl.ds(16 * (i + 5), 8)]
        snd[0] = inner(7)
        snd[1] = inner(0)
        snd[2] = ref[pl.ds(16 * 5 + 7, 8, stride=16)]
        snd[3] = ref[pl.ds(16 * 5, 8, stride=16)]
        snd[4] = pack(inner, 8, 8, 63)
        snd[5] = pack(inner, 8, 8, 0)
        return copies(
            FACES,
            lambda k: snd.at[k],
            lambda k: rcv.at[k],
            getattr(s, key + "_ss"),
            getattr(s, key + "_rs"),
        )

    def fill1(ref, halo):
        low, high = halo[4], halo[5]
        for i in range(8):
            own = pl.ds(16 * (i + 5), 8)
            v = jnp.where(lane8 == 64, turn(high, 64 - i), ref[own])
            ref[own] = jnp.where(lane8 == 127, turn(low, 127 - i), v)
        ref[pl.ds(16 * 4, 8)] = halo[0]
        ref[pl.ds(16 * 13, 8)] = halo[1]
        ref[pl.ds(16 * 5 + 15, 8, stride=16)] = halo[2]
        ref[pl.ds(16 * 5 + 8, 8, stride=16)] = halo[3]

    def stencil1(first, last, ref, emit):
        for k in range(first, last + 1):
            own = ext1(k)
            v = ref[pad1(k)]
            t_x = s.cxl1[own] * ref[pad1(k - 1)] + s.cxu1[own] * ref[pad1(k + 1)]
            t_y = s.cyl1[own] * turn(v, 1, 0) + s.cyu1[own] * turn(v, -1, 0)
            t_z = s.czl1[own] * turn(v, 1) + s.czu1[own] * turn(v, -1)
            emit(k, v, s.g1[own] + (t_x + t_y + t_z))

    def smooth1(first, last, source, target):
        def emit(k, v, total):
            target[pad1(k)] = v * THIRD + total

        stencil1(first, last, source, emit)

    even8 = (2 * lane8) & 127
    half16 = lane16 >> 1

    def pair_z(value):
        return value + turn(value, -1)

    def stage_z(arrays, snd):
        group = lane16 >> 4
        packed = jnp.zeros((16, 128), F32)
        for a in range(arrays):
            whole = s.t16[a]
            for p in range(2):
                moved = take(whole, 4 * (lane16 & 15) + 2 * p)
                packed = jnp.where(group == ((gz + 2 * a + p) & 7), moved, packed)
        snd[...] = packed

    def merge_z(arrays, own, others, target):
        group = lane16 >> 4
        parts = [(0, own)] + [(RING_Z[k][2], others(k)) for k in range(7)]
        for q in range(2 * arrays):
            merged = jnp.zeros((16, 128), F32)
            for distance, part in parts:
                merged = jnp.where(group == ((gz - distance + q) & 7), part, merged)
            target[q] = turn(merged, -16 * q)

    for load in loads[:3]:
        load.wait()
    round_a0 = send_upper(s.fx, s.fy, s.fz, "a0")

    for i in range(8):
        own = pl.ds(8 * i, 8)
        here = lambda ref, shift: ref[pl.ds(32 * i + shift, 8, stride=2)]
        s.fx1[own] = take(pair_z(here(s.fx, 0) + here(s.fx, 1)), even8) * 0.25
        s.fy1[own] = take(pair_z(here(s.fy, 0) + here(s.fy, 16)), even8) * 0.25
        total = (here(s.fz, 0) + here(s.fz, 1)) + (here(s.fz, 16) + here(s.fz, 17))
        s.fz1[own] = take(total, even8) * 0.25
    s.a1_snd[0] = s.fx1[pl.ds(0, 8)]
    s.a1_snd[1] = s.fy1[pl.ds(0, 8, stride=8)]
    s.a1_snd[2] = pack(lambda i: s.fz1[pl.ds(8 * i, 8)], 8, 8, 0)
    round_a1 = copies(
        DOWN, lambda k: s.a1_snd.at[k], lambda k: s.a1_rcv.at[k], s.a1_ss, s.a1_rs
    )
    for i in range(4):
        own = pl.ds(4 * i, 4)
        here = lambda ref, shift: ref[pl.ds(16 * i + shift, 4, stride=2)]
        s.t16[0, own] = here(s.fx1, 0) + here(s.fx1, 1)
        s.t16[1, own] = here(s.fy1, 0) + here(s.fy1, 8)
        total = (here(s.fz1, 0) + here(s.fz1, 1)) + (here(s.fz1, 8) + here(s.fz1, 9))
        s.t16[2, own] = total * 0.25
    s.t16[0] = pair_z(s.t16[0]) * 0.25
    s.t16[1] = pair_z(s.t16[1]) * 0.25
    stage_z(3, s.zf_snd.at[0])
    round_nf = copies(
        SIDES, lambda k: s.zf_snd.at[0], lambda k: s.zf_snd.at[k + 1], s.nf_ss, s.nf_rs
    )
    for ref in (s.va1, s.vb1):
        for k in (-1, 17):
            ref[pad1(k)] = jnp.zeros((16, 128), F32)
    for p in range(2):
        for x in range(16):
            for ref in (s.lx2, s.ly2, s.lz2):
                ref[p, x + 2, pl.ds(8, 8)] = jnp.ones((8, 128), F32)
        for x in (0, 1, 18, 19):
            for ref in (s.va2, s.vb2):
                ref[p, x] = jnp.zeros((16, 128), F32)
        for x in range(16):
            s.f2[p, x + 2] = jnp.zeros((16, 128), F32)
    for ref in (s.va3, s.vb3):
        for k in range(2):
            ref[pl.ds(8 * k, 8)] = jnp.zeros((8, 128), F32)
            ref[pl.ds(144 + 8 * k, 8)] = jnp.zeros((8, 128), F32)
    s.p2[...] = jnp.zeros_like(s.p2)
    s.ext1[...] = jnp.ones_like(s.ext1)
    for k in (0, 1, 2, 3, 12, 13, 14, 15):
        s.va1[pad1(k)] = jnp.zeros((16, 128), F32)
        s.vb1[pad1(k)] = jnp.zeros((16, 128), F32)

    loads[3].wait()
    finish(round_a0)
    coefficients(0, s.fx, s.fy, s.fz, "a0")
    for i in range(16):
        own = B0.own(i)
        start = s.kw0[own] * s.rhs[own]
        s.g0[own] = start
        s.va0[B0.at(i)] = start
    round_b = send_faces(B0, s.va0, "b")
    finish(round_a1)
    for i in range(8):
        own, here = pl.ds(8 * i, 8), pl.ds(16 * (i + 4), 8)
        s.ext1[0, here] = s.fx1[own]
        s.ext1[1, here] = s.fy1[own]
        upper = turn(s.a1_rcv[2], 64 - i)
        s.ext1[2, here] = jnp.where(lane8 == 64, upper, s.fz1[own])
        s.hw_own[0, i] = s.fx1[own]
        s.hw_own[1, i] = s.fy1[own]
        s.hw_own[2, i] = s.fz1[own]
    s.ext1[0, pl.ds(16 * 12, 8)] = s.a1_rcv[0]
    s.ext1[1, pl.ds(16 * 4 + 8, 8, stride=16)] = s.a1_rcv[1]
    coefficients1(4, 11)
    finish(round_b)
    fill(B0, s.va0, s.b_rcv)
    smooth(0, s.va0, s.vb0, s.b_rcv[4], s.b_rcv[5])
    round_c = send_faces(B0, s.vb0, "c")
    finish(round_c)
    fill(B0, s.vb0, s.c_rcv)
    residual(0, s.vb0, s.c_rcv[4], s.c_rcv[5])

    for i in range(8):
        here = lambda shift: s.r0[pl.ds(32 * i + shift, 8, stride=2)]
        total = (here(0) + here(1)) + (here(16) + here(17))
        forcing = take(pair_z(total), even8) * 0.125
        s.hw_own[3, i] = forcing
        start = s.kw1[pl.ds(16 * (i + 4), 8)] * forcing
        s.g1[pl.ds(16 * (i + 4), 8)] = start
        s.g1[pl.ds(16 * (i + 4) + 8, 8)] = jnp.zeros((8, 128), F32)
        s.va1[pl.ds(16 * (i + 5), 8)] = start
        s.va1[pl.ds(16 * (i + 5) + 8, 8)] = jnp.zeros((8, 128), F32)
    round_d = send_faces1(s.va1, "d")
    finish(round_nf)
    round_zf = copies(
        RING_Z, lambda k: s.zf_snd, lambda k: s.zf_rcv.at[k], s.zf_ss, s.zf_rs
    )
    kept = (s.t0, s.cxl0, s.cxu0, s.cyl0, s.cyu0, s.czl0, s.czu0)
    for a, ref in enumerate(kept):
        s.hh_snd[0, a] = ref[B0.own(15)]
        s.hh_snd[1, a] = ref[B0.own(0)]
        s.hh_snd[2, a] = ref[pl.ds(15, 16, stride=16)]
        s.hh_snd[3, a] = ref[pl.ds(0, 16, stride=16)]
        s.hh_snd[4, a] = pack(lambda i: ref[B0.own(i)], 16, 16, 127)
        s.hh_snd[5, a] = pack(lambda i: ref[B0.own(i)], 16, 16, 0)
    finish(round_d)
    fill1(s.va1, s.d_rcv)
    smooth1(4, 11, s.va1, s.vb1)
    for i in range(8):
        s.hw_own[4, i] = s.vb1[pl.ds(16 * (i + 5), 8)]
    round_e = send_faces1(s.vb1, "e")
    finish(round_zf)
    for side in range(3):
        merge_z(3, s.zf_snd[side], lambda k: s.zf_rcv[k, side], s.xf_snd.at[side])
    round_xf = copies(
        LINE, lambda k: s.xf_snd, lambda k: s.xf_rcv.at[k], s.xf_ss, s.xf_rs
    )
    pack_around()


    def block2(p, x):
        return (p, x + 2)

    def spread(arrays, offsets, snd, rcv, targets):
        parts = [((0, 0, 0), lambda q: snd.at[q])]
        for k, offset in enumerate(offsets):
            parts.append((offset, lambda q, k=k: rcv.at[k, q]))
        for offset, part in parts:
            first = 4 * ((gx - offset[0]) & 3)
            place = pl.ds(4 * (1 - offset[1]), 4)
            for a in range(arrays):
                for p in range(2):
                    for x in range(4):
                        piece = part(2 * a + p)[pl.ds(4 * x, 4)]
                        targets[a][p, x + 2 + first, place] = piece

    def send_sides(refs, key):
        snd, rcv = getattr(s, key + "_snd"), getattr(s, key + "_rcv")
        for a, ref in enumerate(refs):
            for p in range(2):
                for i in range(8):
                    even = ref[p, 2 * i + 2, pl.ds(0, 8)]
                    odd = ref[p, 2 * i + 3, pl.ds(0, 8)]
                    snd[a, p, i] = jnp.where(upper_half, turn(even, 4, 0), odd)
        return copies(
            SIDES,
            lambda k: snd,
            lambda k: rcv.at[k],
            getattr(s, key + "_ss"),
            getattr(s, key + "_rs"),
        )

    def take_sides(refs, key, rest):
        rcv = getattr(s, key + "_rcv")
        for a, ref in enumerate(refs):
            for p in range(2):
                for x in range(16):
                    below, above = rcv[0, a, p, x // 2], rcv[1, a, p, x // 2]
                    if x % 2 == 1:
                        below, above = turn(below, 4, 0), turn(above, 4, 0)
                    own = ref[p, x + 2, pl.ds(0, 8)]
                    ref[p, x + 2, pl.ds(0, 8)] = jnp.where(upper_half, below, own)
                    ref[p, x + 2, pl.ds(8, 8)] = jnp.where(upper_half, above, rest)

    faces2 = (s.lx2, s.ly2, s.lz2)
    global_y = row16 + 4 * gy - 4
    not_low, not_top = global_y != 0, global_y != 4 * GY - 1

    finish(round_e)
    fill1(s.vb1, s.e_rcv)

    def emit_r1(k, v, total):
        r = s.d151[ext1(k)] * (total - RELAX * v)
        s.r1[pl.ds(8 * (k - 4), 8)] = r[0:8]

    stencil1(4, 11, s.vb1, emit_r1)
    for i in range(4):
        here = lambda shift: s.r1[pl.ds(16 * i + shift, 4, stride=2)]
        s.t16[0, pl.ds(4 * i, 4)] = (here(0) + here(1)) + (here(8) + here(9))
    s.t16[0] = pair_z(s.t16[0]) * 0.125
    stage_z(1, s.zr_snd)
    round_zr = copies(
        RING_Z, lambda k: s.zr_snd, lambda k: s.zr_rcv.at[k], s.zr_ss, s.zr_rs
    )


    mine = pl.ds(pl.multiple_of(16 * gy, 16), 16)

    def stencil2(ref, emit):
        for p in range(2):
            for x in range(16):
                j, other = block2(p, x), block2(1 - p, x)
                v, w = ref[j], ref[other]
                t_x = s.cxl2[j] * ref[block2(p, x - 1)] + s.cxu2[j] * ref[block2(p, x + 1)]
                t_y = s.cyl2[j] * turn(v, 1, 0) + s.cyu2[j] * turn(v, -1, 0)
                down, up = (turn(w, 1), w) if p == 0 else (w, turn(w, -1))
                t_z = s.czl2[j] * down + s.czu2[j] * up
                emit(j, v, s.g2[j] + (t_x + t_y + t_z))

    def smooth2(source, target):
        def emit(j, v, total):
            target[j] = v * THIRD + total

        stencil2(source, emit)

    finish(round_zr)
    merge_z(1, s.zr_snd[...], lambda k: s.zr_rcv[k], s.xr_snd)
    round_xr = copies(
        PLANE, lambda k: s.xr_snd, lambda k: s.xr_rcv.at[k], s.xr_ss, s.xr_rs
    )

    round_hw = send_around()
    finish(round_xf)
    for line in range(4):
        first = 4 * ((gx - ((0, 0, 0), *LINE)[line][0]) & 3)
        for side in range(3):
            part = s.xf_snd.at[side] if line == 0 else s.xf_rcv.at[line - 1, side]
            place = pl.ds((4, 0, 8)[side], 4)
            for a in range(3):
                for p in range(2):
                    for x in range(4):
                        piece = part[2 * a + p, pl.ds(4 * x, 4)]
                        faces2[a][p, x + 2 + first, place] = piece
    for a, ref in enumerate((s.lx2, s.ly2, s.lz2)):
        for i in range(8):
            total = ref[block2(0, 2 * i)]
            if a != 2:
                total = total + ref[block2(1, 2 * i)]
            if a != 0:
                total = total + ref[block2(0, 2 * i + 1)]
            if a == 1:
                total = total + ref[block2(1, 2 * i + 1)]
            s.s2[pl.ds(16 * i, 16)] = total
        for j in range(2):
            total = s.s2[pl.ds(4 + 2 * j, 8, stride=16)]
            if a != 1:
                total = total + s.s2[pl.ds(5 + 2 * j, 8, stride=16)]
            s.face3[a, pl.ds(pl.multiple_of(16 * gy + 8 * j, 8), 8)] = total * 0.25
    round_yf = copies(
        RING_Y,
        lambda k: s.face3.at[:, mine],
        lambda k: s.face3.at[:, mine],
        s.yf_ss,
        s.yf_rs,
    )
    for p in range(2):
        for x in range(16):
            j = block2(p, x)
            a_xl, a_yl, a_zl = s.lx2[j], s.ly2[j], s.lz2[j]
            a_xu = s.lx2[block2(p, x + 1)] if x < 15 else jnp.zeros((16, 128), F32)
            a_yu = jnp.where(not_top, turn(a_yl, -1, 0), 0.0)
            if p == 0:
                a_zu = s.lz2[block2(1, x)]
            else:
                a_zu = jnp.where(lane16 == 127, 0.0, turn(s.lz2[block2(0, x)], -1))
            total = (a_xl + a_yl + a_zl) + (a_xu + a_yu + a_zu)
            scale = RELAX / total
            s.d152[j] = (1.5 * 0.0625) * total
            s.kw2[j] = scale * 16.0
            s.cxl2[j] = scale * a_xl if x > 0 else jnp.zeros((16, 128), F32)
            s.cxu2[j] = scale * a_xu
            s.cyl2[j] = jnp.where(not_low, scale * a_yl, 0.0)
            s.cyu2[j] = scale * a_yu
            s.czl2[j] = scale * a_zl if p == 1 else jnp.where(lane16 == 0, 0.0, scale * a_zl)
            s.czu2[j] = scale * a_zu

    finish(round_xr)
    spread(1, PLANE, s.xr_snd, s.xr_rcv, (s.f2,))
    for p in range(2):
        for x in range(16):
            j = block2(p, x)
            start = s.kw2[j] * s.f2[j]
            s.g2[j] = start
            s.va2[j] = start
    smooth2(s.va2, s.vb2)

    def emit_r2(j, v, total):
        s.f2[j] = s.d152[j] * (total - RELAX * v)

    stencil2(s.vb2, emit_r2)
    for i in range(8):
        total = (s.f2[block2(0, 2 * i)] + s.f2[block2(1, 2 * i)]) + (
            s.f2[block2(0, 2 * i + 1)] + s.f2[block2(1, 2 * i + 1)]
        )
        s.s2[pl.ds(16 * i, 16)] = total
    for j in range(2):
        total = s.s2[pl.ds(4 + 2 * j, 8, stride=16)] + s.s2[pl.ds(5 + 2 * j, 8, stride=16)]
        s.f3[pl.ds(pl.multiple_of(16 * gy + 8 * j, 8), 8)] = total * 0.125
    round_yr = copies(
        RING_Y, lambda k: s.f3.at[mine], lambda k: s.f3.at[mine], s.yr_ss, s.yr_rs
    )
    round_nv = send_sides((s.vb2,), "nv")
    round_hh = copies(
        FACES, lambda k: s.hh_snd.at[k], lambda k: s.hh_rcv.at[k], s.hh_ss, s.hh_rs
    )

    finish(round_yf)
    zero8 = jnp.zeros((8, 128), F32)
    for y in range(16):
        own = pl.ds(8 * y, 8)
        a_xl, a_yl, a_zl = s.face3[0, own], s.face3[1, own], s.face3[2, own]
        a_xu = jnp.where(row8 == 7, 0.0, turn(a_xl, -1, 0))
        a_yu = s.face3[1, pl.ds(8 * y + 8, 8)] if y < 15 else zero8
        a_zu = jnp.where(lane8 == 127, 0.0, turn(a_zl, -1))
        total = (a_xl + a_yl + a_zl) + (a_xu + a_yu + a_zu)
        scale = RELAX / total
        s.d153[own] = (1.5 * 0.25**3) * total
        s.kw3[own] = scale * 64.0
        s.cxl3[own] = jnp.where(row8 == 0, 0.0, scale * a_xl)
        s.cxu3[own] = scale * a_xu
        s.cyl3[own] = scale * a_yl if y > 0 else zero8
        s.cyu3[own] = scale * a_yu
        s.czl3[own] = jnp.where(lane8 == 0, 0.0, scale * a_zl)
        s.czu3[own] = scale * a_zu

    lane32, row32 = lanes(32), sublanes(32)

    def both(value, lane, step):
        return value + jnp.where(
            (lane & step) == 0, turn(value, -step), turn(value, step)
        )

    def lower_of(value, lane, step):
        return jnp.where((lane & step) == 0, value, turn(value, step))

    for a in range(3):
        for y in range(8):
            here = lambda shift: s.face3[a, pl.ds(16 * y + shift, 4, stride=2)]
            if a == 0:
                total = here(0) + here(8)
            elif a == 1:
                total = here(0) + here(1)
            else:
                total = (here(0) + here(1)) + (here(8) + here(9))
            s.t4[pl.ds(4 * y, 4)] = total
        total = s.t4[...]
        total = both(total, lane32, 1) if a < 2 else lower_of(total, lane32, 1)
        s.fc4[a] = total * 0.25
    a_xl, a_yl, a_zl = s.fc4[0], s.fc4[1], s.fc4[2]
    a_xu = jnp.where((row32 & 3) == 3, 0.0, turn(a_xl, -1, 0))
    a_yu = jnp.where(row32 >= 28, 0.0, turn(a_yl, -4, 0))
    a_zu = jnp.where(lane32 >= 126, 0.0, turn(a_zl, -2))
    total = (a_xl + a_yl + a_zl) + (a_xu + a_yu + a_zu)
    scale = RELAX / total
    s.d154[...] = (1.5 * 0.25**4) * total
    s.kw4[...] = scale * 256.0
    s.cxl4[...] = jnp.where((row32 & 3) == 0, 0.0, scale * a_xl)
    s.cxu4[...] = scale * a_xu
    s.cyl4[...] = jnp.where(row32 < 4, 0.0, scale * a_yl)
    s.cyu4[...] = scale * a_yu
    s.czl4[...] = jnp.where(lane32 < 2, 0.0, scale * a_zl)
    s.czu4[...] = scale * a_zu

    faces5 = []
    for a in range(3):
        for x in range(2):
            here = lambda shift: s.fc4[a, pl.ds(2 * x + shift, 4, stride=8)]
            if a == 0:
                total = here(0) + here(4)
            elif a == 1:
                total = here(0) + here(1)
            else:
                total = (here(0) + here(1)) + (here(4) + here(5))
            s.t5[pl.ds(4 * x, 4)] = total
        total = s.t5[...]
        total = both(total, lane8, 2) if a < 2 else lower_of(total, lane8, 2)
        faces5.append(total * 0.25)
    a_xl, a_yl, a_zl = faces5
    a_xu = jnp.where(row8 >= 4, 0.0, turn(a_xl, 4, 0))
    a_yu = jnp.where((row8 & 3) == 3, 0.0, turn(a_yl, -1, 0))
    a_zu = jnp.where(lane8 >= 124, 0.0, turn(a_zl, -4))
    total = (a_xl + a_yl + a_zl) + (a_xu + a_yu + a_zu)
    scale = RELAX / total
    s.kw5[...] = scale * 1024.0
    s.cx5[...] = jnp.where(row8 >= 4, scale * a_xl, scale * a_xu)
    s.cyl5[...] = jnp.where((row8 & 3) == 0, 0.0, scale * a_yl)
    s.cyu5[...] = scale * a_yu
    s.czl5[...] = jnp.where(lane8 < 4, 0.0, scale * a_zl)
    s.czu5[...] = scale * a_zu

    finish(round_hw)
    for k in range(1, 15):
        for a in range(4):
            s.ext1[a, ext1(k)] = assemble(a, k)
        s.vb1[pad1(k)] = assemble(4, k)
    coefficients1(2, 13)
    for k in range(2, 14):
        s.g1[ext1(k)] = s.kw1[ext1(k)] * s.ext1[3, ext1(k)]
    finish(round_yr)

    def at3(y):
        return pl.ds(16 + 8 * y, 8)

    def stencil3(ref, emit):
        for y in range(16):
            own = pl.ds(8 * y, 8)
            v = ref[at3(y)]
            t_x = s.cxl3[own] * turn(v, 1, 0) + s.cxu3[own] * turn(v, -1, 0)
            t_y = s.cyl3[own] * ref[at3(y - 1)] + s.cyu3[own] * ref[at3(y + 1)]
            t_z = s.czl3[own] * turn(v, 1) + s.czu3[own] * turn(v, -1)
            emit(y, v, s.g3[own] + (t_x + t_y + t_z))

    def smooth3(source, target):
        def emit(y, v, total):
            target[at3(y)] = v * THIRD + total

        stencil3(source, emit)

    for y in range(16):
        own = pl.ds(8 * y, 8)
        start = s.kw3[own] * s.f3[own]
        s.g3[own] = start
        s.va3[at3(y)] = start
    smooth3(s.va3, s.vb3)

    def emit_r3(y, v, total):
        own = pl.ds(8 * y, 8)
        s.r3[own] = s.d153[own] * (total - RELAX * v)

    stencil3(s.vb3, emit_r3)
    for y in range(8):
        here = lambda shift: s.r3[pl.ds(16 * y + shift, 4, stride=2)]
        s.t4[pl.ds(4 * y, 4)] = (here(0) + here(1)) + (here(8) + here(9))
    f4 = both(s.t4[...], lane32, 1) * 0.125

    def total4(v):
        t_x = s.cxl4[...] * turn(v, 1, 0) + s.cxu4[...] * turn(v, -1, 0)
        t_y = s.cyl4[...] * turn(v, 4, 0) + s.cyu4[...] * turn(v, -4, 0)
        t_z = s.czl4[...] * turn(v, 2) + s.czu4[...] * turn(v, -2)
        return g4 + (t_x + t_y + t_z)

    g4 = s.kw4[...] * f4
    v4 = g4
    v4 = v4 * THIRD + total4(v4)
    s.r4[...] = s.d154[...] * (total4(v4) - RELAX * v4)
    for x in range(2):
        here = lambda shift: s.r4[pl.ds(2 * x + shift, 4, stride=8)]
        s.t5[pl.ds(4 * x, 4)] = (here(0) + here(1)) + (here(4) + here(5))
    g5 = s.kw5[...] * (both(s.t5[...], lane8, 2) * 0.125)
    cx5, cyl5, cyu5, czl5, czu5 = s.cx5[...], s.cyl5[...], s.cyu5[...], s.czl5[...], s.czu5[...]

    def sweep5(index, v):
        t_y = cyl5 * turn(v, 1, 0) + cyu5 * turn(v, -1, 0)
        t_z = czl5 * turn(v, 4) + czu5 * turn(v, -4)
        return (v * THIRD + g5) + (cx5 * turn(v, 4, 0) + (t_y + t_z))

    s.e5[...] = lax.fori_loop(0, COARSE_SWEEPS - 1, sweep5, g5)
    for x in range(2):
        piece = s.e5[pl.ds(4 * x, 4)]
        for shift in (0, 1, 4, 5):
            s.p4[pl.ds(2 * x + shift, 4, stride=8)] = piece
    v4 = v4 + s.p4[...]
    v4 = v4 * THIRD + total4(v4)
    v4 = v4 * THIRD + total4(v4)
    s.r4[...] = v4
    for x in range(4):
        piece = s.r4[pl.ds(x, 8, stride=4)]
        for shift in (0, 1, 8, 9):
            s.p3[pl.ds(2 * x + shift, 8, stride=16)] = piece
    for y in range(16):
        s.vb3[at3(y)] = s.vb3[at3(y)] + s.p3[pl.ds(8 * y, 8)]
    smooth3(s.vb3, s.va3)
    smooth3(s.va3, s.vb3)

    finish(round_nv)
    take_sides((s.vb2,), "nv", 0.0)
    for k in range(6):
        piece = s.vb3[pl.ds(pl.multiple_of(16 * gy + 8 * k, 8), 8)]
        for x in range(2):
            for y in range(2):
                s.p2[pl.ds(16 * x + 2 * k + y, 8, stride=32)] = piece
    for x in range(16):
        more = s.p2[pl.ds(16 * x, 16)]
        for p in range(2):
            s.vb2[block2(p, x)] = s.vb2[block2(p, x)] + more
    smooth2(s.vb2, s.va2)
    smooth2(s.va2, s.vb2)

    signed = jnp.where(lane16 < 96, lane16, lane16 - 128)
    index = (16 * gz + (signed >> 2)) & 127
    odd = ((signed >> 1) & 1) == 1
    for k in range(8):
        x = 4 * gx + k
        piece = jnp.where(odd, take(s.vb2[1, x], index), take(s.vb2[0, x], index))
        rows = jnp.where(row16 < 6, turn(piece, -4, 0), turn(piece, 4, 0))[0:8]
        for y in range(2):
            s.q1[pl.ds(16 * k + y, 8, stride=2)] = rows
        more = s.q1[pl.ds(16 * k, 16)]
        for i in (2 * k, 2 * k + 1):
            if 1 <= i <= 14:
                s.vb1[pad1(i)] = s.vb1[pad1(i)] + more
    smooth1(2, 13, s.vb1, s.va1)
    smooth1(3, 12, s.va1, s.vb1)
    inner = lambda i: s.vb1[pl.ds(16 * (i + 5), 8)]

    def widen(value, ref, start):
        ref[pl.ds(start, 8, stride=2)] = value
        ref[pl.ds(start + 1, 8, stride=2)] = value
        return take(ref[pl.ds(start, 16)], half16)

    for i in range(8):
        more = widen(inner(i), s.w0, 16 * i)
        for x in (2 * i, 2 * i + 1):
            s.vb0[B0.at(x)] = s.vb0[B0.at(x)] + more

    sides = [s.vb1[pl.ds(16 * 4, 16)], s.vb1[pl.ds(16 * 13, 16)]]
    near = [inner(0), inner(7)]
    for k, row, edge in ((2, 15, 0), (3, 8, 7)):
        s.side1[k, pl.ds(8, 8)] = jnp.zeros((8, 128), F32)
        s.side1[k, pl.ds(0, 8)] = s.vb1[pl.ds(16 * 5 + row, 8, stride=16)]
        s.side1[k, pl.ds(8, 1)] = s.vb1[pl.ds(16 * 13 + row, 1)]
        s.side1[k, pl.ds(15, 1)] = s.vb1[pl.ds(16 * 4 + row, 1)]
        sides.append(s.side1[k])
        near.append(s.vb1[pl.ds(16 * 5 + edge, 8, stride=16)])
    for column, edge in ((127, 0), (64, 63)):
        packed = jnp.zeros((16, 128), F32)
        for k in range(3, 13):
            place = (k - 4) & 127
            packed = jnp.where(lane16 == place, turn(s.vb1[pad1(k)], place - column), packed)
        sides.append(packed)
        near.append(pack(inner, 8, 8, edge))

    def tall(value, ref):
        ref[pl.ds(0, 8, stride=2)] = value
        ref[pl.ds(1, 8, stride=2)] = value
        return ref[...]

    first_row, first_lane = (row16 & 1) == 0, (lane16 & 1) == 0
    layers = []
    finish(round_hh)
    for k in range(6):
        side = sides[k]
        rows = tall(side[0:8], s.wide1.at[k, 0])
        here = take(rows, half16)
        inside = take(tall(near[k], s.wide1.at[k, 1]), half16)
        before = take(tall(turn(side, 1, 0)[0:8], s.wide1.at[k, 2]), half16)
        after = take(tall(turn(side, -1, 0)[0:8], s.wide1.at[k, 3]), half16)
        row_low = jnp.where(first_row, before, here)
        row_high = jnp.where(first_row, here, after)
        lane_low = jnp.where(first_lane, take(turn(rows, 1), half16), here)
        lane_high = jnp.where(first_lane, here, take(turn(rows, -1), half16))
        axis = k // 2
        of_rows, of_lanes = ((1, 2), (0, 2), (1, 0))[axis]
        c = lambda d, upper: s.hh_rcv[k, 1 + 2 * d + upper]
        upper = 1 - k % 2
        total = s.hh_rcv[k, 0] + (THIRD + c(axis, 1 - upper)) * here + c(axis, upper) * inside
        total = total + c(of_rows, 0) * row_low + c(of_rows, 1) * row_high
        layers.append(total + (c(of_lanes, 0) * lane_low + c(of_lanes, 1) * lane_high))
        s.c_rcv[k] = s.c_rcv[k] + here
    fill(B0, s.vb0, s.c_rcv)
    smooth(0, s.vb0, s.va0, s.c_rcv[4], s.c_rcv[5])
    fill(B0, s.va0, layers)

    def emit_out(i, v, total):
        out[B0.own(i)] = v * THIRD + total

    stencil(0, s.va0, layers[4], layers[5], emit_out)


def shards(rhs, face_x, face_y, face_z):
    flat = [a.reshape(256, 128) for a in (rhs, face_x, face_y, face_z)]
    whole = pl.pallas_call(
        cycle,
        out_shape=jax.ShapeDtypeStruct((256, 128), F32),
        in_specs=[pl.BlockSpec(memory_space=pltpu.HBM)] * 4,
        out_specs=pl.BlockSpec(memory_space=pltpu.VMEM),
        scratch_shapes=list(SCRATCH.values()),
        compiler_params=pltpu.CompilerParams(
            collective_id=0, has_side_effects=True, vmem_limit_bytes=64 * 1024 * 1024
        ),
        name="vcycle",
    )(*flat)
    return whole.reshape(16, 16, 128)


def solution(mesh):
    placed = P("gx", "gy", "gz")
    return jax.shard_map(
        shards, mesh=mesh, in_specs=(placed,) * 4, out_specs=placed, check_vma=False
    )
```

```python
import jax
import jax.numpy as jnp
from jax import lax
from jax.experimental import pallas as pl
from jax.experimental.pallas import tpu as pltpu
from jax.sharding import PartitionSpec as P

RELAX = 2.0 / 3.0
THIRD = 1.0 / 3.0
COARSE_SWEEPS = 24
GX, GY, GZ = 4, 8, 8
F32 = jnp.float32
MESH = pl.DeviceIdType.MESH

FACES = [(1, 0, 0), (-1, 0, 0), (0, 1, 0), (0, -1, 0), (0, 0, 1), (0, 0, -1)]
DOWN = [(-1, 0, 0), (0, -1, 0), (0, 0, -1)]
RING_Z = [(0, 0, k) for k in (4, 3, 5, 2, 6, 1, 7)]
RING_Y = [(0, k, 0) for k in (4, 3, 5, 2, 6, 1, 7)]
AROUND = [
    (x, y, z) for x in (1, -1, 0) for y in (1, -1, 0) for z in (1, -1, 0) if (x, y, z) != (0, 0, 0)
]
AROUND.sort(key=lambda d: -(abs(d[0]) + abs(d[1]) + abs(d[2])))
LINE = [(2, 0, 0), (1, 0, 0), (3, 0, 0)]
FRIENDS = [(0, 0, 4), (0, 0, 3), (0, 0, 5), (0, 0, 2), (0, 0, 6)] + FACES
SIDES = [(0, 1, 0), (0, -1, 0)]
PLANE = [(2, 1, 0), (2, -1, 0), (1, 1, 0), (1, -1, 0), (3, 1, 0), (3, -1, 0)]
PLANE += [(2, 0, 0), (0, 1, 0), (0, -1, 0), (1, 0, 0), (3, 0, 0)]


def lanes(rows):
    return lax.broadcasted_iota(jnp.int32, (rows, 128), 1)


def sublanes(rows):
    return lax.broadcasted_iota(jnp.int32, (rows, 128), 0)


def turn(value, steps, axis=1):
    steps %= value.shape[axis]
    return value if steps == 0 else pltpu.roll(value, steps, axis)


def take(value, index):
    return jnp.take_along_axis(value, index, axis=1, mode="promise_in_bounds")


class Block:
    def __init__(self, size_x, size_y, size_z, weight):
        self.X, self.Y, self.Z, self.weight = size_x, size_y, size_z, weight
        self.pitch = size_y + 8
        self.rows = size_x * size_y
        self.padded = 8 + (size_x + 2) * self.pitch

    def base(self, i):
        return 8 + (i + 1) * self.pitch

    def own(self, i):
        return pl.ds(i * self.Y, self.Y)

    def at(self, i, shift=0):
        return pl.ds(self.base(i) + shift, self.Y)

    def row_of_each(self, y):
        return pl.ds(self.base(0) + y, self.X, stride=self.pitch)


B0 = Block(16, 16, 128, 1.0)

SCRATCH = {}


def vmem(name, *shape):
    SCRATCH[name] = pltpu.VMEM(shape, F32)


def dma(name, *shape):
    SCRATCH[name] = pltpu.SemaphoreType.DMA(shape)


for key in ("rhs", "fx", "fy", "fz"):
    vmem(key, 256, 128)
dma("in_sem", 5)
for key in ("cxl0", "cxu0", "cyl0", "cyu0", "czl0", "czu0", "g0", "d150", "kw0", "r0", "w0"):
    vmem(key, 256, 128)
vmem("va0", B0.padded, 128)
vmem("vb0", B0.padded, 128)
vmem("lyp0", B0.X * B0.pitch, 128)
for key in ("fx1", "fy1", "fz1", "r1"):
    vmem(key, 64, 128)
for key in ("cxl1", "cxu1", "cyl1", "cyu1", "czl1", "czu1", "g1", "d151", "kw1"):
    vmem(key, 17 * 16, 128)
for key in ("va1", "vb1"):
    vmem(key, 19 * 16, 128)
vmem("ext1", 4, 17 * 16, 128)
vmem("hw_own", 5, 8, 8, 128)
vmem("hw_pack", 3, 8, 8, 128)
vmem("hw_low", 3, 4, 8, 128)
vmem("hw_high", 3, 4, 8, 128)
vmem("hw_zed", 2, 8, 128)
vmem("hw_xr", 2, 3, 3, 8, 128)
vmem("hw_yr", 6, 3, 4, 8, 128)
vmem("hw_zr", 18, 8, 128)
dma("hw_ss", 26)
dma("hw_rs", 26)
vmem("q1", 8 * 16, 128)
for key, rows, count in (("a0", 16, 3), ("b", 16, 6), ("c", 16, 6), ("a1", 8, 3), ("d", 8, 6), ("e", 8, 6)):
    vmem(f"{key}_snd", count, rows, 128)
    vmem(f"{key}_rcv", count, rows, 128)
    dma(f"{key}_ss", count)
    dma(f"{key}_rs", count)
vmem("t0", 256, 128)
vmem("hh_snd", 6, 7, 16, 128)
vmem("hh_rcv", 6, 7, 16, 128)
dma("hh_ss", 6)
dma("hh_rs", 6)
vmem("side1", 6, 16, 128)
vmem("wide1", 6, 4, 16, 128)
vmem("t16", 3, 16, 128)
vmem("zf_snd", 3, 16, 128)
vmem("zf_rcv", 7, 3, 16, 128)
vmem("xf_snd", 3, 6, 16, 128)
vmem("xf_rcv", 3, 3, 6, 16, 128)
vmem("zr_snd", 16, 128)
vmem("zr_rcv", 7, 16, 128)
vmem("xr_snd", 2, 16, 128)
vmem("xr_rcv", 11, 2, 16, 128)
for key, count in (("zf", 7), ("zr", 7), ("xr", 11), ("xf", 3), ("nf", 2)):
    dma(f"{key}_ss", count)
    dma(f"{key}_rs", count)
for key in ("f2", "lx2", "ly2", "lz2", "va2", "vb2"):
    vmem(key, 2, 20, 16, 128)
for key in ("cxl2", "cxu2", "cyl2", "cyu2", "czl2", "czu2", "g2", "d152", "kw2"):
    vmem(key, 2, 20, 16, 128)
vmem("nv_snd", 1, 2, 8, 8, 128)
vmem("nv_rcv", 2, 1, 2, 8, 8, 128)
dma("nv_ss", 2)
dma("nv_rs", 2)
vmem("s2", 128, 128)
vmem("p2", 256, 128)
vmem("face3", 3, 128, 128)
vmem("f3", 128, 128)
for key in ("yf", "yr"):
    dma(f"{key}_ss", 7)
    dma(f"{key}_rs", 7)
for key in ("cxl3", "cxu3", "cyl3", "cyu3", "czl3", "czu3", "g3", "d153", "kw3", "r3", "p3"):
    vmem(key, 128, 128)
vmem("va3", 160, 128)
vmem("vb3", 160, 128)
for key in ("t4", "cxl4", "cxu4", "cyl4", "cyu4", "czl4", "czu4", "d154", "kw4", "r4", "p4"):
    vmem(key, 32, 128)
vmem("fc4", 3, 32, 128)
for key in ("t5", "cx5", "cyl5", "cyu5", "czl5", "czu5", "kw5", "e5"):
    vmem(key, 8, 128)


class Space:
    pass


def cycle(rhs_in, fx_in, fy_in, fz_in, out, *scratch):
    s = Space()
    for name, ref in zip(SCRATCH, scratch):
        setattr(s, name, ref)
    gx, gy, gz = lax.axis_index("gx"), lax.axis_index("gy"), lax.axis_index("gz")

    def peer(offset):
        return (
            (gx + offset[0]) & (GX - 1),
            (gy + offset[1]) & (GY - 1),
            (gz + offset[2]) & (GZ - 1),
        )

    loads = [
        pltpu.make_async_copy(source, target, s.in_sem.at[k])
        for k, (source, target) in enumerate(
            ((fx_in, s.fx), (fy_in, s.fy), (fz_in, s.fz), (rhs_in, s.rhs))
        )
    ]
    for load in loads:
        load.start()

    barrier = pltpu.get_barrier_semaphore()
    for offset in FRIENDS:
        pl.semaphore_signal(barrier, inc=1, device_id=peer(offset), device_id_type=MESH)

    def copies(offsets, sources, targets, ss, rs):
        made = [
            pltpu.make_async_remote_copy(
                src_ref=sources(k),
                dst_ref=targets(k),
                send_sem=ss.at[k],
                recv_sem=rs.at[k],
                device_id=peer(offset),
                device_id_type=MESH,
            )
            for k, offset in enumerate(offsets)
        ]
        for one in made:
            one.start()
        return made

    sent = []

    def finish(made):
        for one in made:
            one.wait_recv()
        sent.extend(made)

    def drain():
        for one in sent:
            one.wait_send()
        sent.clear()

    def flag(condition):
        return jnp.where(condition, 1.0, 0.0).astype(F32)

    low_x, low_y, low_z = flag(gx > 0), flag(gy > 0), flag(gz > 0)
    top_x, top_y, top_z = flag(gx < GX - 1), flag(gy < GY - 1), flag(gz < GZ - 1)


    def pack(read, rows, count, column):
        packed = jnp.zeros((rows, 128), F32)
        lane = lanes(rows)
        for i in range(count):
            packed = jnp.where(lane == i, turn(read(i), i - column), packed)
        return packed

    def send_faces(block, ref, key):
        snd = getattr(s, key + "_snd")
        snd[0] = ref[block.at(block.X - 1)]
        snd[1] = ref[block.at(0)]
        snd[2] = ref[block.row_of_each(block.Y - 1)]
        snd[3] = ref[block.row_of_each(0)]
        snd[4] = pack(lambda i: ref[block.at(i)], 16, 16, 127)
        snd[5] = pack(lambda i: ref[block.at(i)], 16, 16, 0)
        rcv = getattr(s, key + "_rcv")
        return copies(
            FACES,
            lambda k: snd.at[k],
            lambda k: rcv.at[k],
            getattr(s, key + "_ss"),
            getattr(s, key + "_rs"),
        )

    def fill(block, ref, halo):
        ref[block.at(-1)] = halo[0]
        ref[block.at(block.X)] = halo[1]
        ref[block.row_of_each(-1)] = halo[2]
        ref[block.row_of_each(block.Y)] = halo[3]

    def send_upper(lx, ly, lz, key):
        block = B0
        snd = getattr(s, key + "_snd")
        snd[0] = lx[block.own(0)]
        snd[1] = ly[pl.ds(0, block.X, stride=block.Y)]
        snd[2] = pack(lambda i: lz[block.own(i)], 16, 16, 0)
        rcv = getattr(s, key + "_rcv")
        pl.semaphore_wait(barrier, len(FRIENDS))
        return copies(
            DOWN,
            lambda k: snd.at[k],
            lambda k: rcv.at[k],
            getattr(s, key + "_ss"),
            getattr(s, key + "_rs"),
        )

    def coefficients(level, lx, ly, lz, key):
        block = B0
        rcv = getattr(s, key + "_rcv")
        lyp = getattr(s, f"lyp{level}")
        c = {k: getattr(s, f"{k}{level}") for k in ("cxl", "cxu", "cyl", "cyu", "czl", "czu")}
        d15, kw = getattr(s, f"d15{level}"), getattr(s, f"kw{level}")
        for i in range(block.X):
            lyp[pl.ds(i * block.pitch, block.Y)] = ly[block.own(i)]
        lyp[pl.ds(block.Y, block.X, stride=block.pitch)] = rcv[1] * top_y
        next_x = rcv[0] * top_x
        next_z = rcv[2] * top_z
        lane, row = lanes(block.Y), sublanes(block.Y)
        keep_y = jnp.where(row == 0, low_y, 1.0)
        keep_z = jnp.where(lane == 0, low_z, 1.0)
        for i in range(block.X):
            own = block.own(i)
            a_xl = lx[own]
            a_xu = lx[block.own(i + 1)] if i + 1 < block.X else next_x
            a_yl = ly[own]
            a_yu = lyp[pl.ds(i * block.pitch + 1, block.Y)]
            a_zl = lz[own]
            a_zu = jnp.where(
                lane == block.Z - 1, turn(next_z, block.Z - 1 - i), turn(a_zl, -1)
            )
            total = (a_xl + a_yl + a_zl) + (a_xu + a_yu + a_zu)
            scale = RELAX / total
            d15[own] = (1.5 * block.weight) * total
            kw[own] = scale * (1.0 / block.weight)
            c["cxl"][own] = scale * a_xl * (low_x if i == 0 else 1.0)
            c["cxu"][own] = scale * a_xu
            c["cyl"][own] = scale * a_yl * keep_y
            c["cyu"][own] = scale * a_yu
            c["czl"][own] = scale * a_zl * keep_z
            c["czu"][own] = scale * a_zu

    def stencil(level, ref, low, high, emit):
        block = B0
        lane = lanes(block.Y)
        get = lambda k: getattr(s, f"{k}{level}")
        for i in range(block.X):
            own = block.own(i)
            v = ref[block.at(i)]
            down = jnp.where(lane == 0, turn(low, -i), turn(v, 1))
            up = jnp.where(lane == block.Z - 1, turn(high, block.Z - 1 - i), turn(v, -1))
            t_x = get("cxl")[own] * ref[block.at(i - 1)] + get("cxu")[own] * ref[block.at(i + 1)]
            t_y = get("cyl")[own] * ref[block.at(i, -1)] + get("cyu")[own] * ref[block.at(i, 1)]
            t_z = get("czl")[own] * down + get("czu")[own] * up
            emit(i, v, get("g")[own] + (t_x + t_y + t_z))

    def smooth(level, source, target, low, high):
        block = B0

        def emit(i, v, total):
            target[block.at(i)] = v * THIRD + total

        stencil(level, source, low, high, emit)

    def residual(level, source, low, high):
        block = B0
        d15, r = getattr(s, f"d15{level}"), getattr(s, f"r{level}")

        def emit(i, v, total):
            r[block.own(i)] = d15[block.own(i)] * (total - RELAX * v)
            s.t0[block.own(i)] = v * THIRD + total

        stencil(level, source, low, high, emit)


    lane8, lane16 = lanes(8), lanes(16)
    row8, row16 = sublanes(8), sublanes(16)
    upper_half = row8 < 4
    slices_x = {1: (5, 3), -1: (0, 3), 0: (0, 8)}
    pairs_x = {1: (2, 2), -1: (0, 2), 0: (0, 4)}
    flat_yr = [(x, y) for x in (1, -1, 0) for y in (1, -1)]
    flat_zr = [(x, y, z) for x in (1, -1, 0) for y in (1, -1, 0) for z in (1, -1)]

    def pack_around():
        zeds = [jnp.zeros((8, 128), F32)] * 2
        group = lane8 // 3
        for a in range(5):
            for x in range(8):
                v, place = s.hw_own[a, x], 8 * a + x
                zeds = [
                    jnp.where(group == place, turn(v, 3 * place - first), zed)
                    for zed, first in zip(zeds, (61, 0))
                ]
        s.hw_zed[0], s.hw_zed[1] = zeds
        for t in range(3):
            tiles = []
            for x in range(8):
                v = s.hw_own[2 * t, x]
                if t < 2:
                    v = jnp.where(lane8 < 64, v, turn(s.hw_own[2 * t + 1, x], 64))
                s.hw_pack[t, x] = v
                tiles.append(v)
            for i in range(4):
                even, odd = tiles[2 * i], tiles[2 * i + 1]
                s.hw_low[t, i] = jnp.where(upper_half, even, turn(odd, 4, 0))
                s.hw_high[t, i] = jnp.where(upper_half, turn(even, 4, 0), odd)

    def send_around():
        def source(k):
            x, y, z = AROUND[k]
            if z != 0:
                return s.hw_zed.at[0 if z > 0 else 1]
            if y != 0:
                return (s.hw_low if y < 0 else s.hw_high).at[:, pl.ds(*pairs_x[x])]
            return s.hw_pack.at[:, pl.ds(*slices_x[x])]

        def target(k):
            x, y, z = AROUND[k]
            if z != 0:
                return s.hw_zr.at[flat_zr.index((x, y, z))]
            if y != 0:
                return s.hw_yr.at[flat_yr.index((x, y)), :, pl.ds(0, pairs_x[x][1])]
            return s.hw_xr.at[0 if x > 0 else 1]

        return copies(AROUND, source, target, s.hw_ss, s.hw_rs)

    def assemble(a, k):
        x = k - 4
        if x < 0:
            d, layer, first = 1, x + 8, 5
        elif x < 8:
            d, layer, first = 0, x, 0
        else:
            d, layer, first = -1, x - 8, 0
        place = 3 * (8 * a + layer)
        t = a // 2
        inner = s.hw_own[a, layer] if d == 0 else s.hw_xr[0 if d > 0 else 1, t, layer - first]
        pair = layer // 2 - pairs_x[d][0]
        above = s.hw_yr[flat_yr.index((d, -1)), t, pair]
        below = s.hw_yr[flat_yr.index((d, 1)), t, pair]
        if layer % 2 == 0:
            below = turn(below, 4, 0)
        else:
            above = turn(above, 4, 0)
        outer = jnp.where(upper_half, above, below)
        if a % 2 == 1:
            outer = turn(outer, 64)
            inner = inner if d == 0 else turn(inner, 64)
        whole = jnp.concatenate([inner, outer], axis=0)

        def side(z):
            zed = lambda y: s.hw_zr[flat_zr.index((d, y, z))]
            outer = jnp.where(upper_half, zed(-1), zed(1))
            return jnp.concatenate([zed(0), outer], axis=0)

        whole = jnp.where((lane16 >= 64) & (lane16 < 72), turn(side(-1), 64 - place), whole)
        return jnp.where(lane16 >= 120, turn(side(1), 125 - place), whole)

    def ext1(k):
        return pl.ds(16 * k, 16)

    def pad1(k):
        return pl.ds(16 * k + 16, 16)

    def coefficients1(first, last):
        keep_y = jnp.where(row16 == 0, low_y, 1.0)
        keep_z = jnp.where(lane16 == 0, low_z, 1.0)
        last_y = jnp.where(row16 == 7, top_y, 1.0)
        last_z = jnp.where(lane16 == 63, top_z, 1.0)
        for k in range(first, last + 1):
            own = ext1(k)
            a_xl, a_yl, a_zl = s.ext1[0, own], s.ext1[1, own], s.ext1[2, own]
            a_xu = s.ext1[0, ext1(k + 1)]
            if k == 11:
                a_xu = a_xu * top_x
            a_yu = turn(a_yl, -1, 0) * last_y
            a_zu = turn(a_zl, -1) * last_z
            total = (a_xl + a_yl + a_zl) + (a_xu + a_yu + a_zu)
            scale = RELAX / total
            s.kw1[own] = scale * 4.0
            s.d151[own] = (1.5 * 0.25) * total
            s.cxl1[own] = scale * a_xl * (low_x if k == 4 else 1.0)
            s.cxu1[own] = scale * a_xu
            s.cyl1[own] = scale * a_yl * keep_y
            s.cyu1[own] = scale * a_yu
            s.czl1[own] = scale * a_zl * keep_z
            s.czu1[own] = scale * a_zu

    def send_faces1(ref, key):
        snd, rcv = getattr(s, key + "_snd"), getattr(s, key + "_rcv")
        inner = lambda i: ref[pl.ds(16 * (i + 5), 8)]
        snd[0] = inner(7)
        snd[1] = inner(0)
        snd[2] = ref[pl.ds(16 * 5 + 7, 8, stride=16)]
        snd[3] = ref[pl.ds(16 * 5, 8, stride=16)]
        snd[4] = pack(inner, 8, 8, 63)
        snd[5] = pack(inner, 8, 8, 0)
        return copies(
            FACES,
            lambda k: snd.at[k],
            lambda k: rcv.at[k],
            getattr(s, key + "_ss"),
            getattr(s, key + "_rs"),
        )

    def fill1(ref, halo):
        low, high = halo[4], halo[5]
        for i in range(8):
            own = pl.ds(16 * (i + 5), 8)
            v = jnp.where(lane8 == 64, turn(high, 64 - i), ref[own])
            ref[own] = jnp.where(lane8 == 127, turn(low, 127 - i), v)
        ref[pl.ds(16 * 4, 8)] = halo[0]
        ref[pl.ds(16 * 13, 8)] = halo[1]
        ref[pl.ds(16 * 5 + 15, 8, stride=16)] = halo[2]
        ref[pl.ds(16 * 5 + 8, 8, stride=16)] = halo[3]

    def stencil1(first, last, ref, emit):
        for k in range(first, last + 1):
            own = ext1(k)
            v = ref[pad1(k)]
            t_x = s.cxl1[own] * ref[pad1(k - 1)] + s.cxu1[own] * ref[pad1(k + 1)]
            t_y = s.cyl1[own] * turn(v, 1, 0) + s.cyu1[own] * turn(v, -1, 0)
            t_z = s.czl1[own] * turn(v, 1) + s.czu1[own] * turn(v, -1)
            emit(k, v, s.g1[own] + (t_x + t_y + t_z))

    def smooth1(first, last, source, target):
        def emit(k, v, total):
            target[pad1(k)] = v * THIRD + total

        stencil1(first, last, source, emit)

    even8 = (2 * lane8) & 127
    half16 = lane16 >> 1

    def pair_z(value):
        return value + turn(value, -1)

    def stage_z(arrays, snd):
        group = lane16 >> 4
        packed = jnp.zeros((16, 128), F32)
        for a in range(arrays):
            whole = s.t16[a]
            for p in range(2):
                moved = take(whole, 4 * (lane16 & 15) + 2 * p)
                packed = jnp.where(group == ((gz + 2 * a + p) & 7), moved, packed)
        snd[...] = packed

    def merge_z(arrays, own, others, target):
        group = lane16 >> 4
        parts = [(0, own)] + [(RING_Z[k][2], others(k)) for k in range(7)]
        for q in range(2 * arrays):
            merged = jnp.zeros((16, 128), F32)
            for distance, part in parts:
                merged = jnp.where(group == ((gz - distance + q) & 7), part, merged)
            target[q] = turn(merged, -16 * q)

    for load in loads[:3]:
        load.wait()
    round_a0 = send_upper(s.fx, s.fy, s.fz, "a0")

    for i in range(8):
        own = pl.ds(8 * i, 8)
        here = lambda ref, shift: ref[pl.ds(32 * i + shift, 8, stride=2)]
        s.fx1[own] = take(pair_z(here(s.fx, 0) + here(s.fx, 1)), even8) * 0.25
        s.fy1[own] = take(pair_z(here(s.fy, 0) + here(s.fy, 16)), even8) * 0.25
        total = (here(s.fz, 0) + here(s.fz, 1)) + (here(s.fz, 16) + here(s.fz, 17))
        s.fz1[own] = take(total, even8) * 0.25
    s.a1_snd[0] = s.fx1[pl.ds(0, 8)]
    s.a1_snd[1] = s.fy1[pl.ds(0, 8, stride=8)]
    s.a1_snd[2] = pack(lambda i: s.fz1[pl.ds(8 * i, 8)], 8, 8, 0)
    round_a1 = copies(
        DOWN, lambda k: s.a1_snd.at[k], lambda k: s.a1_rcv.at[k], s.a1_ss, s.a1_rs
    )
    for i in range(4):
        own = pl.ds(4 * i, 4)
        here = lambda ref, shift: ref[pl.ds(16 * i + shift, 4, stride=2)]
        s.t16[0, own] = here(s.fx1, 0) + here(s.fx1, 1)
        s.t16[1, own] = here(s.fy1, 0) + here(s.fy1, 8)
        total = (here(s.fz1, 0) + here(s.fz1, 1)) + (here(s.fz1, 8) + here(s.fz1, 9))
        s.t16[2, own] = total * 0.25
    s.t16[0] = pair_z(s.t16[0]) * 0.25
    s.t16[1] = pair_z(s.t16[1]) * 0.25
    stage_z(3, s.zf_snd.at[0])
    round_nf = copies(
        SIDES, lambda k: s.zf_snd.at[0], lambda k: s.zf_snd.at[k + 1], s.nf_ss, s.nf_rs
    )
    for ref in (s.va1, s.vb1):
        for k in (-1, 17):
            ref[pad1(k)] = jnp.zeros((16, 128), F32)
    for p in range(2):
        for x in range(16):
            for ref in (s.lx2, s.ly2, s.lz2):
                ref[p, x + 2, pl.ds(8, 8)] = jnp.ones((8, 128), F32)
        for x in (0, 1, 18, 19):
            for ref in (s.va2, s.vb2):
                ref[p, x] = jnp.zeros((16, 128), F32)
        for x in range(16):
            s.f2[p, x + 2] = jnp.zeros((16, 128), F32)
    for ref in (s.va3, s.vb3):
        for k in range(2):
            ref[pl.ds(8 * k, 8)] = jnp.zeros((8, 128), F32)
            ref[pl.ds(144 + 8 * k, 8)] = jnp.zeros((8, 128), F32)
    s.p2[...] = jnp.zeros_like(s.p2)
    s.ext1[...] = jnp.ones_like(s.ext1)
    for k in (0, 1, 2, 3, 12, 13, 14, 15):
        s.va1[pad1(k)] = jnp.zeros((16, 128), F32)
        s.vb1[pad1(k)] = jnp.zeros((16, 128), F32)

    loads[3].wait()
    finish(round_a0)
    coefficients(0, s.fx, s.fy, s.fz, "a0")
    for i in range(16):
        own = B0.own(i)
        start = s.kw0[own] * s.rhs[own]
        s.g0[own] = start
        s.va0[B0.at(i)] = start
    round_b = send_faces(B0, s.va0, "b")
    finish(round_nf)
    round_zf = copies(
        RING_Z, lambda k: s.zf_snd, lambda k: s.zf_rcv.at[k], s.zf_ss, s.zf_rs
    )
    finish(round_a1)
    for i in range(8):
        own, here = pl.ds(8 * i, 8), pl.ds(16 * (i + 4), 8)
        s.ext1[0, here] = s.fx1[own]
        s.ext1[1, here] = s.fy1[own]
        upper = turn(s.a1_rcv[2], 64 - i)
        s.ext1[2, here] = jnp.where(lane8 == 64, upper, s.fz1[own])
        s.hw_own[0, i] = s.fx1[own]
        s.hw_own[1, i] = s.fy1[own]
        s.hw_own[2, i] = s.fz1[own]
    s.ext1[0, pl.ds(16 * 12, 8)] = s.a1_rcv[0]
    s.ext1[1, pl.ds(16 * 4 + 8, 8, stride=16)] = s.a1_rcv[1]
    coefficients1(4, 11)
    finish(round_b)
    fill(B0, s.va0, s.b_rcv)
    smooth(0, s.va0, s.vb0, s.b_rcv[4], s.b_rcv[5])
    round_c = send_faces(B0, s.vb0, "c")
    finish(round_zf)
    for side in range(3):
        merge_z(3, s.zf_snd[side], lambda k: s.zf_rcv[k, side], s.xf_snd.at[side])
    round_xf = copies(
        LINE, lambda k: s.xf_snd, lambda k: s.xf_rcv.at[k], s.xf_ss, s.xf_rs
    )
    finish(round_c)
    fill(B0, s.vb0, s.c_rcv)
    residual(0, s.vb0, s.c_rcv[4], s.c_rcv[5])

    for i in range(8):
        here = lambda shift: s.r0[pl.ds(32 * i + shift, 8, stride=2)]
        total = (here(0) + here(1)) + (here(16) + here(17))
        forcing = take(pair_z(total), even8) * 0.125
        s.hw_own[3, i] = forcing
        start = s.kw1[pl.ds(16 * (i + 4), 8)] * forcing
        s.g1[pl.ds(16 * (i + 4), 8)] = start
        s.g1[pl.ds(16 * (i + 4) + 8, 8)] = jnp.zeros((8, 128), F32)
        s.va1[pl.ds(16 * (i + 5), 8)] = start
        s.va1[pl.ds(16 * (i + 5) + 8, 8)] = jnp.zeros((8, 128), F32)
    round_d = send_faces1(s.va1, "d")
    kept = (s.t0, s.cxl0, s.cxu0, s.cyl0, s.cyu0, s.czl0, s.czu0)
    for a, ref in enumerate(kept):
        s.hh_snd[0, a] = ref[B0.own(15)]
        s.hh_snd[1, a] = ref[B0.own(0)]
        s.hh_snd[2, a] = ref[pl.ds(15, 16, stride=16)]
        s.hh_snd[3, a] = ref[pl.ds(0, 16, stride=16)]
        s.hh_snd[4, a] = pack(lambda i: ref[B0.own(i)], 16, 16, 127)
        s.hh_snd[5, a] = pack(lambda i: ref[B0.own(i)], 16, 16, 0)
    finish(round_d)
    fill1(s.va1, s.d_rcv)
    smooth1(4, 11, s.va1, s.vb1)
    for i in range(8):
        s.hw_own[4, i] = s.vb1[pl.ds(16 * (i + 5), 8)]
    round_e = send_faces1(s.vb1, "e")
    pack_around()


    def block2(p, x):
        return (p, x + 2)

    def spread(arrays, offsets, snd, rcv, targets):
        parts = [((0, 0, 0), lambda q: snd.at[q])]
        for k, offset in enumerate(offsets):
            parts.append((offset, lambda q, k=k: rcv.at[k, q]))
        for offset, part in parts:
            first = 4 * ((gx - offset[0]) & 3)
            place = pl.ds(4 * (1 - offset[1]), 4)
            for a in range(arrays):
                for p in range(2):
                    for x in range(4):
                        piece = part(2 * a + p)[pl.ds(4 * x, 4)]
                        targets[a][p, x + 2 + first, place] = piece

    def send_sides(refs, key):
        snd, rcv = getattr(s, key + "_snd"), getattr(s, key + "_rcv")
        for a, ref in enumerate(refs):
            for p in range(2):
                for i in range(8):
                    even = ref[p, 2 * i + 2, pl.ds(0, 8)]
                    odd = ref[p, 2 * i + 3, pl.ds(0, 8)]
                    snd[a, p, i] = jnp.where(upper_half, turn(even, 4, 0), odd)
        return copies(
            SIDES,
            lambda k: snd,
            lambda k: rcv.at[k],
            getattr(s, key + "_ss"),
            getattr(s, key + "_rs"),
        )

    def take_sides(refs, key, rest):
        rcv = getattr(s, key + "_rcv")
        for a, ref in enumerate(refs):
            for p in range(2):
                for x in range(16):
                    below, above = rcv[0, a, p, x // 2], rcv[1, a, p, x // 2]
                    if x % 2 == 1:
                        below, above = turn(below, 4, 0), turn(above, 4, 0)
                    own = ref[p, x + 2, pl.ds(0, 8)]
                    ref[p, x + 2, pl.ds(0, 8)] = jnp.where(upper_half, below, own)
                    ref[p, x + 2, pl.ds(8, 8)] = jnp.where(upper_half, above, rest)

    faces2 = (s.lx2, s.ly2, s.lz2)
    global_y = row16 + 4 * gy - 4
    not_low, not_top = global_y != 0, global_y != 4 * GY - 1

    mine = pl.ds(pl.multiple_of(16 * gy, 16), 16)

    finish(round_xf)
    for line in range(4):
        first = 4 * ((gx - ((0, 0, 0), *LINE)[line][0]) & 3)
        for side in range(3):
            part = s.xf_snd.at[side] if line == 0 else s.xf_rcv.at[line - 1, side]
            place = pl.ds((4, 0, 8)[side], 4)
            for a in range(3):
                for p in range(2):
                    for x in range(4):
                        piece = part[2 * a + p, pl.ds(4 * x, 4)]
                        faces2[a][p, x + 2 + first, place] = piece
    for a, ref in enumerate((s.lx2, s.ly2, s.lz2)):
        for i in range(8):
            total = ref[block2(0, 2 * i)]
            if a != 2:
                total = total + ref[block2(1, 2 * i)]
            if a != 0:
                total = total + ref[block2(0, 2 * i + 1)]
            if a == 1:
                total = total + ref[block2(1, 2 * i + 1)]
            s.s2[pl.ds(16 * i, 16)] = total
        for j in range(2):
            total = s.s2[pl.ds(4 + 2 * j, 8, stride=16)]
            if a != 1:
                total = total + s.s2[pl.ds(5 + 2 * j, 8, stride=16)]
            s.face3[a, pl.ds(pl.multiple_of(16 * gy + 8 * j, 8), 8)] = total * 0.25
    round_yf = copies(
        RING_Y,
        lambda k: s.face3.at[:, mine],
        lambda k: s.face3.at[:, mine],
        s.yf_ss,
        s.yf_rs,
    )
    finish(round_e)
    fill1(s.vb1, s.e_rcv)

    def emit_r1(k, v, total):
        r = s.d151[ext1(k)] * (total - RELAX * v)
        s.r1[pl.ds(8 * (k - 4), 8)] = r[0:8]

    stencil1(4, 11, s.vb1, emit_r1)
    for i in range(4):
        here = lambda shift: s.r1[pl.ds(16 * i + shift, 4, stride=2)]
        s.t16[0, pl.ds(4 * i, 4)] = (here(0) + here(1)) + (here(8) + here(9))
    s.t16[0] = pair_z(s.t16[0]) * 0.125
    stage_z(1, s.zr_snd)
    round_zr = copies(
        RING_Z, lambda k: s.zr_snd, lambda k: s.zr_rcv.at[k], s.zr_ss, s.zr_rs
    )


    def stencil2(ref, emit):
        for p in range(2):
            for x in range(16):
                j, other = block2(p, x), block2(1 - p, x)
                v, w = ref[j], ref[other]
                t_x = s.cxl2[j] * ref[block2(p, x - 1)] + s.cxu2[j] * ref[block2(p, x + 1)]
                t_y = s.cyl2[j] * turn(v, 1, 0) + s.cyu2[j] * turn(v, -1, 0)
                down, up = (turn(w, 1), w) if p == 0 else (w, turn(w, -1))
                t_z = s.czl2[j] * down + s.czu2[j] * up
                emit(j, v, s.g2[j] + (t_x + t_y + t_z))

    def smooth2(source, target):
        def emit(j, v, total):
            target[j] = v * THIRD + total

        stencil2(source, emit)

    round_hw = send_around()
    for p in range(2):
        for x in range(16):
            j = block2(p, x)
            a_xl, a_yl, a_zl = s.lx2[j], s.ly2[j], s.lz2[j]
            a_xu = s.lx2[block2(p, x + 1)] if x < 15 else jnp.zeros((16, 128), F32)
            a_yu = jnp.where(not_top, turn(a_yl, -1, 0), 0.0)
            if p == 0:
                a_zu = s.lz2[block2(1, x)]
            else:
                a_zu = jnp.where(lane16 == 127, 0.0, turn(s.lz2[block2(0, x)], -1))
            total = (a_xl + a_yl + a_zl) + (a_xu + a_yu + a_zu)
            scale = RELAX / total
            s.d152[j] = (1.5 * 0.0625) * total
            s.kw2[j] = scale * 16.0
            s.cxl2[j] = scale * a_xl if x > 0 else jnp.zeros((16, 128), F32)
            s.cxu2[j] = scale * a_xu
            s.cyl2[j] = jnp.where(not_low, scale * a_yl, 0.0)
            s.cyu2[j] = scale * a_yu
            s.czl2[j] = scale * a_zl if p == 1 else jnp.where(lane16 == 0, 0.0, scale * a_zl)
            s.czu2[j] = scale * a_zu

    finish(round_zr)
    merge_z(1, s.zr_snd[...], lambda k: s.zr_rcv[k], s.xr_snd)
    round_xr = copies(
        PLANE, lambda k: s.xr_snd, lambda k: s.xr_rcv.at[k], s.xr_ss, s.xr_rs
    )

    finish(round_yf)
    zero8 = jnp.zeros((8, 128), F32)
    for y in range(16):
        own = pl.ds(8 * y, 8)
        a_xl, a_yl, a_zl = s.face3[0, own], s.face3[1, own], s.face3[2, own]
        a_xu = jnp.where(row8 == 7, 0.0, turn(a_xl, -1, 0))
        a_yu = s.face3[1, pl.ds(8 * y + 8, 8)] if y < 15 else zero8
        a_zu = jnp.where(lane8 == 127, 0.0, turn(a_zl, -1))
        total = (a_xl + a_yl + a_zl) + (a_xu + a_yu + a_zu)
        scale = RELAX / total
        s.d153[own] = (1.5 * 0.25**3) * total
        s.kw3[own] = scale * 64.0
        s.cxl3[own] = jnp.where(row8 == 0, 0.0, scale * a_xl)
        s.cxu3[own] = scale * a_xu
        s.cyl3[own] = scale * a_yl if y > 0 else zero8
        s.cyu3[own] = scale * a_yu
        s.czl3[own] = jnp.where(lane8 == 0, 0.0, scale * a_zl)
        s.czu3[own] = scale * a_zu

    lane32, row32 = lanes(32), sublanes(32)

    def both(value, lane, step):
        return value + jnp.where(
            (lane & step) == 0, turn(value, -step), turn(value, step)
        )

    def lower_of(value, lane, step):
        return jnp.where((lane & step) == 0, value, turn(value, step))

    for a in range(3):
        for y in range(8):
            here = lambda shift: s.face3[a, pl.ds(16 * y + shift, 4, stride=2)]
            if a == 0:
                total = here(0) + here(8)
            elif a == 1:
                total = here(0) + here(1)
            else:
                total = (here(0) + here(1)) + (here(8) + here(9))
            s.t4[pl.ds(4 * y, 4)] = total
        total = s.t4[...]
        total = both(total, lane32, 1) if a < 2 else lower_of(total, lane32, 1)
        s.fc4[a] = total * 0.25
    a_xl, a_yl, a_zl = s.fc4[0], s.fc4[1], s.fc4[2]
    a_xu = jnp.where((row32 & 3) == 3, 0.0, turn(a_xl, -1, 0))
    a_yu = jnp.where(row32 >= 28, 0.0, turn(a_yl, -4, 0))
    a_zu = jnp.where(lane32 >= 126, 0.0, turn(a_zl, -2))
    total = (a_xl + a_yl + a_zl) + (a_xu + a_yu + a_zu)
    scale = RELAX / total
    s.d154[...] = (1.5 * 0.25**4) * total
    s.kw4[...] = scale * 256.0
    s.cxl4[...] = jnp.where((row32 & 3) == 0, 0.0, scale * a_xl)
    s.cxu4[...] = scale * a_xu
    s.cyl4[...] = jnp.where(row32 < 4, 0.0, scale * a_yl)
    s.cyu4[...] = scale * a_yu
    s.czl4[...] = jnp.where(lane32 < 2, 0.0, scale * a_zl)
    s.czu4[...] = scale * a_zu

    faces5 = []
    for a in range(3):
        for x in range(2):
            here = lambda shift: s.fc4[a, pl.ds(2 * x + shift, 4, stride=8)]
            if a == 0:
                total = here(0) + here(4)
            elif a == 1:
                total = here(0) + here(1)
            else:
                total = (here(0) + here(1)) + (here(4) + here(5))
            s.t5[pl.ds(4 * x, 4)] = total
        total = s.t5[...]
        total = both(total, lane8, 2) if a < 2 else lower_of(total, lane8, 2)
        faces5.append(total * 0.25)
    a_xl, a_yl, a_zl = faces5
    a_xu = jnp.where(row8 >= 4, 0.0, turn(a_xl, 4, 0))
    a_yu = jnp.where((row8 & 3) == 3, 0.0, turn(a_yl, -1, 0))
    a_zu = jnp.where(lane8 >= 124, 0.0, turn(a_zl, -4))
    total = (a_xl + a_yl + a_zl) + (a_xu + a_yu + a_zu)
    scale = RELAX / total
    s.kw5[...] = scale * 1024.0
    s.cx5[...] = jnp.where(row8 >= 4, scale * a_xl, scale * a_xu)
    s.cyl5[...] = jnp.where((row8 & 3) == 0, 0.0, scale * a_yl)
    s.cyu5[...] = scale * a_yu
    s.czl5[...] = jnp.where(lane8 < 4, 0.0, scale * a_zl)
    s.czu5[...] = scale * a_zu

    finish(round_xr)
    spread(1, PLANE, s.xr_snd, s.xr_rcv, (s.f2,))
    for p in range(2):
        for x in range(16):
            j = block2(p, x)
            start = s.kw2[j] * s.f2[j]
            s.g2[j] = start
            s.va2[j] = start
    smooth2(s.va2, s.vb2)

    def emit_r2(j, v, total):
        s.f2[j] = s.d152[j] * (total - RELAX * v)

    stencil2(s.vb2, emit_r2)
    for i in range(8):
        total = (s.f2[block2(0, 2 * i)] + s.f2[block2(1, 2 * i)]) + (
            s.f2[block2(0, 2 * i + 1)] + s.f2[block2(1, 2 * i + 1)]
        )
        s.s2[pl.ds(16 * i, 16)] = total
    for j in range(2):
        total = s.s2[pl.ds(4 + 2 * j, 8, stride=16)] + s.s2[pl.ds(5 + 2 * j, 8, stride=16)]
        s.f3[pl.ds(pl.multiple_of(16 * gy + 8 * j, 8), 8)] = total * 0.125
    round_yr = copies(
        RING_Y, lambda k: s.f3.at[mine], lambda k: s.f3.at[mine], s.yr_ss, s.yr_rs
    )
    round_nv = send_sides((s.vb2,), "nv")
    round_hh = copies(
        FACES, lambda k: s.hh_snd.at[k], lambda k: s.hh_rcv.at[k], s.hh_ss, s.hh_rs
    )

    drain()
    finish(round_hw)
    for k in range(1, 15):
        for a in range(4):
            s.ext1[a, ext1(k)] = assemble(a, k)
        s.vb1[pad1(k)] = assemble(4, k)
    coefficients1(2, 13)
    for k in range(2, 14):
        s.g1[ext1(k)] = s.kw1[ext1(k)] * s.ext1[3, ext1(k)]
    finish(round_yr)

    def at3(y):
        return pl.ds(16 + 8 * y, 8)

    def stencil3(ref, emit):
        for y in range(16):
            own = pl.ds(8 * y, 8)
            v = ref[at3(y)]
            t_x = s.cxl3[own] * turn(v, 1, 0) + s.cxu3[own] * turn(v, -1, 0)
            t_y = s.cyl3[own] * ref[at3(y - 1)] + s.cyu3[own] * ref[at3(y + 1)]
            t_z = s.czl3[own] * turn(v, 1) + s.czu3[own] * turn(v, -1)
            emit(y, v, s.g3[own] + (t_x + t_y + t_z))

    def smooth3(source, target):
        def emit(y, v, total):
            target[at3(y)] = v * THIRD + total

        stencil3(source, emit)

    for y in range(16):
        own = pl.ds(8 * y, 8)
        start = s.kw3[own] * s.f3[own]
        s.g3[own] = start
        s.va3[at3(y)] = start
    smooth3(s.va3, s.vb3)

    def emit_r3(y, v, total):
        own = pl.ds(8 * y, 8)
        s.r3[own] = s.d153[own] * (total - RELAX * v)

    stencil3(s.vb3, emit_r3)
    for y in range(8):
        here = lambda shift: s.r3[pl.ds(16 * y + shift, 4, stride=2)]
        s.t4[pl.ds(4 * y, 4)] = (here(0) + here(1)) + (here(8) + here(9))
    f4 = both(s.t4[...], lane32, 1) * 0.125

    def total4(v):
        t_x = s.cxl4[...] * turn(v, 1, 0) + s.cxu4[...] * turn(v, -1, 0)
        t_y = s.cyl4[...] * turn(v, 4, 0) + s.cyu4[...] * turn(v, -4, 0)
        t_z = s.czl4[...] * turn(v, 2) + s.czu4[...] * turn(v, -2)
        return g4 + (t_x + t_y + t_z)

    g4 = s.kw4[...] * f4
    v4 = g4
    v4 = v4 * THIRD + total4(v4)
    s.r4[...] = s.d154[...] * (total4(v4) - RELAX * v4)
    for x in range(2):
        here = lambda shift: s.r4[pl.ds(2 * x + shift, 4, stride=8)]
        s.t5[pl.ds(4 * x, 4)] = (here(0) + here(1)) + (here(4) + here(5))
    g5 = s.kw5[...] * (both(s.t5[...], lane8, 2) * 0.125)
    cx5, cyl5, cyu5, czl5, czu5 = s.cx5[...], s.cyl5[...], s.cyu5[...], s.czl5[...], s.czu5[...]

    def sweep5(index, v):
        t_y = cyl5 * turn(v, 1, 0) + cyu5 * turn(v, -1, 0)
        t_z = czl5 * turn(v, 4) + czu5 * turn(v, -4)
        return (v * THIRD + g5) + (cx5 * turn(v, 4, 0) + (t_y + t_z))

    s.e5[...] = lax.fori_loop(0, COARSE_SWEEPS - 1, sweep5, g5)
    for x in range(2):
        piece = s.e5[pl.ds(4 * x, 4)]
        for shift in (0, 1, 4, 5):
            s.p4[pl.ds(2 * x + shift, 4, stride=8)] = piece
    v4 = v4 + s.p4[...]
    v4 = v4 * THIRD + total4(v4)
    v4 = v4 * THIRD + total4(v4)
    s.r4[...] = v4
    for x in range(4):
        piece = s.r4[pl.ds(x, 8, stride=4)]
        for shift in (0, 1, 8, 9):
            s.p3[pl.ds(2 * x + shift, 8, stride=16)] = piece
    for y in range(16):
        s.vb3[at3(y)] = s.vb3[at3(y)] + s.p3[pl.ds(8 * y, 8)]
    smooth3(s.vb3, s.va3)
    smooth3(s.va3, s.vb3)

    finish(round_nv)
    take_sides((s.vb2,), "nv", 0.0)
    for k in range(6):
        piece = s.vb3[pl.ds(pl.multiple_of(16 * gy + 8 * k, 8), 8)]
        for x in range(2):
            for y in range(2):
                s.p2[pl.ds(16 * x + 2 * k + y, 8, stride=32)] = piece
    for x in range(16):
        more = s.p2[pl.ds(16 * x, 16)]
        for p in range(2):
            s.vb2[block2(p, x)] = s.vb2[block2(p, x)] + more
    smooth2(s.vb2, s.va2)
    smooth2(s.va2, s.vb2)

    signed = jnp.where(lane16 < 96, lane16, lane16 - 128)
    index = (16 * gz + (signed >> 2)) & 127
    odd = ((signed >> 1) & 1) == 1
    for k in range(8):
        x = 4 * gx + k
        piece = jnp.where(odd, take(s.vb2[1, x], index), take(s.vb2[0, x], index))
        rows = jnp.where(row16 < 6, turn(piece, -4, 0), turn(piece, 4, 0))[0:8]
        for y in range(2):
            s.q1[pl.ds(16 * k + y, 8, stride=2)] = rows
        more = s.q1[pl.ds(16 * k, 16)]
        for i in (2 * k, 2 * k + 1):
            if 1 <= i <= 14:
                s.vb1[pad1(i)] = s.vb1[pad1(i)] + more
    smooth1(2, 13, s.vb1, s.va1)
    smooth1(3, 12, s.va1, s.vb1)
    inner = lambda i: s.vb1[pl.ds(16 * (i + 5), 8)]

    def widen(value, ref, start):
        ref[pl.ds(start, 8, stride=2)] = value
        ref[pl.ds(start + 1, 8, stride=2)] = value
        return take(ref[pl.ds(start, 16)], half16)

    for i in range(8):
        more = widen(inner(i), s.w0, 16 * i)
        for x in (2 * i, 2 * i + 1):
            s.vb0[B0.at(x)] = s.vb0[B0.at(x)] + more

    sides = [s.vb1[pl.ds(16 * 4, 16)], s.vb1[pl.ds(16 * 13, 16)]]
    near = [inner(0), inner(7)]
    for k, row, edge in ((2, 15, 0), (3, 8, 7)):
        s.side1[k, pl.ds(8, 8)] = jnp.zeros((8, 128), F32)
        s.side1[k, pl.ds(0, 8)] = s.vb1[pl.ds(16 * 5 + row, 8, stride=16)]
        s.side1[k, pl.ds(8, 1)] = s.vb1[pl.ds(16 * 13 + row, 1)]
        s.side1[k, pl.ds(15, 1)] = s.vb1[pl.ds(16 * 4 + row, 1)]
        sides.append(s.side1[k])
        near.append(s.vb1[pl.ds(16 * 5 + edge, 8, stride=16)])
    for column, edge in ((127, 0), (64, 63)):
        packed = jnp.zeros((16, 128), F32)
        for k in range(3, 13):
            place = (k - 4) & 127
            packed = jnp.where(lane16 == place, turn(s.vb1[pad1(k)], place - column), packed)
        sides.append(packed)
        near.append(pack(inner, 8, 8, edge))

    def tall(value, ref):
        ref[pl.ds(0, 8, stride=2)] = value
        ref[pl.ds(1, 8, stride=2)] = value
        return ref[...]

    first_row, first_lane = (row16 & 1) == 0, (lane16 & 1) == 0
    layers = []
    finish(round_hh)
    drain()
    for k in range(6):
        side = sides[k]
        rows = tall(side[0:8], s.wide1.at[k, 0])
        here = take(rows, half16)
        inside = take(tall(near[k], s.wide1.at[k, 1]), half16)
        before = take(tall(turn(side, 1, 0)[0:8], s.wide1.at[k, 2]), half16)
        after = take(tall(turn(side, -1, 0)[0:8], s.wide1.at[k, 3]), half16)
        row_low = jnp.where(first_row, before, here)
        row_high = jnp.where(first_row, here, after)
        lane_low = jnp.where(first_lane, take(turn(rows, 1), half16), here)
        lane_high = jnp.where(first_lane, here, take(turn(rows, -1), half16))
        axis = k // 2
        of_rows, of_lanes = ((1, 2), (0, 2), (1, 0))[axis]
        c = lambda d, upper: s.hh_rcv[k, 1 + 2 * d + upper]
        upper = 1 - k % 2
        total = s.hh_rcv[k, 0] + (THIRD + c(axis, 1 - upper)) * here + c(axis, upper) * inside
        total = total + c(of_rows, 0) * row_low + c(of_rows, 1) * row_high
        layers.append(total + (c(of_lanes, 0) * lane_low + c(of_lanes, 1) * lane_high))
        s.c_rcv[k] = s.c_rcv[k] + here
    fill(B0, s.vb0, s.c_rcv)
    smooth(0, s.vb0, s.va0, s.c_rcv[4], s.c_rcv[5])
    fill(B0, s.va0, layers)

    def emit_out(i, v, total):
        out[B0.own(i)] = v * THIRD + total

    stencil(0, s.va0, layers[4], layers[5], emit_out)


def shards(rhs, face_x, face_y, face_z):
    flat = [a.reshape(256, 128) for a in (rhs, face_x, face_y, face_z)]
    whole = pl.pallas_call(
        cycle,
        out_shape=jax.ShapeDtypeStruct((256, 128), F32),
        in_specs=[pl.BlockSpec(memory_space=pltpu.HBM)] * 4,
        out_specs=pl.BlockSpec(memory_space=pltpu.VMEM),
        scratch_shapes=list(SCRATCH.values()),
        compiler_params=pltpu.CompilerParams(
            collective_id=0, has_side_effects=True, vmem_limit_bytes=64 * 1024 * 1024
        ),
        name="vcycle",
    )(*flat)
    return whole.reshape(16, 16, 128)


def solution(mesh):
    placed = P("gx", "gy", "gz")
    return jax.shard_map(
        shards, mesh=mesh, in_specs=(placed,) * 4, out_specs=placed, check_vma=False
    )
```

```python
import jax
import jax.numpy as jnp
from jax import lax
from jax.experimental import pallas as pl
from jax.experimental.pallas import tpu as pltpu
from jax.sharding import PartitionSpec as P

RELAX = 2.0 / 3.0
THIRD = 1.0 / 3.0
COARSE_SWEEPS = 24
GX, GY, GZ = 4, 8, 8
F32 = jnp.float32
MESH = pl.DeviceIdType.MESH

FACES = [(1, 0, 0), (-1, 0, 0), (0, 1, 0), (0, -1, 0), (0, 0, 1), (0, 0, -1)]
DOWN = [(-1, 0, 0), (0, -1, 0), (0, 0, -1)]
RING_Z = [(0, 0, k) for k in (4, 3, 5, 2, 6, 1, 7)]
RING_Y = [(0, k, 0) for k in (4, 3, 5, 2, 6, 1, 7)]
AROUND = [
    (x, y, z) for x in (1, -1, 0) for y in (1, -1, 0) for z in (1, -1, 0) if (x, y, z) != (0, 0, 0)
]
AROUND.sort(key=lambda d: -(abs(d[0]) + abs(d[1]) + abs(d[2])))
LINE = [(2, 0, 0), (1, 0, 0), (3, 0, 0)]
FRIENDS = [(0, 0, 4), (0, 0, 3), (0, 0, 5), (0, 0, 2), (0, 0, 6)] + FACES
SIDES = [(0, 1, 0), (0, -1, 0)]
PLANE = [(2, 1, 0), (2, -1, 0), (1, 1, 0), (1, -1, 0), (3, 1, 0), (3, -1, 0)]
PLANE += [(2, 0, 0), (0, 1, 0), (0, -1, 0), (1, 0, 0), (3, 0, 0)]


def lanes(rows):
    return lax.broadcasted_iota(jnp.int32, (rows, 128), 1)


def sublanes(rows):
    return lax.broadcasted_iota(jnp.int32, (rows, 128), 0)


def turn(value, steps, axis=1):
    steps %= value.shape[axis]
    return value if steps == 0 else pltpu.roll(value, steps, axis)


def take(value, index):
    return jnp.take_along_axis(value, index, axis=1, mode="promise_in_bounds")


class Block:
    def __init__(self, size_x, size_y, size_z, weight):
        self.X, self.Y, self.Z, self.weight = size_x, size_y, size_z, weight
        self.pitch = size_y + 8
        self.rows = size_x * size_y
        self.padded = 8 + (size_x + 2) * self.pitch

    def base(self, i):
        return 8 + (i + 1) * self.pitch

    def own(self, i):
        return pl.ds(i * self.Y, self.Y)

    def at(self, i, shift=0):
        return pl.ds(self.base(i) + shift, self.Y)

    def row_of_each(self, y):
        return pl.ds(self.base(0) + y, self.X, stride=self.pitch)


B0 = Block(16, 16, 128, 1.0)

SCRATCH = {}


def vmem(name, *shape):
    SCRATCH[name] = pltpu.VMEM(shape, F32)


def dma(name, *shape):
    SCRATCH[name] = pltpu.SemaphoreType.DMA(shape)


for key in ("rhs", "fx", "fy", "fz"):
    vmem(key, 256, 128)
dma("in_sem", 5)
for key in ("cxl0", "cxu0", "cyl0", "cyu0", "czl0", "czu0", "g0", "d150", "kw0", "r0", "w0"):
    vmem(key, 256, 128)
vmem("va0", B0.padded, 128)
vmem("vb0", B0.padded, 128)
vmem("lyp0", B0.X * B0.pitch, 128)
for key in ("fx1", "fy1", "fz1", "r1"):
    vmem(key, 64, 128)
for key in ("cxl1", "cxu1", "cyl1", "cyu1", "czl1", "czu1", "g1", "d151", "kw1"):
    vmem(key, 17 * 16, 128)
for key in ("va1", "vb1"):
    vmem(key, 19 * 16, 128)
vmem("ext1", 4, 17 * 16, 128)
vmem("hw_own", 5, 8, 8, 128)
vmem("hw_pack", 3, 8, 8, 128)
vmem("hw_low", 3, 4, 8, 128)
vmem("hw_high", 3, 4, 8, 128)
vmem("hw_zed", 2, 8, 128)
vmem("hw_xr", 2, 3, 3, 8, 128)
vmem("hw_yr", 6, 3, 4, 8, 128)
vmem("hw_zr", 18, 8, 128)
dma("hw_ss", 26)
dma("hw_rs", 26)
vmem("q1", 8 * 16, 128)
for key, rows, count in (("a0", 16, 3), ("b", 16, 6), ("c", 16, 6), ("a1", 8, 3), ("d", 8, 6), ("e", 8, 6)):
    vmem(f"{key}_snd", count, rows, 128)
    vmem(f"{key}_rcv", count, rows, 128)
    dma(f"{key}_ss", count)
    dma(f"{key}_rs", count)
vmem("t0", 256, 128)
vmem("hh_snd", 6, 7, 16, 128)
vmem("hh_rcv", 6, 7, 16, 128)
dma("hh_ss", 6)
dma("hh_rs", 6)
vmem("side1", 6, 16, 128)
vmem("wide1", 6, 4, 16, 128)
vmem("t16", 3, 16, 128)
vmem("zf_snd", 16, 128)
vmem("zf_rcv", 7, 16, 128)
vmem("xf_snd", 6, 16, 128)
vmem("xf_rcv", 3, 6, 16, 128)
vmem("nf_snd", 3, 2, 8, 8, 128)
vmem("nf_rcv", 2, 3, 2, 8, 8, 128)
vmem("zr_snd", 16, 128)
vmem("zr_rcv", 7, 16, 128)
vmem("xr_snd", 2, 16, 128)
vmem("xr_rcv", 11, 2, 16, 128)
for key, count in (("zf", 7), ("zr", 7), ("xr", 11), ("xf", 3), ("nf", 2)):
    dma(f"{key}_ss", count)
    dma(f"{key}_rs", count)
for key in ("f2", "lx2", "ly2", "lz2", "va2", "vb2"):
    vmem(key, 2, 20, 16, 128)
for key in ("cxl2", "cxu2", "cyl2", "cyu2", "czl2", "czu2", "g2", "d152", "kw2"):
    vmem(key, 2, 20, 16, 128)
vmem("nv_snd", 1, 2, 8, 8, 128)
vmem("nv_rcv", 2, 1, 2, 8, 8, 128)
dma("nv_ss", 2)
dma("nv_rs", 2)
vmem("s2", 128, 128)
vmem("p2", 256, 128)
vmem("face3", 3, 128, 128)
vmem("f3", 128, 128)
for key in ("yf", "yr"):
    dma(f"{key}_ss", 7)
    dma(f"{key}_rs", 7)
for key in ("cxl3", "cxu3", "cyl3", "cyu3", "czl3", "czu3", "g3", "d153", "kw3", "r3", "p3"):
    vmem(key, 128, 128)
vmem("va3", 160, 128)
vmem("vb3", 160, 128)
for key in ("t4", "cxl4", "cxu4", "cyl4", "cyu4", "czl4", "czu4", "d154", "kw4", "r4", "p4"):
    vmem(key, 32, 128)
vmem("fc4", 3, 32, 128)
for key in ("t5", "cx5", "cyl5", "cyu5", "czl5", "czu5", "kw5", "e5"):
    vmem(key, 8, 128)


class Space:
    pass


def cycle(rhs_in, fx_in, fy_in, fz_in, out, *scratch):
    s = Space()
    for name, ref in zip(SCRATCH, scratch):
        setattr(s, name, ref)
    gx, gy, gz = lax.axis_index("gx"), lax.axis_index("gy"), lax.axis_index("gz")

    def peer(offset):
        return (
            (gx + offset[0]) & (GX - 1),
            (gy + offset[1]) & (GY - 1),
            (gz + offset[2]) & (GZ - 1),
        )

    loads = [
        pltpu.make_async_copy(source, target, s.in_sem.at[k])
        for k, (source, target) in enumerate(
            ((fx_in, s.fx), (fy_in, s.fy), (fz_in, s.fz), (rhs_in, s.rhs))
        )
    ]
    for load in loads:
        load.start()

    barrier = pltpu.get_barrier_semaphore()
    for offset in FRIENDS:
        pl.semaphore_signal(barrier, inc=1, device_id=peer(offset), device_id_type=MESH)

    def copies(offsets, sources, targets, ss, rs, first=0):
        made = [
            pltpu.make_async_remote_copy(
                src_ref=sources(k),
                dst_ref=targets(k),
                send_sem=ss.at[k],
                recv_sem=rs.at[k],
                device_id=peer(offset),
                device_id_type=MESH,
            )
            for k, offset in enumerate(offsets, first)
        ]
        for one in made:
            one.start()
        return made

    sent = []

    def finish(made):
        for one in made:
            one.wait_recv()
        sent.extend(made)

    def drain():
        for one in sent:
            one.wait_send()
        sent.clear()

    def flag(condition):
        return jnp.where(condition, 1.0, 0.0).astype(F32)

    low_x, low_y, low_z = flag(gx > 0), flag(gy > 0), flag(gz > 0)
    top_x, top_y, top_z = flag(gx < GX - 1), flag(gy < GY - 1), flag(gz < GZ - 1)


    def pack(read, rows, count, column):
        packed = jnp.zeros((rows, 128), F32)
        lane = lanes(rows)
        for i in range(count):
            packed = jnp.where(lane == i, turn(read(i), i - column), packed)
        return packed

    def send_faces(block, ref, key):
        snd, rcv = getattr(s, key + "_snd"), getattr(s, key + "_rcv")
        snd[0] = ref[block.at(block.X - 1)]
        snd[1] = ref[block.at(0)]
        snd[2] = ref[block.row_of_each(block.Y - 1)]
        snd[3] = ref[block.row_of_each(0)]
        sems = getattr(s, key + "_ss"), getattr(s, key + "_rs")
        ends = (lambda k: snd.at[k], lambda k: rcv.at[k], *sems)
        made = copies(FACES[:4], *ends)
        snd[4] = pack(lambda i: ref[block.at(i)], 16, 16, 127)
        snd[5] = pack(lambda i: ref[block.at(i)], 16, 16, 0)
        return made + copies(FACES[4:], *ends, first=4)

    def fill(block, ref, halo):
        ref[block.at(-1)] = halo[0]
        ref[block.at(block.X)] = halo[1]
        ref[block.row_of_each(-1)] = halo[2]
        ref[block.row_of_each(block.Y)] = halo[3]

    def send_upper(lx, ly, lz, key):
        block = B0
        snd = getattr(s, key + "_snd")
        snd[0] = lx[block.own(0)]
        snd[1] = ly[pl.ds(0, block.X, stride=block.Y)]
        snd[2] = pack(lambda i: lz[block.own(i)], 16, 16, 0)
        rcv = getattr(s, key + "_rcv")
        pl.semaphore_wait(barrier, len(FRIENDS))
        return copies(
            DOWN,
            lambda k: snd.at[k],
            lambda k: rcv.at[k],
            getattr(s, key + "_ss"),
            getattr(s, key + "_rs"),
        )

    def coefficients(level, lx, ly, lz, key):
        block = B0
        rcv = getattr(s, key + "_rcv")
        lyp = getattr(s, f"lyp{level}")
        c = {k: getattr(s, f"{k}{level}") for k in ("cxl", "cxu", "cyl", "cyu", "czl", "czu")}
        d15, kw = getattr(s, f"d15{level}"), getattr(s, f"kw{level}")
        for i in range(block.X):
            lyp[pl.ds(i * block.pitch, block.Y)] = ly[block.own(i)]
        lyp[pl.ds(block.Y, block.X, stride=block.pitch)] = rcv[1] * top_y
        next_x = rcv[0] * top_x
        next_z = rcv[2] * top_z
        lane, row = lanes(block.Y), sublanes(block.Y)
        keep_y = jnp.where(row == 0, low_y, 1.0)
        keep_z = jnp.where(lane == 0, low_z, 1.0)
        for i in range(block.X):
            own = block.own(i)
            a_xl = lx[own]
            a_xu = lx[block.own(i + 1)] if i + 1 < block.X else next_x
            a_yl = ly[own]
            a_yu = lyp[pl.ds(i * block.pitch + 1, block.Y)]
            a_zl = lz[own]
            a_zu = jnp.where(
                lane == block.Z - 1, turn(next_z, block.Z - 1 - i), turn(a_zl, -1)
            )
            total = (a_xl + a_yl + a_zl) + (a_xu + a_yu + a_zu)
            scale = RELAX / total
            d15[own] = (1.5 * block.weight) * total
            kw[own] = scale * (1.0 / block.weight)
            c["cxl"][own] = scale * a_xl * (low_x if i == 0 else 1.0)
            c["cxu"][own] = scale * a_xu
            c["cyl"][own] = scale * a_yl * keep_y
            c["cyu"][own] = scale * a_yu
            c["czl"][own] = scale * a_zl * keep_z
            c["czu"][own] = scale * a_zu

    def stencil(level, ref, low, high, emit):
        block = B0
        lane = lanes(block.Y)
        get = lambda k: getattr(s, f"{k}{level}")
        for i in range(block.X):
            own = block.own(i)
            v = ref[block.at(i)]
            down = jnp.where(lane == 0, turn(low, -i), turn(v, 1))
            up = jnp.where(lane == block.Z - 1, turn(high, block.Z - 1 - i), turn(v, -1))
            t_x = get("cxl")[own] * ref[block.at(i - 1)] + get("cxu")[own] * ref[block.at(i + 1)]
            t_y = get("cyl")[own] * ref[block.at(i, -1)] + get("cyu")[own] * ref[block.at(i, 1)]
            t_z = get("czl")[own] * down + get("czu")[own] * up
            emit(i, v, get("g")[own] + (t_x + t_y + t_z))

    def smooth(level, source, target, low, high):
        block = B0

        def emit(i, v, total):
            target[block.at(i)] = v * THIRD + total

        stencil(level, source, low, high, emit)

    def residual(level, source, low, high):
        block = B0
        d15, r = getattr(s, f"d15{level}"), getattr(s, f"r{level}")

        def emit(i, v, total):
            r[block.own(i)] = d15[block.own(i)] * (total - RELAX * v)
            s.t0[block.own(i)] = v * THIRD + total

        stencil(level, source, low, high, emit)


    lane8, lane16 = lanes(8), lanes(16)
    row8, row16 = sublanes(8), sublanes(16)
    upper_half = row8 < 4
    slices_x = {1: (5, 3), -1: (0, 3), 0: (0, 8)}
    pairs_x = {1: (2, 2), -1: (0, 2), 0: (0, 4)}
    flat_yr = [(x, y) for x in (1, -1, 0) for y in (1, -1)]
    flat_zr = [(x, y, z) for x in (1, -1, 0) for y in (1, -1, 0) for z in (1, -1)]

    def pack_around():
        zeds = [jnp.zeros((8, 128), F32)] * 2
        group = lane8 // 3
        for a in range(5):
            for x in range(8):
                v, place = s.hw_own[a, x], 8 * a + x
                zeds = [
                    jnp.where(group == place, turn(v, 3 * place - first), zed)
                    for zed, first in zip(zeds, (61, 0))
                ]
        s.hw_zed[0], s.hw_zed[1] = zeds
        for t in range(3):
            tiles = []
            for x in range(8):
                v = s.hw_own[2 * t, x]
                if t < 2:
                    v = jnp.where(lane8 < 64, v, turn(s.hw_own[2 * t + 1, x], 64))
                s.hw_pack[t, x] = v
                tiles.append(v)
            for i in range(4):
                even, odd = tiles[2 * i], tiles[2 * i + 1]
                s.hw_low[t, i] = jnp.where(upper_half, even, turn(odd, 4, 0))
                s.hw_high[t, i] = jnp.where(upper_half, turn(even, 4, 0), odd)

    def send_around():
        def source(k):
            x, y, z = AROUND[k]
            if z != 0:
                return s.hw_zed.at[0 if z > 0 else 1]
            if y != 0:
                return (s.hw_low if y < 0 else s.hw_high).at[:, pl.ds(*pairs_x[x])]
            return s.hw_pack.at[:, pl.ds(*slices_x[x])]

        def target(k):
            x, y, z = AROUND[k]
            if z != 0:
                return s.hw_zr.at[flat_zr.index((x, y, z))]
            if y != 0:
                return s.hw_yr.at[flat_yr.index((x, y)), :, pl.ds(0, pairs_x[x][1])]
            return s.hw_xr.at[0 if x > 0 else 1]

        return copies(AROUND, source, target, s.hw_ss, s.hw_rs)

    def assemble(a, k):
        x = k - 4
        if x < 0:
            d, layer, first = 1, x + 8, 5
        elif x < 8:
            d, layer, first = 0, x, 0
        else:
            d, layer, first = -1, x - 8, 0
        place = 3 * (8 * a + layer)
        t = a // 2
        inner = s.hw_own[a, layer] if d == 0 else s.hw_xr[0 if d > 0 else 1, t, layer - first]
        pair = layer // 2 - pairs_x[d][0]
        above = s.hw_yr[flat_yr.index((d, -1)), t, pair]
        below = s.hw_yr[flat_yr.index((d, 1)), t, pair]
        if layer % 2 == 0:
            below = turn(below, 4, 0)
        else:
            above = turn(above, 4, 0)
        outer = jnp.where(upper_half, above, below)
        if a % 2 == 1:
            outer = turn(outer, 64)
            inner = inner if d == 0 else turn(inner, 64)
        whole = jnp.concatenate([inner, outer], axis=0)

        def side(z):
            zed = lambda y: s.hw_zr[flat_zr.index((d, y, z))]
            outer = jnp.where(upper_half, zed(-1), zed(1))
            return jnp.concatenate([zed(0), outer], axis=0)

        whole = jnp.where((lane16 >= 64) & (lane16 < 72), turn(side(-1), 64 - place), whole)
        return jnp.where(lane16 >= 120, turn(side(1), 125 - place), whole)

    def ext1(k):
        return pl.ds(16 * k, 16)

    def pad1(k):
        return pl.ds(16 * k + 16, 16)

    def coefficients1(first, last):
        keep_y = jnp.where(row16 == 0, low_y, 1.0)
        keep_z = jnp.where(lane16 == 0, low_z, 1.0)
        last_y = jnp.where(row16 == 7, top_y, 1.0)
        last_z = jnp.where(lane16 == 63, top_z, 1.0)
        for k in range(first, last + 1):
            own = ext1(k)
            a_xl, a_yl, a_zl = s.ext1[0, own], s.ext1[1, own], s.ext1[2, own]
            a_xu = s.ext1[0, ext1(k + 1)]
            if k == 11:
                a_xu = a_xu * top_x
            a_yu = turn(a_yl, -1, 0) * last_y
            a_zu = turn(a_zl, -1) * last_z
            total = (a_xl + a_yl + a_zl) + (a_xu + a_yu + a_zu)
            scale = RELAX / total
            s.kw1[own] = scale * 4.0
            s.d151[own] = (1.5 * 0.25) * total
            s.cxl1[own] = scale * a_xl * (low_x if k == 4 else 1.0)
            s.cxu1[own] = scale * a_xu
            s.cyl1[own] = scale * a_yl * keep_y
            s.cyu1[own] = scale * a_yu
            s.czl1[own] = scale * a_zl * keep_z
            s.czu1[own] = scale * a_zu

    def send_faces1(ref, key):
        snd, rcv = getattr(s, key + "_snd"), getattr(s, key + "_rcv")
        inner = lambda i: ref[pl.ds(16 * (i + 5), 8)]
        snd[0] = inner(7)
        snd[1] = inner(0)
        snd[2] = ref[pl.ds(16 * 5 + 7, 8, stride=16)]
        snd[3] = ref[pl.ds(16 * 5, 8, stride=16)]
        sems = getattr(s, key + "_ss"), getattr(s, key + "_rs")
        ends = (lambda k: snd.at[k], lambda k: rcv.at[k], *sems)
        made = copies(FACES[:4], *ends)
        snd[4] = pack(inner, 8, 8, 63)
        snd[5] = pack(inner, 8, 8, 0)
        return made + copies(FACES[4:], *ends, first=4)

    def fill1(ref, halo):
        low, high = halo[4], halo[5]
        for i in range(8):
            own = pl.ds(16 * (i + 5), 8)
            v = jnp.where(lane8 == 64, turn(high, 64 - i), ref[own])
            ref[own] = jnp.where(lane8 == 127, turn(low, 127 - i), v)
        ref[pl.ds(16 * 4, 8)] = halo[0]
        ref[pl.ds(16 * 13, 8)] = halo[1]
        ref[pl.ds(16 * 5 + 15, 8, stride=16)] = halo[2]
        ref[pl.ds(16 * 5 + 8, 8, stride=16)] = halo[3]

    def stencil1(first, last, ref, emit):
        for k in range(first, last + 1):
            own = ext1(k)
            v = ref[pad1(k)]
            t_x = s.cxl1[own] * ref[pad1(k - 1)] + s.cxu1[own] * ref[pad1(k + 1)]
            t_y = s.cyl1[own] * turn(v, 1, 0) + s.cyu1[own] * turn(v, -1, 0)
            t_z = s.czl1[own] * turn(v, 1) + s.czu1[own] * turn(v, -1)
            emit(k, v, s.g1[own] + (t_x + t_y + t_z))

    def smooth1(first, last, source, target):
        def emit(k, v, total):
            target[pad1(k)] = v * THIRD + total

        stencil1(first, last, source, emit)

    even8 = (2 * lane8) & 127
    half16 = lane16 >> 1

    def pair_z(value):
        return value + turn(value, -1)

    def stage_z(arrays, snd):
        group = lane16 >> 4
        packed = jnp.zeros((16, 128), F32)
        for a in range(arrays):
            whole = s.t16[a]
            for p in range(2):
                moved = take(whole, 4 * (lane16 & 15) + 2 * p)
                packed = jnp.where(group == ((gz + 2 * a + p) & 7), moved, packed)
        snd[...] = packed

    def merge_z(arrays, own, others, target):
        group = lane16 >> 4
        parts = [(0, own)] + [(RING_Z[k][2], others(k)) for k in range(7)]
        for q in range(2 * arrays):
            merged = jnp.zeros((16, 128), F32)
            for distance, part in parts:
                merged = jnp.where(group == ((gz - distance + q) & 7), part, merged)
            target[q] = turn(merged, -16 * q)

    for load in loads[:3]:
        load.wait()
    round_a0 = send_upper(s.fx, s.fy, s.fz, "a0")

    for i in range(8):
        own = pl.ds(8 * i, 8)
        here = lambda ref, shift: ref[pl.ds(32 * i + shift, 8, stride=2)]
        s.fx1[own] = take(pair_z(here(s.fx, 0) + here(s.fx, 1)), even8) * 0.25
        s.fy1[own] = take(pair_z(here(s.fy, 0) + here(s.fy, 16)), even8) * 0.25
        total = (here(s.fz, 0) + here(s.fz, 1)) + (here(s.fz, 16) + here(s.fz, 17))
        s.fz1[own] = take(total, even8) * 0.25
    s.a1_snd[0] = s.fx1[pl.ds(0, 8)]
    s.a1_snd[1] = s.fy1[pl.ds(0, 8, stride=8)]
    s.a1_snd[2] = pack(lambda i: s.fz1[pl.ds(8 * i, 8)], 8, 8, 0)
    round_a1 = copies(
        DOWN, lambda k: s.a1_snd.at[k], lambda k: s.a1_rcv.at[k], s.a1_ss, s.a1_rs
    )
    for i in range(4):
        own = pl.ds(4 * i, 4)
        here = lambda ref, shift: ref[pl.ds(16 * i + shift, 4, stride=2)]
        s.t16[0, own] = here(s.fx1, 0) + here(s.fx1, 1)
        s.t16[1, own] = here(s.fy1, 0) + here(s.fy1, 8)
        total = (here(s.fz1, 0) + here(s.fz1, 1)) + (here(s.fz1, 8) + here(s.fz1, 9))
        s.t16[2, own] = total * 0.25
    s.t16[0] = pair_z(s.t16[0]) * 0.25
    s.t16[1] = pair_z(s.t16[1]) * 0.25
    stage_z(3, s.zf_snd)
    round_zf = copies(
        RING_Z, lambda k: s.zf_snd, lambda k: s.zf_rcv.at[k], s.zf_ss, s.zf_rs
    )
    for p in range(2):
        for x in (0, 1, 18, 19):
            for ref in (s.va2, s.vb2):
                ref[p, x] = jnp.zeros((16, 128), F32)
        for x in range(16):
            s.f2[p, x + 2] = jnp.zeros((16, 128), F32)
    for ref in (s.va3, s.vb3):
        for k in range(2):
            ref[pl.ds(8 * k, 8)] = jnp.zeros((8, 128), F32)
            ref[pl.ds(144 + 8 * k, 8)] = jnp.zeros((8, 128), F32)
    s.p2[...] = jnp.zeros_like(s.p2)
    s.ext1[...] = jnp.ones_like(s.ext1)
    for k in (0, 1, 2, 3, 12, 13, 14, 15):
        s.va1[pad1(k)] = jnp.zeros((16, 128), F32)
        s.vb1[pad1(k)] = jnp.zeros((16, 128), F32)

    loads[3].wait()
    finish(round_a0)
    coefficients(0, s.fx, s.fy, s.fz, "a0")
    for i in range(16):
        own = B0.own(i)
        start = s.kw0[own] * s.rhs[own]
        s.g0[own] = start
        s.va0[B0.at(i)] = start
    round_b = send_faces(B0, s.va0, "b")
    finish(round_a1)
    for i in range(8):
        own, here = pl.ds(8 * i, 8), pl.ds(16 * (i + 4), 8)
        s.ext1[0, here] = s.fx1[own]
        s.ext1[1, here] = s.fy1[own]
        upper = turn(s.a1_rcv[2], 64 - i)
        s.ext1[2, here] = jnp.where(lane8 == 64, upper, s.fz1[own])
        s.hw_own[0, i] = s.fx1[own]
        s.hw_own[1, i] = s.fy1[own]
        s.hw_own[2, i] = s.fz1[own]
    s.ext1[0, pl.ds(16 * 12, 8)] = s.a1_rcv[0]
    s.ext1[1, pl.ds(16 * 4 + 8, 8, stride=16)] = s.a1_rcv[1]
    coefficients1(4, 11)
    finish(round_zf)
    merge_z(3, s.zf_snd[...], lambda k: s.zf_rcv[k], s.xf_snd)
    finish(round_b)
    fill(B0, s.va0, s.b_rcv)
    smooth(0, s.va0, s.vb0, s.b_rcv[4], s.b_rcv[5])
    round_c = send_faces(B0, s.vb0, "c")
    round_xf = copies(
        LINE, lambda k: s.xf_snd, lambda k: s.xf_rcv.at[k], s.xf_ss, s.xf_rs
    )
    finish(round_c)
    fill(B0, s.vb0, s.c_rcv)
    residual(0, s.vb0, s.c_rcv[4], s.c_rcv[5])

    for i in range(8):
        here = lambda shift: s.r0[pl.ds(32 * i + shift, 8, stride=2)]
        total = (here(0) + here(1)) + (here(16) + here(17))
        forcing = take(pair_z(total), even8) * 0.125
        s.hw_own[3, i] = forcing
        start = s.kw1[pl.ds(16 * (i + 4), 8)] * forcing
        s.g1[pl.ds(16 * (i + 4), 8)] = start
        s.g1[pl.ds(16 * (i + 4) + 8, 8)] = jnp.zeros((8, 128), F32)
        s.va1[pl.ds(16 * (i + 5), 8)] = start
        s.va1[pl.ds(16 * (i + 5) + 8, 8)] = jnp.zeros((8, 128), F32)

    def block2(p, x):
        return (p, x + 2)

    def spread(arrays, offsets, snd, rcv, targets):
        parts = [((0, 0, 0), lambda q: snd.at[q])]
        for k, offset in enumerate(offsets):
            parts.append((offset, lambda q, k=k: rcv.at[k, q]))
        for offset, part in parts:
            first = 4 * ((gx - offset[0]) & 3)
            place = pl.ds(4 * (1 - offset[1]), 4)
            for a in range(arrays):
                for p in range(2):
                    for x in range(4):
                        piece = part(2 * a + p)[pl.ds(4 * x, 4)]
                        targets[a][p, x + 2 + first, place] = piece

    def send_sides(refs, key):
        snd, rcv = getattr(s, key + "_snd"), getattr(s, key + "_rcv")
        for a, ref in enumerate(refs):
            for p in range(2):
                for i in range(8):
                    even = ref[p, 2 * i + 2, pl.ds(0, 8)]
                    odd = ref[p, 2 * i + 3, pl.ds(0, 8)]
                    snd[a, p, i] = jnp.where(upper_half, turn(even, 4, 0), odd)
        return copies(
            SIDES,
            lambda k: snd,
            lambda k: rcv.at[k],
            getattr(s, key + "_ss"),
            getattr(s, key + "_rs"),
        )

    def take_sides(refs, key, rest):
        rcv = getattr(s, key + "_rcv")
        for a, ref in enumerate(refs):
            for p in range(2):
                for x in range(16):
                    below, above = rcv[0, a, p, x // 2], rcv[1, a, p, x // 2]
                    if x % 2 == 1:
                        below, above = turn(below, 4, 0), turn(above, 4, 0)
                    own = ref[p, x + 2, pl.ds(0, 8)]
                    ref[p, x + 2, pl.ds(0, 8)] = jnp.where(upper_half, below, own)
                    ref[p, x + 2, pl.ds(8, 8)] = jnp.where(upper_half, above, rest)

    faces2 = (s.lx2, s.ly2, s.lz2)
    global_y = row16 + 4 * gy - 4
    not_low, not_top = global_y != 0, global_y != 4 * GY - 1

    round_d = send_faces1(s.va1, "d")
    mine = pl.ds(pl.multiple_of(16 * gy, 16), 16)

    finish(round_xf)
    spread(3, LINE, s.xf_snd, s.xf_rcv, faces2)
    round_nf = send_sides(faces2, "nf")
    for a, ref in enumerate((s.lx2, s.ly2, s.lz2)):
        for i in range(8):
            total = ref[block2(0, 2 * i)]
            if a != 2:
                total = total + ref[block2(1, 2 * i)]
            if a != 0:
                total = total + ref[block2(0, 2 * i + 1)]
            if a == 1:
                total = total + ref[block2(1, 2 * i + 1)]
            s.s2[pl.ds(16 * i, 16)] = total
        for j in range(2):
            total = s.s2[pl.ds(4 + 2 * j, 8, stride=16)]
            if a != 1:
                total = total + s.s2[pl.ds(5 + 2 * j, 8, stride=16)]
            s.face3[a, pl.ds(pl.multiple_of(16 * gy + 8 * j, 8), 8)] = total * 0.25
    round_yf = copies(
        RING_Y,
        lambda k: s.face3.at[:, mine],
        lambda k: s.face3.at[:, mine],
        s.yf_ss,
        s.yf_rs,
    )
    finish(round_d)
    fill1(s.va1, s.d_rcv)
    smooth1(4, 11, s.va1, s.vb1)
    for i in range(8):
        s.hw_own[4, i] = s.vb1[pl.ds(16 * (i + 5), 8)]
    round_e = send_faces1(s.vb1, "e")
    kept = (s.t0, s.cxl0, s.cxu0, s.cyl0, s.cyu0, s.czl0, s.czu0)
    for a, ref in enumerate(kept):
        s.hh_snd[0, a] = ref[B0.own(15)]
        s.hh_snd[1, a] = ref[B0.own(0)]
        s.hh_snd[2, a] = ref[pl.ds(15, 16, stride=16)]
        s.hh_snd[3, a] = ref[pl.ds(0, 16, stride=16)]
        s.hh_snd[4, a] = pack(lambda i: ref[B0.own(i)], 16, 16, 127)
        s.hh_snd[5, a] = pack(lambda i: ref[B0.own(i)], 16, 16, 0)
    pack_around()

    finish(round_e)
    fill1(s.vb1, s.e_rcv)

    def emit_r1(k, v, total):
        r = s.d151[ext1(k)] * (total - RELAX * v)
        s.r1[pl.ds(8 * (k - 4), 8)] = r[0:8]

    stencil1(4, 11, s.vb1, emit_r1)
    for i in range(4):
        here = lambda shift: s.r1[pl.ds(16 * i + shift, 4, stride=2)]
        s.t16[0, pl.ds(4 * i, 4)] = (here(0) + here(1)) + (here(8) + here(9))
    s.t16[0] = pair_z(s.t16[0]) * 0.125
    stage_z(1, s.zr_snd)
    round_zr = copies(
        RING_Z, lambda k: s.zr_snd, lambda k: s.zr_rcv.at[k], s.zr_ss, s.zr_rs
    )


    def stencil2(ref, emit):
        for p in range(2):
            for x in range(16):
                j, other = block2(p, x), block2(1 - p, x)
                v, w = ref[j], ref[other]
                t_x = s.cxl2[j] * ref[block2(p, x - 1)] + s.cxu2[j] * ref[block2(p, x + 1)]
                t_y = s.cyl2[j] * turn(v, 1, 0) + s.cyu2[j] * turn(v, -1, 0)
                down, up = (turn(w, 1), w) if p == 0 else (w, turn(w, -1))
                t_z = s.czl2[j] * down + s.czu2[j] * up
                emit(j, v, s.g2[j] + (t_x + t_y + t_z))

    def smooth2(source, target):
        def emit(j, v, total):
            target[j] = v * THIRD + total

        stencil2(source, emit)

    round_hw = send_around()
    finish(round_nf)
    take_sides(faces2, "nf", 1.0)
    for p in range(2):
        for x in range(16):
            j = block2(p, x)
            a_xl, a_yl, a_zl = s.lx2[j], s.ly2[j], s.lz2[j]
            a_xu = s.lx2[block2(p, x + 1)] if x < 15 else jnp.zeros((16, 128), F32)
            a_yu = jnp.where(not_top, turn(a_yl, -1, 0), 0.0)
            if p == 0:
                a_zu = s.lz2[block2(1, x)]
            else:
                a_zu = jnp.where(lane16 == 127, 0.0, turn(s.lz2[block2(0, x)], -1))
            total = (a_xl + a_yl + a_zl) + (a_xu + a_yu + a_zu)
            scale = RELAX / total
            s.d152[j] = (1.5 * 0.0625) * total
            s.kw2[j] = scale * 16.0
            s.cxl2[j] = scale * a_xl if x > 0 else jnp.zeros((16, 128), F32)
            s.cxu2[j] = scale * a_xu
            s.cyl2[j] = jnp.where(not_low, scale * a_yl, 0.0)
            s.cyu2[j] = scale * a_yu
            s.czl2[j] = scale * a_zl if p == 1 else jnp.where(lane16 == 0, 0.0, scale * a_zl)
            s.czu2[j] = scale * a_zu

    finish(round_zr)
    merge_z(1, s.zr_snd[...], lambda k: s.zr_rcv[k], s.xr_snd)
    round_xr = copies(
        PLANE, lambda k: s.xr_snd, lambda k: s.xr_rcv.at[k], s.xr_ss, s.xr_rs
    )

    finish(round_yf)
    zero8 = jnp.zeros((8, 128), F32)
    for y in range(16):
        own = pl.ds(8 * y, 8)
        a_xl, a_yl, a_zl = s.face3[0, own], s.face3[1, own], s.face3[2, own]
        a_xu = jnp.where(row8 == 7, 0.0, turn(a_xl, -1, 0))
        a_yu = s.face3[1, pl.ds(8 * y + 8, 8)] if y < 15 else zero8
        a_zu = jnp.where(lane8 == 127, 0.0, turn(a_zl, -1))
        total = (a_xl + a_yl + a_zl) + (a_xu + a_yu + a_zu)
        scale = RELAX / total
        s.d153[own] = (1.5 * 0.25**3) * total
        s.kw3[own] = scale * 64.0
        s.cxl3[own] = jnp.where(row8 == 0, 0.0, scale * a_xl)
        s.cxu3[own] = scale * a_xu
        s.cyl3[own] = scale * a_yl if y > 0 else zero8
        s.cyu3[own] = scale * a_yu
        s.czl3[own] = jnp.where(lane8 == 0, 0.0, scale * a_zl)
        s.czu3[own] = scale * a_zu

    lane32, row32 = lanes(32), sublanes(32)

    def both(value, lane, step):
        return value + jnp.where(
            (lane & step) == 0, turn(value, -step), turn(value, step)
        )

    def lower_of(value, lane, step):
        return jnp.where((lane & step) == 0, value, turn(value, step))

    for a in range(3):
        for y in range(8):
            here = lambda shift: s.face3[a, pl.ds(16 * y + shift, 4, stride=2)]
            if a == 0:
                total = here(0) + here(8)
            elif a == 1:
                total = here(0) + here(1)
            else:
                total = (here(0) + here(1)) + (here(8) + here(9))
            s.t4[pl.ds(4 * y, 4)] = total
        total = s.t4[...]
        total = both(total, lane32, 1) if a < 2 else lower_of(total, lane32, 1)
        s.fc4[a] = total * 0.25
    a_xl, a_yl, a_zl = s.fc4[0], s.fc4[1], s.fc4[2]
    a_xu = jnp.where((row32 & 3) == 3, 0.0, turn(a_xl, -1, 0))
    a_yu = jnp.where(row32 >= 28, 0.0, turn(a_yl, -4, 0))
    a_zu = jnp.where(lane32 >= 126, 0.0, turn(a_zl, -2))
    total = (a_xl + a_yl + a_zl) + (a_xu + a_yu + a_zu)
    scale = RELAX / total
    s.d154[...] = (1.5 * 0.25**4) * total
    s.kw4[...] = scale * 256.0
    s.cxl4[...] = jnp.where((row32 & 3) == 0, 0.0, scale * a_xl)
    s.cxu4[...] = scale * a_xu
    s.cyl4[...] = jnp.where(row32 < 4, 0.0, scale * a_yl)
    s.cyu4[...] = scale * a_yu
    s.czl4[...] = jnp.where(lane32 < 2, 0.0, scale * a_zl)
    s.czu4[...] = scale * a_zu

    faces5 = []
    for a in range(3):
        for x in range(2):
            here = lambda shift: s.fc4[a, pl.ds(2 * x + shift, 4, stride=8)]
            if a == 0:
                total = here(0) + here(4)
            elif a == 1:
                total = here(0) + here(1)
            else:
                total = (here(0) + here(1)) + (here(4) + here(5))
            s.t5[pl.ds(4 * x, 4)] = total
        total = s.t5[...]
        total = both(total, lane8, 2) if a < 2 else lower_of(total, lane8, 2)
        faces5.append(total * 0.25)
    a_xl, a_yl, a_zl = faces5
    a_xu = jnp.where(row8 >= 4, 0.0, turn(a_xl, 4, 0))
    a_yu = jnp.where((row8 & 3) == 3, 0.0, turn(a_yl, -1, 0))
    a_zu = jnp.where(lane8 >= 124, 0.0, turn(a_zl, -4))
    total = (a_xl + a_yl + a_zl) + (a_xu + a_yu + a_zu)
    scale = RELAX / total
    s.kw5[...] = scale * 1024.0
    s.cx5[...] = jnp.where(row8 >= 4, scale * a_xl, scale * a_xu)
    s.cyl5[...] = jnp.where((row8 & 3) == 0, 0.0, scale * a_yl)
    s.cyu5[...] = scale * a_yu
    s.czl5[...] = jnp.where(lane8 < 4, 0.0, scale * a_zl)
    s.czu5[...] = scale * a_zu

    finish(round_xr)
    spread(1, PLANE, s.xr_snd, s.xr_rcv, (s.f2,))
    for p in range(2):
        for x in range(16):
            j = block2(p, x)
            start = s.kw2[j] * s.f2[j]
            s.g2[j] = start
            s.va2[j] = start
    smooth2(s.va2, s.vb2)

    def emit_r2(j, v, total):
        s.f2[j] = s.d152[j] * (total - RELAX * v)

    stencil2(s.vb2, emit_r2)
    for i in range(8):
        total = (s.f2[block2(0, 2 * i)] + s.f2[block2(1, 2 * i)]) + (
            s.f2[block2(0, 2 * i + 1)] + s.f2[block2(1, 2 * i + 1)]
        )
        s.s2[pl.ds(16 * i, 16)] = total
    for j in range(2):
        total = s.s2[pl.ds(4 + 2 * j, 8, stride=16)] + s.s2[pl.ds(5 + 2 * j, 8, stride=16)]
        s.f3[pl.ds(pl.multiple_of(16 * gy + 8 * j, 8), 8)] = total * 0.125
    round_yr = copies(
        RING_Y, lambda k: s.f3.at[mine], lambda k: s.f3.at[mine], s.yr_ss, s.yr_rs
    )
    round_nv = send_sides((s.vb2,), "nv")
    round_hh = copies(
        FACES, lambda k: s.hh_snd.at[k], lambda k: s.hh_rcv.at[k], s.hh_ss, s.hh_rs
    )

    drain()
    finish(round_hw)
    for k in range(1, 15):
        for a in range(4):
            s.ext1[a, ext1(k)] = assemble(a, k)
        s.vb1[pad1(k)] = assemble(4, k)
    coefficients1(2, 13)
    for k in range(2, 14):
        s.g1[ext1(k)] = s.kw1[ext1(k)] * s.ext1[3, ext1(k)]
    finish(round_yr)

    def at3(y):
        return pl.ds(16 + 8 * y, 8)

    def stencil3(ref, emit):
        for y in range(16):
            own = pl.ds(8 * y, 8)
            v = ref[at3(y)]
            t_x = s.cxl3[own] * turn(v, 1, 0) + s.cxu3[own] * turn(v, -1, 0)
            t_y = s.cyl3[own] * ref[at3(y - 1)] + s.cyu3[own] * ref[at3(y + 1)]
            t_z = s.czl3[own] * turn(v, 1) + s.czu3[own] * turn(v, -1)
            emit(y, v, s.g3[own] + (t_x + t_y + t_z))

    def smooth3(source, target):
        def emit(y, v, total):
            target[at3(y)] = v * THIRD + total

        stencil3(source, emit)

    for y in range(16):
        own = pl.ds(8 * y, 8)
        start = s.kw3[own] * s.f3[own]
        s.g3[own] = start
        s.va3[at3(y)] = start
    smooth3(s.va3, s.vb3)

    def emit_r3(y, v, total):
        own = pl.ds(8 * y, 8)
        s.r3[own] = s.d153[own] * (total - RELAX * v)

    stencil3(s.vb3, emit_r3)
    for y in range(8):
        here = lambda shift: s.r3[pl.ds(16 * y + shift, 4, stride=2)]
        s.t4[pl.ds(4 * y, 4)] = (here(0) + here(1)) + (here(8) + here(9))
    f4 = both(s.t4[...], lane32, 1) * 0.125

    def total4(v):
        t_x = s.cxl4[...] * turn(v, 1, 0) + s.cxu4[...] * turn(v, -1, 0)
        t_y = s.cyl4[...] * turn(v, 4, 0) + s.cyu4[...] * turn(v, -4, 0)
        t_z = s.czl4[...] * turn(v, 2) + s.czu4[...] * turn(v, -2)
        return g4 + (t_x + t_y + t_z)

    g4 = s.kw4[...] * f4
    v4 = g4
    v4 = v4 * THIRD + total4(v4)
    s.r4[...] = s.d154[...] * (total4(v4) - RELAX * v4)
    for x in range(2):
        here = lambda shift: s.r4[pl.ds(2 * x + shift, 4, stride=8)]
        s.t5[pl.ds(4 * x, 4)] = (here(0) + here(1)) + (here(4) + here(5))
    g5 = s.kw5[...] * (both(s.t5[...], lane8, 2) * 0.125)
    cx5, cyl5, cyu5, czl5, czu5 = s.cx5[...], s.cyl5[...], s.cyu5[...], s.czl5[...], s.czu5[...]

    def sweep5(index, v):
        t_y = cyl5 * turn(v, 1, 0) + cyu5 * turn(v, -1, 0)
        t_z = czl5 * turn(v, 4) + czu5 * turn(v, -4)
        return (v * THIRD + g5) + (cx5 * turn(v, 4, 0) + (t_y + t_z))

    s.e5[...] = lax.fori_loop(0, COARSE_SWEEPS - 1, sweep5, g5)
    for x in range(2):
        piece = s.e5[pl.ds(4 * x, 4)]
        for shift in (0, 1, 4, 5):
            s.p4[pl.ds(2 * x + shift, 4, stride=8)] = piece
    v4 = v4 + s.p4[...]
    v4 = v4 * THIRD + total4(v4)
    v4 = v4 * THIRD + total4(v4)
    s.r4[...] = v4
    for x in range(4):
        piece = s.r4[pl.ds(x, 8, stride=4)]
        for shift in (0, 1, 8, 9):
            s.p3[pl.ds(2 * x + shift, 8, stride=16)] = piece
    for y in range(16):
        s.vb3[at3(y)] = s.vb3[at3(y)] + s.p3[pl.ds(8 * y, 8)]
    smooth3(s.vb3, s.va3)
    smooth3(s.va3, s.vb3)

    finish(round_nv)
    take_sides((s.vb2,), "nv", 0.0)
    for k in range(6):
        piece = s.vb3[pl.ds(pl.multiple_of(16 * gy + 8 * k, 8), 8)]
        for x in range(2):
            for y in range(2):
                s.p2[pl.ds(16 * x + 2 * k + y, 8, stride=32)] = piece
    for x in range(16):
        more = s.p2[pl.ds(16 * x, 16)]
        for p in range(2):
            s.vb2[block2(p, x)] = s.vb2[block2(p, x)] + more
    smooth2(s.vb2, s.va2)
    smooth2(s.va2, s.vb2)

    signed = jnp.where(lane16 < 96, lane16, lane16 - 128)
    index = (16 * gz + (signed >> 2)) & 127
    odd = ((signed >> 1) & 1) == 1
    for k in range(8):
        x = 4 * gx + k
        piece = jnp.where(odd, take(s.vb2[1, x], index), take(s.vb2[0, x], index))
        rows = jnp.where(row16 < 6, turn(piece, -4, 0), turn(piece, 4, 0))[0:8]
        for y in range(2):
            s.q1[pl.ds(16 * k + y, 8, stride=2)] = rows
        more = s.q1[pl.ds(16 * k, 16)]
        for i in (2 * k, 2 * k + 1):
            if 1 <= i <= 14:
                s.vb1[pad1(i)] = s.vb1[pad1(i)] + more
    smooth1(2, 13, s.vb1, s.va1)
    smooth1(3, 12, s.va1, s.vb1)
    inner = lambda i: s.vb1[pl.ds(16 * (i + 5), 8)]

    def widen(value, ref, start):
        ref[pl.ds(start, 8, stride=2)] = value
        ref[pl.ds(start + 1, 8, stride=2)] = value
        return take(ref[pl.ds(start, 16)], half16)

    for i in range(8):
        more = widen(inner(i), s.w0, 16 * i)
        for x in (2 * i, 2 * i + 1):
            s.vb0[B0.at(x)] = s.vb0[B0.at(x)] + more

    sides = [s.vb1[pl.ds(16 * 4, 16)], s.vb1[pl.ds(16 * 13, 16)]]
    near = [inner(0), inner(7)]
    for k, row, edge in ((2, 15, 0), (3, 8, 7)):
        s.side1[k, pl.ds(8, 8)] = jnp.zeros((8, 128), F32)
        s.side1[k, pl.ds(0, 8)] = s.vb1[pl.ds(16 * 5 + row, 8, stride=16)]
        s.side1[k, pl.ds(8, 1)] = s.vb1[pl.ds(16 * 13 + row, 1)]
        s.side1[k, pl.ds(15, 1)] = s.vb1[pl.ds(16 * 4 + row, 1)]
        sides.append(s.side1[k])
        near.append(s.vb1[pl.ds(16 * 5 + edge, 8, stride=16)])
    for column, edge in ((127, 0), (64, 63)):
        packed = jnp.zeros((16, 128), F32)
        for k in range(3, 13):
            place = (k - 4) & 127
            packed = jnp.where(lane16 == place, turn(s.vb1[pad1(k)], place - column), packed)
        sides.append(packed)
        near.append(pack(inner, 8, 8, edge))

    def tall(value, ref):
        ref[pl.ds(0, 8, stride=2)] = value
        ref[pl.ds(1, 8, stride=2)] = value
        return ref[...]

    first_row, first_lane = (row16 & 1) == 0, (lane16 & 1) == 0
    layers = []
    finish(round_hh)
    drain()
    for k in range(6):
        side = sides[k]
        rows = tall(side[0:8], s.wide1.at[k, 0])
        here = take(rows, half16)
        inside = take(tall(near[k], s.wide1.at[k, 1]), half16)
        before = take(tall(turn(side, 1, 0)[0:8], s.wide1.at[k, 2]), half16)
        after = take(tall(turn(side, -1, 0)[0:8], s.wide1.at[k, 3]), half16)
        row_low = jnp.where(first_row, before, here)
        row_high = jnp.where(first_row, here, after)
        lane_low = jnp.where(first_lane, take(turn(rows, 1), half16), here)
        lane_high = jnp.where(first_lane, here, take(turn(rows, -1), half16))
        axis = k // 2
        of_rows, of_lanes = ((1, 2), (0, 2), (1, 0))[axis]
        c = lambda d, upper: s.hh_rcv[k, 1 + 2 * d + upper]
        upper = 1 - k % 2
        total = s.hh_rcv[k, 0] + (THIRD + c(axis, 1 - upper)) * here + c(axis, upper) * inside
        total = total + c(of_rows, 0) * row_low + c(of_rows, 1) * row_high
        layers.append(total + (c(of_lanes, 0) * lane_low + c(of_lanes, 1) * lane_high))
        s.c_rcv[k] = s.c_rcv[k] + here
    fill(B0, s.vb0, s.c_rcv)
    smooth(0, s.vb0, s.va0, s.c_rcv[4], s.c_rcv[5])
    fill(B0, s.va0, layers)

    def emit_out(i, v, total):
        out[B0.own(i)] = v * THIRD + total

    stencil(0, s.va0, layers[4], layers[5], emit_out)


def shards(rhs, face_x, face_y, face_z):
    flat = [a.reshape(256, 128) for a in (rhs, face_x, face_y, face_z)]
    whole = pl.pallas_call(
        cycle,
        out_shape=jax.ShapeDtypeStruct((256, 128), F32),
        in_specs=[pl.BlockSpec(memory_space=pltpu.HBM)] * 4,
        out_specs=pl.BlockSpec(memory_space=pltpu.VMEM),
        scratch_shapes=list(SCRATCH.values()),
        compiler_params=pltpu.CompilerParams(
            collective_id=0, has_side_effects=True, vmem_limit_bytes=64 * 1024 * 1024
        ),
        name="vcycle",
    )(*flat)
    return whole.reshape(16, 16, 128)


def solution(mesh):
    placed = P("gx", "gy", "gz")
    return jax.shard_map(
        shards, mesh=mesh, in_specs=(placed,) * 4, out_specs=placed, check_vma=False
    )
```

```python
import jax
import jax.numpy as jnp
from jax import lax
from jax.experimental import pallas as pl
from jax.experimental.pallas import tpu as pltpu
from jax.sharding import PartitionSpec as P

RELAX = 2.0 / 3.0
THIRD = 1.0 / 3.0
COARSE_SWEEPS = 24
GX, GY, GZ = 4, 8, 8
F32 = jnp.float32
MESH = pl.DeviceIdType.MESH

FACES = [(1, 0, 0), (-1, 0, 0), (0, 1, 0), (0, -1, 0), (0, 0, 1), (0, 0, -1)]
DOWN = [(-1, 0, 0), (0, -1, 0), (0, 0, -1)]
RING_Z = [(0, 0, k) for k in (4, 3, 5, 2, 6, 1, 7)]
RING_Y = [(0, k, 0) for k in (4, 3, 5, 2, 6, 1, 7)]
AROUND = [
    (x, y, z) for x in (1, -1, 0) for y in (1, -1, 0) for z in (1, -1, 0) if (x, y, z) != (0, 0, 0)
]
AROUND.sort(key=lambda d: -(abs(d[0]) + abs(d[1]) + abs(d[2])))
LINE = [(2, 0, 0), (1, 0, 0), (3, 0, 0)]
FRIENDS = [(0, 0, 4), (0, 0, 3), (0, 0, 5), (0, 0, 2), (0, 0, 6)] + FACES
SIDES = [(0, 1, 0), (0, -1, 0)]
PLANE = [(2, 1, 0), (2, -1, 0), (1, 1, 0), (1, -1, 0), (3, 1, 0), (3, -1, 0)]
PLANE += [(2, 0, 0), (0, 1, 0), (0, -1, 0), (1, 0, 0), (3, 0, 0)]


def lanes(rows):
    return lax.broadcasted_iota(jnp.int32, (rows, 128), 1)


def sublanes(rows):
    return lax.broadcasted_iota(jnp.int32, (rows, 128), 0)


def turn(value, steps, axis=1):
    steps %= value.shape[axis]
    return value if steps == 0 else pltpu.roll(value, steps, axis)


def take(value, index):
    return jnp.take_along_axis(value, index, axis=1, mode="promise_in_bounds")


class Block:
    def __init__(self, size_x, size_y, size_z, weight):
        self.X, self.Y, self.Z, self.weight = size_x, size_y, size_z, weight
        self.pitch = size_y + 8
        self.rows = size_x * size_y
        self.padded = 8 + (size_x + 2) * self.pitch

    def base(self, i):
        return 8 + (i + 1) * self.pitch

    def own(self, i):
        return pl.ds(i * self.Y, self.Y)

    def at(self, i, shift=0):
        return pl.ds(self.base(i) + shift, self.Y)

    def row_of_each(self, y):
        return pl.ds(self.base(0) + y, self.X, stride=self.pitch)


B0 = Block(16, 16, 128, 1.0)

SCRATCH = {}


def vmem(name, *shape):
    SCRATCH[name] = pltpu.VMEM(shape, F32)


def dma(name, *shape):
    SCRATCH[name] = pltpu.SemaphoreType.DMA(shape)


for key in ("rhs", "fx", "fy", "fz"):
    vmem(key, 256, 128)
dma("in_sem", 5)
for key in ("cxl0", "cxu0", "cyl0", "cyu0", "czl0", "czu0", "g0", "d150", "kw0", "r0", "w0"):
    vmem(key, 256, 128)
vmem("va0", B0.padded, 128)
vmem("vb0", B0.padded, 128)
vmem("lyp0", B0.X * B0.pitch, 128)
for key in ("fx1", "fy1", "fz1", "r1"):
    vmem(key, 64, 128)
for key in ("cxl1", "cxu1", "cyl1", "cyu1", "czl1", "czu1", "g1", "d151", "kw1"):
    vmem(key, 17 * 16, 128)
for key in ("va1", "vb1"):
    vmem(key, 19 * 16, 128)
vmem("ext1", 4, 17 * 16, 128)
vmem("hw_own", 5, 8, 8, 128)
vmem("hw_pack", 3, 8, 8, 128)
vmem("hw_low", 3, 4, 8, 128)
vmem("hw_high", 3, 4, 8, 128)
vmem("hw_zed", 2, 8, 128)
vmem("hw_xr", 2, 3, 3, 8, 128)
vmem("hw_yr", 6, 3, 4, 8, 128)
vmem("hw_zr", 18, 8, 128)
dma("hw_ss", 26)
dma("hw_rs", 26)
vmem("q1", 8 * 16, 128)
for key, rows, count in (("a0", 16, 3), ("b", 16, 6), ("c", 16, 6), ("a1", 8, 3), ("d", 8, 6), ("e", 8, 6)):
    vmem(f"{key}_snd", count, rows, 128)
    vmem(f"{key}_rcv", count, rows, 128)
    dma(f"{key}_ss", count)
    dma(f"{key}_rs", count)
vmem("t0", 256, 128)
vmem("hh_snd", 6, 7, 16, 128)
vmem("hh_rcv", 6, 7, 16, 128)
dma("hh_ss", 6)
dma("hh_rs", 6)
vmem("side1", 6, 16, 128)
vmem("wide1", 6, 4, 16, 128)
vmem("t16", 3, 16, 128)
vmem("zf_snd", 16, 128)
vmem("zf_rcv", 7, 16, 128)
vmem("xf_snd", 6, 16, 128)
vmem("xf_rcv", 3, 6, 16, 128)
vmem("nf_snd", 3, 2, 8, 8, 128)
vmem("nf_rcv", 2, 3, 2, 8, 8, 128)
for key in ("nf_half", "nf_mate"):
    vmem(key, 2, 3, 2, 4, 8, 128)
for key in ("face_half", "face_mate"):
    vmem(key, 3, 8, 8, 128)
for key in ("nm", "ym"):
    dma(f"{key}_ss", 1)
    dma(f"{key}_rs", 1)
vmem("zr_snd", 16, 128)
vmem("zr_rcv", 7, 16, 128)
vmem("xr_snd", 2, 16, 128)
vmem("xr_rcv", 11, 2, 16, 128)
for key, count in (("zf", 7), ("zr", 7), ("xr", 11), ("xf", 3), ("nf", 2)):
    dma(f"{key}_ss", count)
    dma(f"{key}_rs", count)
for key in ("f2", "lx2", "ly2", "lz2", "va2", "vb2"):
    vmem(key, 2, 20, 16, 128)
for key in ("cxl2", "cxu2", "cyl2", "cyu2", "czl2", "czu2", "g2", "d152", "kw2"):
    vmem(key, 2, 20, 16, 128)
vmem("nv_snd", 1, 2, 8, 8, 128)
vmem("nv_rcv", 2, 1, 2, 8, 8, 128)
dma("nv_ss", 2)
dma("nv_rs", 2)
vmem("s2", 128, 128)
vmem("p2", 256, 128)
vmem("face3", 3, 128, 128)
vmem("f3", 128, 128)
for key in ("yf", "yr"):
    dma(f"{key}_ss", 7)
    dma(f"{key}_rs", 7)
for key in ("cxl3", "cxu3", "cyl3", "cyu3", "czl3", "czu3", "g3", "d153", "kw3", "r3", "p3"):
    vmem(key, 128, 128)
vmem("va3", 160, 128)
vmem("vb3", 160, 128)
for key in ("t4", "cxl4", "cxu4", "cyl4", "cyu4", "czl4", "czu4", "d154", "kw4", "r4", "p4"):
    vmem(key, 32, 128)
vmem("fc4", 3, 32, 128)
for key in ("t5", "cx5", "cyl5", "cyu5", "czl5", "czu5", "kw5", "e5"):
    vmem(key, 8, 128)


class Space:
    pass


def cycle(rhs_in, fx_in, fy_in, fz_in, out, *scratch):
    s = Space()
    for name, ref in zip(SCRATCH, scratch):
        setattr(s, name, ref)
    gx, gy, gz = lax.axis_index("gx"), lax.axis_index("gy"), lax.axis_index("gz")

    def peer(offset):
        return (
            (gx + offset[0]) & (GX - 1),
            (gy + offset[1]) & (GY - 1),
            (gz + offset[2]) & (GZ - 1),
        )

    loads = [
        pltpu.make_async_copy(source, target, s.in_sem.at[k])
        for k, (source, target) in enumerate(
            ((fx_in, s.fx), (fy_in, s.fy), (fz_in, s.fz), (rhs_in, s.rhs))
        )
    ]
    for load in loads:
        load.start()

    barrier = pltpu.get_barrier_semaphore()
    for offset in FRIENDS:
        pl.semaphore_signal(barrier, inc=1, device_id=peer(offset), device_id_type=MESH)

    def copies(offsets, sources, targets, ss, rs, first=0):
        made = [
            pltpu.make_async_remote_copy(
                src_ref=sources(k),
                dst_ref=targets(k),
                send_sem=ss.at[k],
                recv_sem=rs.at[k],
                device_id=peer(offset),
                device_id_type=MESH,
            )
            for k, offset in enumerate(offsets, first)
        ]
        for one in made:
            one.start()
        return made

    core = gz & 1
    mate = (gx, gy, gz + 1 - 2 * core)

    def to_mate(source, target, key):
        one = pltpu.make_async_remote_copy(
            src_ref=source,
            dst_ref=target,
            send_sem=getattr(s, key + "_ss").at[0],
            recv_sem=getattr(s, key + "_rs").at[0],
            device_id=mate,
            device_id_type=MESH,
        )
        one.start()
        return [one]

    sent = []

    def finish(made):
        for one in made:
            one.wait_recv()
        sent.extend(made)

    def drain():
        for one in sent:
            one.wait_send()
        sent.clear()

    def flag(condition):
        return jnp.where(condition, 1.0, 0.0).astype(F32)

    low_x, low_y, low_z = flag(gx > 0), flag(gy > 0), flag(gz > 0)
    top_x, top_y, top_z = flag(gx < GX - 1), flag(gy < GY - 1), flag(gz < GZ - 1)


    def pack(read, rows, count, column):
        packed = jnp.zeros((rows, 128), F32)
        lane = lanes(rows)
        for i in range(count):
            packed = jnp.where(lane == i, turn(read(i), i - column), packed)
        return packed

    def send_faces(block, ref, key):
        snd, rcv = getattr(s, key + "_snd"), getattr(s, key + "_rcv")
        snd[0] = ref[block.at(block.X - 1)]
        snd[1] = ref[block.at(0)]
        snd[2] = ref[block.row_of_each(block.Y - 1)]
        snd[3] = ref[block.row_of_each(0)]
        sems = getattr(s, key + "_ss"), getattr(s, key + "_rs")
        ends = (lambda k: snd.at[k], lambda k: rcv.at[k], *sems)
        made = copies(FACES[:4], *ends)
        snd[4] = pack(lambda i: ref[block.at(i)], 16, 16, 127)
        snd[5] = pack(lambda i: ref[block.at(i)], 16, 16, 0)
        return made + copies(FACES[4:], *ends, first=4)

    def fill(block, ref, halo):
        ref[block.at(-1)] = halo[0]
        ref[block.at(block.X)] = halo[1]
        ref[block.row_of_each(-1)] = halo[2]
        ref[block.row_of_each(block.Y)] = halo[3]

    def send_upper(lx, ly, lz, key):
        block = B0
        snd = getattr(s, key + "_snd")
        snd[0] = lx[block.own(0)]
        snd[1] = ly[pl.ds(0, block.X, stride=block.Y)]
        snd[2] = pack(lambda i: lz[block.own(i)], 16, 16, 0)
        rcv = getattr(s, key + "_rcv")
        pl.semaphore_wait(barrier, len(FRIENDS))
        return copies(
            DOWN,
            lambda k: snd.at[k],
            lambda k: rcv.at[k],
            getattr(s, key + "_ss"),
            getattr(s, key + "_rs"),
        )

    def coefficients(level, lx, ly, lz, key):
        block = B0
        rcv = getattr(s, key + "_rcv")
        lyp = getattr(s, f"lyp{level}")
        c = {k: getattr(s, f"{k}{level}") for k in ("cxl", "cxu", "cyl", "cyu", "czl", "czu")}
        d15, kw = getattr(s, f"d15{level}"), getattr(s, f"kw{level}")
        for i in range(block.X):
            lyp[pl.ds(i * block.pitch, block.Y)] = ly[block.own(i)]
        lyp[pl.ds(block.Y, block.X, stride=block.pitch)] = rcv[1] * top_y
        next_x = rcv[0] * top_x
        next_z = rcv[2] * top_z
        lane, row = lanes(block.Y), sublanes(block.Y)
        keep_y = jnp.where(row == 0, low_y, 1.0)
        keep_z = jnp.where(lane == 0, low_z, 1.0)
        for i in range(block.X):
            own = block.own(i)
            a_xl = lx[own]
            a_xu = lx[block.own(i + 1)] if i + 1 < block.X else next_x
            a_yl = ly[own]
            a_yu = lyp[pl.ds(i * block.pitch + 1, block.Y)]
            a_zl = lz[own]
            a_zu = jnp.where(
                lane == block.Z - 1, turn(next_z, block.Z - 1 - i), turn(a_zl, -1)
            )
            total = (a_xl + a_yl + a_zl) + (a_xu + a_yu + a_zu)
            scale = RELAX / total
            d15[own] = (1.5 * block.weight) * total
            kw[own] = scale * (1.0 / block.weight)
            c["cxl"][own] = scale * a_xl * (low_x if i == 0 else 1.0)
            c["cxu"][own] = scale * a_xu
            c["cyl"][own] = scale * a_yl * keep_y
            c["cyu"][own] = scale * a_yu
            c["czl"][own] = scale * a_zl * keep_z
            c["czu"][own] = scale * a_zu

    def stencil(level, ref, low, high, emit):
        block = B0
        lane = lanes(block.Y)
        get = lambda k: getattr(s, f"{k}{level}")
        for i in range(block.X):
            own = block.own(i)
            v = ref[block.at(i)]
            down = jnp.where(lane == 0, turn(low, -i), turn(v, 1))
            up = jnp.where(lane == block.Z - 1, turn(high, block.Z - 1 - i), turn(v, -1))
            t_x = get("cxl")[own] * ref[block.at(i - 1)] + get("cxu")[own] * ref[block.at(i + 1)]
            t_y = get("cyl")[own] * ref[block.at(i, -1)] + get("cyu")[own] * ref[block.at(i, 1)]
            t_z = get("czl")[own] * down + get("czu")[own] * up
            emit(i, v, get("g")[own] + (t_x + t_y + t_z))

    def smooth(level, source, target, low, high):
        block = B0

        def emit(i, v, total):
            target[block.at(i)] = v * THIRD + total

        stencil(level, source, low, high, emit)

    def residual(level, source, low, high):
        block = B0
        d15, r = getattr(s, f"d15{level}"), getattr(s, f"r{level}")

        def emit(i, v, total):
            r[block.own(i)] = d15[block.own(i)] * (total - RELAX * v)
            s.t0[block.own(i)] = v * THIRD + total

        stencil(level, source, low, high, emit)


    lane8, lane16 = lanes(8), lanes(16)
    row8, row16 = sublanes(8), sublanes(16)
    upper_half = row8 < 4
    slices_x = {1: (5, 3), -1: (0, 3), 0: (0, 8)}
    pairs_x = {1: (2, 2), -1: (0, 2), 0: (0, 4)}
    flat_yr = [(x, y) for x in (1, -1, 0) for y in (1, -1)]
    flat_zr = [(x, y, z) for x in (1, -1, 0) for y in (1, -1, 0) for z in (1, -1)]

    def pack_around():
        zeds = [jnp.zeros((8, 128), F32)] * 2
        group = lane8 // 3
        for a in range(5):
            for x in range(8):
                v, place = s.hw_own[a, x], 8 * a + x
                zeds = [
                    jnp.where(group == place, turn(v, 3 * place - first), zed)
                    for zed, first in zip(zeds, (61, 0))
                ]
        s.hw_zed[0], s.hw_zed[1] = zeds
        for t in range(3):
            tiles = []
            for x in range(8):
                v = s.hw_own[2 * t, x]
                if t < 2:
                    v = jnp.where(lane8 < 64, v, turn(s.hw_own[2 * t + 1, x], 64))
                s.hw_pack[t, x] = v
                tiles.append(v)
            for i in range(4):
                even, odd = tiles[2 * i], tiles[2 * i + 1]
                s.hw_low[t, i] = jnp.where(upper_half, even, turn(odd, 4, 0))
                s.hw_high[t, i] = jnp.where(upper_half, turn(even, 4, 0), odd)

    def send_around():
        def source(k):
            x, y, z = AROUND[k]
            if z != 0:
                return s.hw_zed.at[0 if z > 0 else 1]
            if y != 0:
                return (s.hw_low if y < 0 else s.hw_high).at[:, pl.ds(*pairs_x[x])]
            return s.hw_pack.at[:, pl.ds(*slices_x[x])]

        def target(k):
            x, y, z = AROUND[k]
            if z != 0:
                return s.hw_zr.at[flat_zr.index((x, y, z))]
            if y != 0:
                return s.hw_yr.at[flat_yr.index((x, y)), :, pl.ds(0, pairs_x[x][1])]
            return s.hw_xr.at[0 if x > 0 else 1]

        return copies(AROUND, source, target, s.hw_ss, s.hw_rs)

    def assemble(a, k):
        x = k - 4
        if x < 0:
            d, layer, first = 1, x + 8, 5
        elif x < 8:
            d, layer, first = 0, x, 0
        else:
            d, layer, first = -1, x - 8, 0
        place = 3 * (8 * a + layer)
        t = a // 2
        inner = s.hw_own[a, layer] if d == 0 else s.hw_xr[0 if d > 0 else 1, t, layer - first]
        pair = layer // 2 - pairs_x[d][0]
        above = s.hw_yr[flat_yr.index((d, -1)), t, pair]
        below = s.hw_yr[flat_yr.index((d, 1)), t, pair]
        if layer % 2 == 0:
            below = turn(below, 4, 0)
        else:
            above = turn(above, 4, 0)
        outer = jnp.where(upper_half, above, below)
        if a % 2 == 1:
            outer = turn(outer, 64)
            inner = inner if d == 0 else turn(inner, 64)
        whole = jnp.concatenate([inner, outer], axis=0)

        def side(z):
            zed = lambda y: s.hw_zr[flat_zr.index((d, y, z))]
            outer = jnp.where(upper_half, zed(-1), zed(1))
            return jnp.concatenate([zed(0), outer], axis=0)

        whole = jnp.where((lane16 >= 64) & (lane16 < 72), turn(side(-1), 64 - place), whole)
        return jnp.where(lane16 >= 120, turn(side(1), 125 - place), whole)

    def ext1(k):
        return pl.ds(16 * k, 16)

    def pad1(k):
        return pl.ds(16 * k + 16, 16)

    def coefficients1(first, last):
        keep_y = jnp.where(row16 == 0, low_y, 1.0)
        keep_z = jnp.where(lane16 == 0, low_z, 1.0)
        last_y = jnp.where(row16 == 7, top_y, 1.0)
        last_z = jnp.where(lane16 == 63, top_z, 1.0)
        for k in range(first, last + 1):
            own = ext1(k)
            a_xl, a_yl, a_zl = s.ext1[0, own], s.ext1[1, own], s.ext1[2, own]
            a_xu = s.ext1[0, ext1(k + 1)]
            if k == 11:
                a_xu = a_xu * top_x
            a_yu = turn(a_yl, -1, 0) * last_y
            a_zu = turn(a_zl, -1) * last_z
            total = (a_xl + a_yl + a_zl) + (a_xu + a_yu + a_zu)
            scale = RELAX / total
            s.kw1[own] = scale * 4.0
            s.d151[own] = (1.5 * 0.25) * total
            s.cxl1[own] = scale * a_xl * (low_x if k == 4 else 1.0)
            s.cxu1[own] = scale * a_xu
            s.cyl1[own] = scale * a_yl * keep_y
            s.cyu1[own] = scale * a_yu
            s.czl1[own] = scale * a_zl * keep_z
            s.czu1[own] = scale * a_zu

    def send_faces1(ref, key):
        snd, rcv = getattr(s, key + "_snd"), getattr(s, key + "_rcv")
        inner = lambda i: ref[pl.ds(16 * (i + 5), 8)]
        snd[0] = inner(7)
        snd[1] = inner(0)
        snd[2] = ref[pl.ds(16 * 5 + 7, 8, stride=16)]
        snd[3] = ref[pl.ds(16 * 5, 8, stride=16)]
        sems = getattr(s, key + "_ss"), getattr(s, key + "_rs")
        ends = (lambda k: snd.at[k], lambda k: rcv.at[k], *sems)
        made = copies(FACES[:4], *ends)
        snd[4] = pack(inner, 8, 8, 63)
        snd[5] = pack(inner, 8, 8, 0)
        return made + copies(FACES[4:], *ends, first=4)

    def fill1(ref, halo):
        low, high = halo[4], halo[5]
        for i in range(8):
            own = pl.ds(16 * (i + 5), 8)
            v = jnp.where(lane8 == 64, turn(high, 64 - i), ref[own])
            ref[own] = jnp.where(lane8 == 127, turn(low, 127 - i), v)
        ref[pl.ds(16 * 4, 8)] = halo[0]
        ref[pl.ds(16 * 13, 8)] = halo[1]
        ref[pl.ds(16 * 5 + 15, 8, stride=16)] = halo[2]
        ref[pl.ds(16 * 5 + 8, 8, stride=16)] = halo[3]

    def stencil1(first, last, ref, emit):
        for k in range(first, last + 1):
            own = ext1(k)
            v = ref[pad1(k)]
            t_x = s.cxl1[own] * ref[pad1(k - 1)] + s.cxu1[own] * ref[pad1(k + 1)]
            t_y = s.cyl1[own] * turn(v, 1, 0) + s.cyu1[own] * turn(v, -1, 0)
            t_z = s.czl1[own] * turn(v, 1) + s.czu1[own] * turn(v, -1)
            emit(k, v, s.g1[own] + (t_x + t_y + t_z))

    def smooth1(first, last, source, target):
        def emit(k, v, total):
            target[pad1(k)] = v * THIRD + total

        stencil1(first, last, source, emit)

    even8 = (2 * lane8) & 127
    half16 = lane16 >> 1

    def pair_z(value):
        return value + turn(value, -1)

    def stage_z(arrays, snd):
        group = lane16 >> 4
        packed = jnp.zeros((16, 128), F32)
        for a in range(arrays):
            whole = s.t16[a]
            for p in range(2):
                moved = take(whole, 4 * (lane16 & 15) + 2 * p)
                packed = jnp.where(group == ((gz + 2 * a + p) & 7), moved, packed)
        snd[...] = packed

    def merge_z(arrays, own, others, target):
        group = lane16 >> 4
        parts = [(0, own)] + [(RING_Z[k][2], others(k)) for k in range(7)]
        for q in range(2 * arrays):
            merged = jnp.zeros((16, 128), F32)
            for distance, part in parts:
                merged = jnp.where(group == ((gz - distance + q) & 7), part, merged)
            target[q] = turn(merged, -16 * q)

    for load in loads[:3]:
        load.wait()
    round_a0 = send_upper(s.fx, s.fy, s.fz, "a0")

    for i in range(8):
        own = pl.ds(8 * i, 8)
        here = lambda ref, shift: ref[pl.ds(32 * i + shift, 8, stride=2)]
        s.fx1[own] = take(pair_z(here(s.fx, 0) + here(s.fx, 1)), even8) * 0.25
        s.fy1[own] = take(pair_z(here(s.fy, 0) + here(s.fy, 16)), even8) * 0.25
        total = (here(s.fz, 0) + here(s.fz, 1)) + (here(s.fz, 16) + here(s.fz, 17))
        s.fz1[own] = take(total, even8) * 0.25
    s.a1_snd[0] = s.fx1[pl.ds(0, 8)]
    s.a1_snd[1] = s.fy1[pl.ds(0, 8, stride=8)]
    s.a1_snd[2] = pack(lambda i: s.fz1[pl.ds(8 * i, 8)], 8, 8, 0)
    round_a1 = copies(
        DOWN, lambda k: s.a1_snd.at[k], lambda k: s.a1_rcv.at[k], s.a1_ss, s.a1_rs
    )
    for i in range(4):
        own = pl.ds(4 * i, 4)
        here = lambda ref, shift: ref[pl.ds(16 * i + shift, 4, stride=2)]
        s.t16[0, own] = here(s.fx1, 0) + here(s.fx1, 1)
        s.t16[1, own] = here(s.fy1, 0) + here(s.fy1, 8)
        total = (here(s.fz1, 0) + here(s.fz1, 1)) + (here(s.fz1, 8) + here(s.fz1, 9))
        s.t16[2, own] = total * 0.25
    s.t16[0] = pair_z(s.t16[0]) * 0.25
    s.t16[1] = pair_z(s.t16[1]) * 0.25
    stage_z(3, s.zf_snd)
    round_zf = copies(
        RING_Z, lambda k: s.zf_snd, lambda k: s.zf_rcv.at[k], s.zf_ss, s.zf_rs
    )
    for p in range(2):
        for x in (0, 1, 18, 19):
            for ref in (s.va2, s.vb2):
                ref[p, x] = jnp.zeros((16, 128), F32)
        for x in range(16):
            s.f2[p, x + 2] = jnp.zeros((16, 128), F32)
    for ref in (s.va3, s.vb3):
        for k in range(2):
            ref[pl.ds(8 * k, 8)] = jnp.zeros((8, 128), F32)
            ref[pl.ds(144 + 8 * k, 8)] = jnp.zeros((8, 128), F32)
    s.p2[...] = jnp.zeros_like(s.p2)
    s.ext1[...] = jnp.ones_like(s.ext1)
    for k in (0, 1, 2, 3, 12, 13, 14, 15):
        s.va1[pad1(k)] = jnp.zeros((16, 128), F32)
        s.vb1[pad1(k)] = jnp.zeros((16, 128), F32)

    loads[3].wait()
    finish(round_a0)
    coefficients(0, s.fx, s.fy, s.fz, "a0")
    for i in range(16):
        own = B0.own(i)
        start = s.kw0[own] * s.rhs[own]
        s.g0[own] = start
        s.va0[B0.at(i)] = start
    round_b = send_faces(B0, s.va0, "b")
    finish(round_a1)
    for i in range(8):
        own, here = pl.ds(8 * i, 8), pl.ds(16 * (i + 4), 8)
        s.ext1[0, here] = s.fx1[own]
        s.ext1[1, here] = s.fy1[own]
        upper = turn(s.a1_rcv[2], 64 - i)
        s.ext1[2, here] = jnp.where(lane8 == 64, upper, s.fz1[own])
        s.hw_own[0, i] = s.fx1[own]
        s.hw_own[1, i] = s.fy1[own]
        s.hw_own[2, i] = s.fz1[own]
    s.ext1[0, pl.ds(16 * 12, 8)] = s.a1_rcv[0]
    s.ext1[1, pl.ds(16 * 4 + 8, 8, stride=16)] = s.a1_rcv[1]
    coefficients1(4, 11)
    finish(round_zf)
    merge_z(3, s.zf_snd[...], lambda k: s.zf_rcv[k], s.xf_snd)
    finish(round_b)
    fill(B0, s.va0, s.b_rcv)
    smooth(0, s.va0, s.vb0, s.b_rcv[4], s.b_rcv[5])
    round_c = send_faces(B0, s.vb0, "c")
    round_xf = copies(
        LINE, lambda k: s.xf_snd, lambda k: s.xf_rcv.at[k], s.xf_ss, s.xf_rs
    )
    finish(round_c)
    fill(B0, s.vb0, s.c_rcv)
    residual(0, s.vb0, s.c_rcv[4], s.c_rcv[5])

    for i in range(8):
        here = lambda shift: s.r0[pl.ds(32 * i + shift, 8, stride=2)]
        total = (here(0) + here(1)) + (here(16) + here(17))
        forcing = take(pair_z(total), even8) * 0.125
        s.hw_own[3, i] = forcing
        start = s.kw1[pl.ds(16 * (i + 4), 8)] * forcing
        s.g1[pl.ds(16 * (i + 4), 8)] = start
        s.g1[pl.ds(16 * (i + 4) + 8, 8)] = jnp.zeros((8, 128), F32)
        s.va1[pl.ds(16 * (i + 5), 8)] = start
        s.va1[pl.ds(16 * (i + 5) + 8, 8)] = jnp.zeros((8, 128), F32)

    def block2(p, x):
        return (p, x + 2)

    def spread(arrays, offsets, snd, rcv, targets):
        parts = [((0, 0, 0), lambda q: snd.at[q])]
        for k, offset in enumerate(offsets):
            parts.append((offset, lambda q, k=k: rcv.at[k, q]))
        for offset, part in parts:
            first = 4 * ((gx - offset[0]) & 3)
            place = pl.ds(4 * (1 - offset[1]), 4)
            for a in range(arrays):
                for p in range(2):
                    for x in range(4):
                        piece = part(2 * a + p)[pl.ds(4 * x, 4)]
                        targets[a][p, x + 2 + first, place] = piece

    def pack_sides(refs, snd):
        for a, ref in enumerate(refs):
            for p in range(2):
                for i in range(8):
                    even = ref[p, 2 * i + 2, pl.ds(0, 8)]
                    odd = ref[p, 2 * i + 3, pl.ds(0, 8)]
                    snd[a, p, i] = jnp.where(upper_half, turn(even, 4, 0), odd)

    def take_sides(refs, key, rest):
        rcv = getattr(s, key + "_rcv")
        for a, ref in enumerate(refs):
            for p in range(2):
                for x in range(16):
                    below, above = rcv[0, a, p, x // 2], rcv[1, a, p, x // 2]
                    if x % 2 == 1:
                        below, above = turn(below, 4, 0), turn(above, 4, 0)
                    own = ref[p, x + 2, pl.ds(0, 8)]
                    ref[p, x + 2, pl.ds(0, 8)] = jnp.where(upper_half, below, own)
                    ref[p, x + 2, pl.ds(8, 8)] = jnp.where(upper_half, above, rest)

    faces2 = (s.lx2, s.ly2, s.lz2)
    global_y = row16 + 4 * gy - 4
    not_low, not_top = global_y != 0, global_y != 4 * GY - 1

    round_d = send_faces1(s.va1, "d")
    mine = pl.ds(pl.multiple_of(16 * gy, 16), 16)

    finish(round_xf)
    spread(3, LINE, s.xf_snd, s.xf_rcv, faces2)
    pack_sides(faces2, s.nf_snd)
    round_nf = copies(
        SIDES,
        lambda k: s.nf_snd.at[:, :, pl.ds(4 * core, 4)],
        lambda k: s.nf_half.at[k],
        s.nf_ss,
        s.nf_rs,
    )
    for a, ref in enumerate((s.lx2, s.ly2, s.lz2)):
        for i in range(8):
            total = ref[block2(0, 2 * i)]
            if a != 2:
                total = total + ref[block2(1, 2 * i)]
            if a != 0:
                total = total + ref[block2(0, 2 * i + 1)]
            if a == 1:
                total = total + ref[block2(1, 2 * i + 1)]
            s.s2[pl.ds(16 * i, 16)] = total
        halves = []
        for j in range(2):
            total = s.s2[pl.ds(4 + 2 * j, 8, stride=16)]
            if a != 1:
                total = total + s.s2[pl.ds(5 + 2 * j, 8, stride=16)]
            halves.append(total * 0.25)
        s.face_half[a, gy] = jnp.where(core == 0, halves[0], halves[1])
    round_yf = copies(
        RING_Y,
        lambda k: s.face_half.at[:, gy],
        lambda k: s.face_half.at[:, gy],
        s.yf_ss,
        s.yf_rs,
    )
    finish(round_d)
    fill1(s.va1, s.d_rcv)
    smooth1(4, 11, s.va1, s.vb1)
    for i in range(8):
        s.hw_own[4, i] = s.vb1[pl.ds(16 * (i + 5), 8)]
    round_e = send_faces1(s.vb1, "e")
    kept = (s.t0, s.cxl0, s.cxu0, s.cyl0, s.cyu0, s.czl0, s.czu0)
    for a, ref in enumerate(kept):
        s.hh_snd[0, a] = ref[B0.own(15)]
        s.hh_snd[1, a] = ref[B0.own(0)]
        s.hh_snd[2, a] = ref[pl.ds(15, 16, stride=16)]
        s.hh_snd[3, a] = ref[pl.ds(0, 16, stride=16)]
        s.hh_snd[4, a] = pack(lambda i: ref[B0.own(i)], 16, 16, 127)
        s.hh_snd[5, a] = pack(lambda i: ref[B0.own(i)], 16, 16, 0)
    pack_around()
    finish(round_nf)
    round_nm = to_mate(s.nf_half, s.nf_mate, "nm")

    finish(round_e)
    fill1(s.vb1, s.e_rcv)

    def emit_r1(k, v, total):
        r = s.d151[ext1(k)] * (total - RELAX * v)
        s.r1[pl.ds(8 * (k - 4), 8)] = r[0:8]

    stencil1(4, 11, s.vb1, emit_r1)
    for i in range(4):
        here = lambda shift: s.r1[pl.ds(16 * i + shift, 4, stride=2)]
        s.t16[0, pl.ds(4 * i, 4)] = (here(0) + here(1)) + (here(8) + here(9))
    s.t16[0] = pair_z(s.t16[0]) * 0.125
    stage_z(1, s.zr_snd)
    round_zr = copies(
        RING_Z, lambda k: s.zr_snd, lambda k: s.zr_rcv.at[k], s.zr_ss, s.zr_rs
    )


    def stencil2(ref, emit):
        for p in range(2):
            for x in range(16):
                j, other = block2(p, x), block2(1 - p, x)
                v, w = ref[j], ref[other]
                t_x = s.cxl2[j] * ref[block2(p, x - 1)] + s.cxu2[j] * ref[block2(p, x + 1)]
                t_y = s.cyl2[j] * turn(v, 1, 0) + s.cyu2[j] * turn(v, -1, 0)
                down, up = (turn(w, 1), w) if p == 0 else (w, turn(w, -1))
                t_z = s.czl2[j] * down + s.czu2[j] * up
                emit(j, v, s.g2[j] + (t_x + t_y + t_z))

    def smooth2(source, target):
        def emit(j, v, total):
            target[j] = v * THIRD + total

        stencil2(source, emit)

    round_hw = send_around()
    finish(round_yf)
    round_ym = to_mate(s.face_half, s.face_mate, "ym")
    finish(round_nm)
    for k in range(2):
        for a in range(3):
            for p in range(2):
                for i in range(4):
                    s.nf_rcv[k, a, p, 4 * core + i] = s.nf_half[k, a, p, i]
                    s.nf_rcv[k, a, p, 4 - 4 * core + i] = s.nf_mate[k, a, p, i]
    take_sides(faces2, "nf", 1.0)
    for p in range(2):
        for x in range(16):
            j = block2(p, x)
            a_xl, a_yl, a_zl = s.lx2[j], s.ly2[j], s.lz2[j]
            a_xu = s.lx2[block2(p, x + 1)] if x < 15 else jnp.zeros((16, 128), F32)
            a_yu = jnp.where(not_top, turn(a_yl, -1, 0), 0.0)
            if p == 0:
                a_zu = s.lz2[block2(1, x)]
            else:
                a_zu = jnp.where(lane16 == 127, 0.0, turn(s.lz2[block2(0, x)], -1))
            total = (a_xl + a_yl + a_zl) + (a_xu + a_yu + a_zu)
            scale = RELAX / total
            s.d152[j] = (1.5 * 0.0625) * total
            s.kw2[j] = scale * 16.0
            s.cxl2[j] = scale * a_xl if x > 0 else jnp.zeros((16, 128), F32)
            s.cxu2[j] = scale * a_xu
            s.cyl2[j] = jnp.where(not_low, scale * a_yl, 0.0)
            s.cyu2[j] = scale * a_yu
            s.czl2[j] = scale * a_zl if p == 1 else jnp.where(lane16 == 0, 0.0, scale * a_zl)
            s.czu2[j] = scale * a_zu

    finish(round_zr)
    merge_z(1, s.zr_snd[...], lambda k: s.zr_rcv[k], s.xr_snd)
    round_xr = copies(
        PLANE, lambda k: s.xr_snd, lambda k: s.xr_rcv.at[k], s.xr_ss, s.xr_rs
    )

    finish(round_ym)
    for a in range(3):
        for y in range(8):
            first = pl.ds(pl.multiple_of(16 * y + 8 * core, 8), 8)
            second = pl.ds(pl.multiple_of(16 * y + 8 - 8 * core, 8), 8)
            s.face3[a, first] = s.face_half[a, y]
            s.face3[a, second] = s.face_mate[a, y]
    zero8 = jnp.zeros((8, 128), F32)
    for y in range(16):
        own = pl.ds(8 * y, 8)
        a_xl, a_yl, a_zl = s.face3[0, own], s.face3[1, own], s.face3[2, own]
        a_xu = jnp.where(row8 == 7, 0.0, turn(a_xl, -1, 0))
        a_yu = s.face3[1, pl.ds(8 * y + 8, 8)] if y < 15 else zero8
        a_zu = jnp.where(lane8 == 127, 0.0, turn(a_zl, -1))
        total = (a_xl + a_yl + a_zl) + (a_xu + a_yu + a_zu)
        scale = RELAX / total
        s.d153[own] = (1.5 * 0.25**3) * total
        s.kw3[own] = scale * 64.0
        s.cxl3[own] = jnp.where(row8 == 0, 0.0, scale * a_xl)
        s.cxu3[own] = scale * a_xu
        s.cyl3[own] = scale * a_yl if y > 0 else zero8
        s.cyu3[own] = scale * a_yu
        s.czl3[own] = jnp.where(lane8 == 0, 0.0, scale * a_zl)
        s.czu3[own] = scale * a_zu

    lane32, row32 = lanes(32), sublanes(32)

    def both(value, lane, step):
        return value + jnp.where(
            (lane & step) == 0, turn(value, -step), turn(value, step)
        )

    def lower_of(value, lane, step):
        return jnp.where((lane & step) == 0, value, turn(value, step))

    for a in range(3):
        for y in range(8):
            here = lambda shift: s.face3[a, pl.ds(16 * y + shift, 4, stride=2)]
            if a == 0:
                total = here(0) + here(8)
            elif a == 1:
                total = here(0) + here(1)
            else:
                total = (here(0) + here(1)) + (here(8) + here(9))
            s.t4[pl.ds(4 * y, 4)] = total
        total = s.t4[...]
        total = both(total, lane32, 1) if a < 2 else lower_of(total, lane32, 1)
        s.fc4[a] = total * 0.25
    a_xl, a_yl, a_zl = s.fc4[0], s.fc4[1], s.fc4[2]
    a_xu = jnp.where((row32 & 3) == 3, 0.0, turn(a_xl, -1, 0))
    a_yu = jnp.where(row32 >= 28, 0.0, turn(a_yl, -4, 0))
    a_zu = jnp.where(lane32 >= 126, 0.0, turn(a_zl, -2))
    total = (a_xl + a_yl + a_zl) + (a_xu + a_yu + a_zu)
    scale = RELAX / total
    s.d154[...] = (1.5 * 0.25**4) * total
    s.kw4[...] = scale * 256.0
    s.cxl4[...] = jnp.where((row32 & 3) == 0, 0.0, scale * a_xl)
    s.cxu4[...] = scale * a_xu
    s.cyl4[...] = jnp.where(row32 < 4, 0.0, scale * a_yl)
    s.cyu4[...] = scale * a_yu
    s.czl4[...] = jnp.where(lane32 < 2, 0.0, scale * a_zl)
    s.czu4[...] = scale * a_zu

    faces5 = []
    for a in range(3):
        for x in range(2):
            here = lambda shift: s.fc4[a, pl.ds(2 * x + shift, 4, stride=8)]
            if a == 0:
                total = here(0) + here(4)
            elif a == 1:
                total = here(0) + here(1)
            else:
                total = (here(0) + here(1)) + (here(4) + here(5))
            s.t5[pl.ds(4 * x, 4)] = total
        total = s.t5[...]
        total = both(total, lane8, 2) if a < 2 else lower_of(total, lane8, 2)
        faces5.append(total * 0.25)
    a_xl, a_yl, a_zl = faces5
    a_xu = jnp.where(row8 >= 4, 0.0, turn(a_xl, 4, 0))
    a_yu = jnp.where((row8 & 3) == 3, 0.0, turn(a_yl, -1, 0))
    a_zu = jnp.where(lane8 >= 124, 0.0, turn(a_zl, -4))
    total = (a_xl + a_yl + a_zl) + (a_xu + a_yu + a_zu)
    scale = RELAX / total
    s.kw5[...] = scale * 1024.0
    s.cx5[...] = jnp.where(row8 >= 4, scale * a_xl, scale * a_xu)
    s.cyl5[...] = jnp.where((row8 & 3) == 0, 0.0, scale * a_yl)
    s.cyu5[...] = scale * a_yu
    s.czl5[...] = jnp.where(lane8 < 4, 0.0, scale * a_zl)
    s.czu5[...] = scale * a_zu

    finish(round_xr)
    spread(1, PLANE, s.xr_snd, s.xr_rcv, (s.f2,))
    for p in range(2):
        for x in range(16):
            j = block2(p, x)
            start = s.kw2[j] * s.f2[j]
            s.g2[j] = start
            s.va2[j] = start
    smooth2(s.va2, s.vb2)

    def emit_r2(j, v, total):
        s.f2[j] = s.d152[j] * (total - RELAX * v)

    stencil2(s.vb2, emit_r2)
    for i in range(8):
        total = (s.f2[block2(0, 2 * i)] + s.f2[block2(1, 2 * i)]) + (
            s.f2[block2(0, 2 * i + 1)] + s.f2[block2(1, 2 * i + 1)]
        )
        s.s2[pl.ds(16 * i, 16)] = total
    for j in range(2):
        total = s.s2[pl.ds(4 + 2 * j, 8, stride=16)] + s.s2[pl.ds(5 + 2 * j, 8, stride=16)]
        s.f3[pl.ds(pl.multiple_of(16 * gy + 8 * j, 8), 8)] = total * 0.125
    round_yr = copies(
        RING_Y, lambda k: s.f3.at[mine], lambda k: s.f3.at[mine], s.yr_ss, s.yr_rs
    )
    pack_sides((s.vb2,), s.nv_snd)
    round_nv = copies(
        SIDES, lambda k: s.nv_snd, lambda k: s.nv_rcv.at[k], s.nv_ss, s.nv_rs
    )
    round_hh = copies(
        FACES, lambda k: s.hh_snd.at[k], lambda k: s.hh_rcv.at[k], s.hh_ss, s.hh_rs
    )

    drain()
    finish(round_hw)
    for k in range(1, 15):
        for a in range(4):
            s.ext1[a, ext1(k)] = assemble(a, k)
        s.vb1[pad1(k)] = assemble(4, k)
    coefficients1(2, 13)
    for k in range(2, 14):
        s.g1[ext1(k)] = s.kw1[ext1(k)] * s.ext1[3, ext1(k)]
    finish(round_yr)

    def at3(y):
        return pl.ds(16 + 8 * y, 8)

    def stencil3(ref, emit):
        for y in range(16):
            own = pl.ds(8 * y, 8)
            v = ref[at3(y)]
            t_x = s.cxl3[own] * turn(v, 1, 0) + s.cxu3[own] * turn(v, -1, 0)
            t_y = s.cyl3[own] * ref[at3(y - 1)] + s.cyu3[own] * ref[at3(y + 1)]
            t_z = s.czl3[own] * turn(v, 1) + s.czu3[own] * turn(v, -1)
            emit(y, v, s.g3[own] + (t_x + t_y + t_z))

    def smooth3(source, target):
        def emit(y, v, total):
            target[at3(y)] = v * THIRD + total

        stencil3(source, emit)

    for y in range(16):
        own = pl.ds(8 * y, 8)
        start = s.kw3[own] * s.f3[own]
        s.g3[own] = start
        s.va3[at3(y)] = start
    smooth3(s.va3, s.vb3)

    def emit_r3(y, v, total):
        own = pl.ds(8 * y, 8)
        s.r3[own] = s.d153[own] * (total - RELAX * v)

    stencil3(s.vb3, emit_r3)
    for y in range(8):
        here = lambda shift: s.r3[pl.ds(16 * y + shift, 4, stride=2)]
        s.t4[pl.ds(4 * y, 4)] = (here(0) + here(1)) + (here(8) + here(9))
    f4 = both(s.t4[...], lane32, 1) * 0.125

    def total4(v):
        t_x = s.cxl4[...] * turn(v, 1, 0) + s.cxu4[...] * turn(v, -1, 0)
        t_y = s.cyl4[...] * turn(v, 4, 0) + s.cyu4[...] * turn(v, -4, 0)
        t_z = s.czl4[...] * turn(v, 2) + s.czu4[...] * turn(v, -2)
        return g4 + (t_x + t_y + t_z)

    g4 = s.kw4[...] * f4
    v4 = g4
    v4 = v4 * THIRD + total4(v4)
    s.r4[...] = s.d154[...] * (total4(v4) - RELAX * v4)
    for x in range(2):
        here = lambda shift: s.r4[pl.ds(2 * x + shift, 4, stride=8)]
        s.t5[pl.ds(4 * x, 4)] = (here(0) + here(1)) + (here(4) + here(5))
    g5 = s.kw5[...] * (both(s.t5[...], lane8, 2) * 0.125)
    cx5, cyl5, cyu5, czl5, czu5 = s.cx5[...], s.cyl5[...], s.cyu5[...], s.czl5[...], s.czu5[...]

    def sweep5(index, v):
        t_y = cyl5 * turn(v, 1, 0) + cyu5 * turn(v, -1, 0)
        t_z = czl5 * turn(v, 4) + czu5 * turn(v, -4)
        return (v * THIRD + g5) + (cx5 * turn(v, 4, 0) + (t_y + t_z))

    s.e5[...] = lax.fori_loop(0, COARSE_SWEEPS - 1, sweep5, g5)
    for x in range(2):
        piece = s.e5[pl.ds(4 * x, 4)]
        for shift in (0, 1, 4, 5):
            s.p4[pl.ds(2 * x + shift, 4, stride=8)] = piece
    v4 = v4 + s.p4[...]
    v4 = v4 * THIRD + total4(v4)
    v4 = v4 * THIRD + total4(v4)
    s.r4[...] = v4
    for x in range(4):
        piece = s.r4[pl.ds(x, 8, stride=4)]
        for shift in (0, 1, 8, 9):
            s.p3[pl.ds(2 * x + shift, 8, stride=16)] = piece
    for y in range(16):
        s.vb3[at3(y)] = s.vb3[at3(y)] + s.p3[pl.ds(8 * y, 8)]
    smooth3(s.vb3, s.va3)
    smooth3(s.va3, s.vb3)

    finish(round_nv)
    take_sides((s.vb2,), "nv", 0.0)
    for k in range(6):
        piece = s.vb3[pl.ds(pl.multiple_of(16 * gy + 8 * k, 8), 8)]
        for x in range(2):
            for y in range(2):
                s.p2[pl.ds(16 * x + 2 * k + y, 8, stride=32)] = piece
    for x in range(16):
        more = s.p2[pl.ds(16 * x, 16)]
        for p in range(2):
            s.vb2[block2(p, x)] = s.vb2[block2(p, x)] + more
    smooth2(s.vb2, s.va2)
    smooth2(s.va2, s.vb2)

    signed = jnp.where(lane16 < 96, lane16, lane16 - 128)
    index = (16 * gz + (signed >> 2)) & 127
    odd = ((signed >> 1) & 1) == 1
    for k in range(8):
        x = 4 * gx + k
        piece = jnp.where(odd, take(s.vb2[1, x], index), take(s.vb2[0, x], index))
        rows = jnp.where(row16 < 6, turn(piece, -4, 0), turn(piece, 4, 0))[0:8]
        for y in range(2):
            s.q1[pl.ds(16 * k + y, 8, stride=2)] = rows
        more = s.q1[pl.ds(16 * k, 16)]
        for i in (2 * k, 2 * k + 1):
            if 1 <= i <= 14:
                s.vb1[pad1(i)] = s.vb1[pad1(i)] + more
    smooth1(2, 13, s.vb1, s.va1)
    smooth1(3, 12, s.va1, s.vb1)
    inner = lambda i: s.vb1[pl.ds(16 * (i + 5), 8)]

    def widen(value, ref, start):
        ref[pl.ds(start, 8, stride=2)] = value
        ref[pl.ds(start + 1, 8, stride=2)] = value
        return take(ref[pl.ds(start, 16)], half16)

    for i in range(8):
        more = widen(inner(i), s.w0, 16 * i)
        for x in (2 * i, 2 * i + 1):
            s.vb0[B0.at(x)] = s.vb0[B0.at(x)] + more

    sides = [s.vb1[pl.ds(16 * 4, 16)], s.vb1[pl.ds(16 * 13, 16)]]
    near = [inner(0), inner(7)]
    for k, row, edge in ((2, 15, 0), (3, 8, 7)):
        s.side1[k, pl.ds(8, 8)] = jnp.zeros((8, 128), F32)
        s.side1[k, pl.ds(0, 8)] = s.vb1[pl.ds(16 * 5 + row, 8, stride=16)]
        s.side1[k, pl.ds(8, 1)] = s.vb1[pl.ds(16 * 13 + row, 1)]
        s.side1[k, pl.ds(15, 1)] = s.vb1[pl.ds(16 * 4 + row, 1)]
        sides.append(s.side1[k])
        near.append(s.vb1[pl.ds(16 * 5 + edge, 8, stride=16)])
    for column, edge in ((127, 0), (64, 63)):
        packed = jnp.zeros((16, 128), F32)
        for k in range(3, 13):
            place = (k - 4) & 127
            packed = jnp.where(lane16 == place, turn(s.vb1[pad1(k)], place - column), packed)
        sides.append(packed)
        near.append(pack(inner, 8, 8, edge))

    def tall(value, ref):
        ref[pl.ds(0, 8, stride=2)] = value
        ref[pl.ds(1, 8, stride=2)] = value
        return ref[...]

    first_row, first_lane = (row16 & 1) == 0, (lane16 & 1) == 0
    layers = []
    finish(round_hh)
    drain()
    for k in range(6):
        side = sides[k]
        rows = tall(side[0:8], s.wide1.at[k, 0])
        here = take(rows, half16)
        inside = take(tall(near[k], s.wide1.at[k, 1]), half16)
        before = take(tall(turn(side, 1, 0)[0:8], s.wide1.at[k, 2]), half16)
        after = take(tall(turn(side, -1, 0)[0:8], s.wide1.at[k, 3]), half16)
        row_low = jnp.where(first_row, before, here)
        row_high = jnp.where(first_row, here, after)
        lane_low = jnp.where(first_lane, take(turn(rows, 1), half16), here)
        lane_high = jnp.where(first_lane, here, take(turn(rows, -1), half16))
        axis = k // 2
        of_rows, of_lanes = ((1, 2), (0, 2), (1, 0))[axis]
        c = lambda d, upper: s.hh_rcv[k, 1 + 2 * d + upper]
        upper = 1 - k % 2
        total = s.hh_rcv[k, 0] + (THIRD + c(axis, 1 - upper)) * here + c(axis, upper) * inside
        total = total + c(of_rows, 0) * row_low + c(of_rows, 1) * row_high
        layers.append(total + (c(of_lanes, 0) * lane_low + c(of_lanes, 1) * lane_high))
        s.c_rcv[k] = s.c_rcv[k] + here
    fill(B0, s.vb0, s.c_rcv)
    smooth(0, s.vb0, s.va0, s.c_rcv[4], s.c_rcv[5])
    fill(B0, s.va0, layers)

    def emit_out(i, v, total):
        out[B0.own(i)] = v * THIRD + total

    stencil(0, s.va0, layers[4], layers[5], emit_out)


def shards(rhs, face_x, face_y, face_z):
    flat = [a.reshape(256, 128) for a in (rhs, face_x, face_y, face_z)]
    whole = pl.pallas_call(
        cycle,
        out_shape=jax.ShapeDtypeStruct((256, 128), F32),
        in_specs=[pl.BlockSpec(memory_space=pltpu.HBM)] * 4,
        out_specs=pl.BlockSpec(memory_space=pltpu.VMEM),
        scratch_shapes=list(SCRATCH.values()),
        compiler_params=pltpu.CompilerParams(
            collective_id=0, has_side_effects=True, vmem_limit_bytes=64 * 1024 * 1024
        ),
        name="vcycle",
    )(*flat)
    return whole.reshape(16, 16, 128)


def solution(mesh):
    placed = P("gx", "gy", "gz")
    return jax.shard_map(
        shards, mesh=mesh, in_specs=(placed,) * 4, out_specs=placed, check_vma=False
    )
```
